32 devices in a mesh: section: 4 (over z), dp: 8 (over y, x, core).
Axes of the slice: x: 2, y: 2, z: 4, core: 2. Of those that a mesh axis runs over, the one named last changes fastest.
Arguments:
- tokens: int32 [32, 640], P('dp'), may hold values from 0 to 255
- padding_mask: int32 [32, 640], P('dp'), may hold values from 0 to 1, as said below
- embedding: float32 [512, 256], P('dp', 'section'), may hold values from -0.5 to 0.5
- mixer_weight: float32 [2, 512, 1536], P(None, 'dp'), may hold values from -0.25 to 0.25
- output_weight: float32 [2, 512, 512], P(None, 'dp'), may hold values from -0.75 to 0.75
- mixer_gain: float32 [2, 512], P(None, 'dp'), may hold values from 0.5 to 1.5
- expand_weight: float32 [2, 512, 2048], P(None, 'dp'), may hold values from -0.25 to 0.25
- reduce_weight: float32 [2, 2048, 512], P(None, 'dp'), may hold values from -0.125 to 0.125
- feed_gain: float32 [2, 512], P(None, 'dp'), may hold values from 0.5 to 1.5
- final_gain: float32 [512], P('dp'), may hold values from 0.5 to 1.5
Outputs:
- item_loss: float32 [32], P('dp')
- logit_grad: float32 [32, 640, 256], P('dp', None, 'section')
- embedding_grad: float32 [512, 256], P('dp', 'section')
- mixer_grad: float32 [2, 512, 1536], P(None, 'dp')
- output_grad: float32 [2, 512, 512], P(None, 'dp')
- mixer_gain_grad: float32 [2, 512], P(None, 'dp')
- expand_grad: float32 [2, 512, 2048], P(None, 'dp')
- reduce_grad: float32 [2, 2048, 512], P(None, 'dp')
- feed_gain_grad: float32 [2, 512], P(None, 'dp')
- final_gain_grad: float32 [512], P('dp')
The draws below stay inside these ranges and needn't reach their ends.
Inputs may be any that keep to these rules, and one draw needn't show every extreme that they name: `padding_mask`: each item's mask is 1 on its first 320 or more positions and 0 on all positions after them.
All inputs are finite; a program needn't handle non-finite values.
Results may differ from the reference program's by a relative error of at most 0.006.
The reference program's roundings to bfloat16 on the way count: a program that leaves them out, or rounds other values in their place, can miss the bound.
Values may be sent and summed in bfloat16 or wider, within the bound.
A program may use at most 192 MiB of HBM per device.

```python
import math
import jax
import jax.numpy as jnp
import numpy as np
from jax import lax

D = 512
HEADS = 8
HD = 64
FF = 2048
VOCAB = 256
BAND = 30
LEN = 640
ITEMS = 32


def draw_padding_mask(key, part):
    key = jax.random.fold_in(key, 11)
    lengths = jax.random.randint(key, (ITEMS, 1), LEN // 2, LEN + 1)
    return (jnp.arange(LEN)[None, :] < lengths).astype(jnp.int32)


def plant(result, stream_key, smallest, high):
    index_at = [jax.random.randint(jax.random.fold_in(stream_key, axis), (), 0, length) for axis, length in enumerate(result.shape)]
    longest = result.shape.index(max(result.shape))
    beside = index_at[:longest] + [(index_at[longest] + 1) % result.shape[longest]] + index_at[longest + 1:]
    return result.at[tuple(index_at)].set(smallest).at[tuple(beside)].set(high)


def shard_levels(own_key, dims, pieces, low, high):
    loudness = 1.0
    for dim, blocks in pieces:
        draws = jax.random.uniform(jax.random.fold_in(jax.random.fold_in(own_key, 6), dim), (blocks,), jnp.float32, low / len(pieces), high / len(pieces))
        loudness = loudness * jnp.repeat(jnp.exp(draws), dims[dim] // blocks).reshape((-1,) + (1,) * (len(dims) - 1 - dim))
    return loudness


def cumulative_ranks(amount, slope):
    weights = [(1 << 20) // math.isqrt(grade ** slope) + 1 for grade in range(1, amount + 1)]
    width = 1 + sum(weights) // (1 << 30)
    return np.cumsum(np.array([max(1, weight // width) for weight in weights]))


def ranked_ids(stream_key, shape, count, skew):
    table = cumulative_ranks(count, skew)
    pick = jax.random.randint(jax.random.fold_in(stream_key, 1), shape, 0, int(table[count - 1]))
    rank = jnp.searchsorted(jnp.asarray(table, jnp.int32), pick, side="right")
    return jax.random.permutation(jax.random.fold_in(stream_key, 2), count)[rank].astype(jnp.int32)


def scatter_about(key, dims, spread, limit, split=(), kind=jnp.bfloat16):
    entries = jax.random.normal(key, dims, jnp.float32) * spread
    if len(split) > 0:
        entries = shard_levels(key, dims, split, -0.22, 0.18) * entries
    return jnp.clip(entries, min=-limit, max=limit).astype(kind)


def setup_inputs(seed: int = 0) -> dict:
    seeds = jax.random.split(jax.random.key(seed), 11)
    tokens = plant(ranked_ids(seeds[0], (ITEMS, LEN), VOCAB, 2), jax.random.fold_in(seeds[0], 3), 0, VOCAB - 1).astype(jnp.int32)
    padding_mask = draw_padding_mask(jax.random.fold_in(seeds[10], 71), 0)
    embedding = scatter_about(seeds[2], (D, VOCAB), 128 ** -0.5, 0.5, ((0, 8), (1, 4)), jnp.float32)
    mixer_weight = scatter_about(seeds[3], (2, D, 3 * D), D ** -0.5, 0.25, ((1, 8),), jnp.float32)
    output_weight = scatter_about(seeds[4], (2, D, D), (D // 8) ** -0.5, 0.75, ((1, 8),), jnp.float32)
    mixer_gain = jnp.clip(1.0 + 0.1 * jax.random.normal(seeds[5], (2, D), jnp.float32), 0.5, 1.5)
    expand_weight = scatter_about(seeds[6], (2, D, FF), D ** -0.5, 0.25, ((1, 8),), jnp.float32)
    reduce_weight = scatter_about(seeds[7], (2, FF, D), FF ** -0.5, 0.125, ((1, 8),), jnp.float32)
    feed_gain = jnp.clip(1.0 + 0.1 * jax.random.normal(seeds[8], (2, D), jnp.float32), 0.5, 1.5)
    final_gain = jnp.clip(1.0 + 0.1 * jax.random.normal(seeds[9], (D,), jnp.float32), 0.5, 1.5)
    return dict(tokens=tokens, padding_mask=padding_mask, embedding=embedding, mixer_weight=mixer_weight, output_weight=output_weight, mixer_gain=mixer_gain, expand_weight=expand_weight, reduce_weight=reduce_weight, feed_gain=feed_gain, final_gain=final_gain)


@jax.custom_vjp
def low(v):
    return lax.optimization_barrier(v.astype(jnp.bfloat16)).astype(jnp.float32)

@jax.custom_vjp
def low_back(v):
    return v

def low_keep(v):
    return (low(v), None)

def low_pass(kept, grad):
    return (grad,)

def back_keep(v):
    return (v, None)

def back_low(kept, grad):
    return (low(grad),)
low.defvjp(low_keep, low_pass)
low_back.defvjp(back_keep, back_low)

def product(left, right):
    return jnp.matmul(left, right, precision=lax.Precision.HIGHEST)

def norm_scale(values, gain):
    return values * lax.rsqrt(lax.optimization_barrier(jnp.mean(values * values, axis=-1, keepdims=True)) + 1e-05) * gain

def head_mixture(scores, near_far, tanh_far, band_ok, causal, position):
    shifted = jnp.where(band_ok, 0.125 * scores, -1e+30)
    largest = lax.optimization_barrier(jnp.max(shifted, axis=-1, keepdims=True))
    weights = jnp.where(band_ok, jnp.exp(shifted - largest), 0.0)
    near = weights / lax.optimization_barrier(jnp.sum(weights, axis=-1, keepdims=True))
    kept = jnp.where(causal, near_far, 0.0)
    first_far = kept / (lax.optimization_barrier(jnp.sum(kept, axis=-1, keepdims=True)) + 1.0)
    second_far = jnp.where(causal, tanh_far, 0.0) / (position + 1.0)
    return near + first_far + second_far

def attention(stream, mixer, output, gain):
    batch, length = (stream.shape[0], stream.shape[1])
    normed = low(norm_scale(stream, gain))
    packed = low(low_back(product(normed, mixer)))
    split_parts = packed.reshape(batch, length, 3, HEADS, HD).transpose(2, 0, 3, 1, 4)
    row_index = jnp.arange(length)[:, None]
    col_index = jnp.arange(length)[None, :]
    causal = col_index <= row_index
    band_ok = causal & (row_index - col_index < BAND)
    position = row_index.astype(jnp.float32)

    def one_head(head_query, head_key, head_value):
        scores = low_back(product(head_query, head_key.T))
        first_query = low(jax.nn.elu(head_query) + 1.0)
        first_key = low(jax.nn.elu(head_key) + 1.0)
        second_query = low(jnp.tanh(head_query))
        second_key = low(jnp.tanh(head_key))
        near_far = low_back(product(first_query, first_key.T))
        tanh_far = low_back(product(second_query, second_key.T))
        mixture = low(head_mixture(scores, near_far, tanh_far, band_ok, causal, position))
        return low(low_back(product(mixture, head_value)))
    per_head = jax.vmap(jax.vmap(one_head))(split_parts[0], split_parts[1], split_parts[2])
    joined = per_head.transpose(0, 2, 1, 3).reshape(batch, length, HEADS * HD)
    return low_back(product(joined, output))

def feed_forward(stream, expand, reduce_matrix, gain):
    normed = low(norm_scale(stream, gain))
    hidden = low_back(product(normed, expand))
    active = low(jax.nn.gelu(hidden))
    return low_back(product(active, reduce_matrix))

def block_loss(weights, token_ids, pad_rows, offsets):
    table, mixer, output, mgain, expand, reduce_matrix, fgain, zgain = [low(weight) for weight in weights]
    stream = jnp.take(table.T, token_ids, axis=0)
    for depth in range(2):
        stream = stream + attention(stream, mixer[depth], output[depth], mgain[depth])
        stream = stream + feed_forward(stream, expand[depth], reduce_matrix[depth], fgain[depth])
    normed = low(norm_scale(stream, zgain))
    logits = low_back(product(normed, table)) + offsets
    zero_col = jnp.zeros((token_ids.shape[0], 1), token_ids.dtype)
    targets = jnp.concatenate([token_ids[:, 1:], zero_col], axis=1)
    scored = jnp.concatenate([pad_rows[:, 1:], zero_col], axis=1).astype(jnp.float32)
    largest = lax.optimization_barrier(jnp.max(logits, axis=-1))
    spread_log = largest + jnp.log(lax.optimization_barrier(jnp.sum(jnp.exp(logits - largest[..., None]), axis=-1)))
    picked = jnp.take_along_axis(logits, targets[..., None], axis=-1)[..., 0]
    cross_terms = (spread_log - picked) * scored
    return (jnp.sum(cross_terms), lax.optimization_barrier(jnp.sum(cross_terms, axis=-1)) / lax.optimization_barrier(jnp.sum(scored, axis=-1)))

def reference(tokens, padding_mask, embedding, mixer_weight, output_weight, mixer_gain, expand_weight, reduce_weight, feed_gain, final_gain):
    blocks = tokens.shape[0] // 4
    id_blocks = tokens.reshape(blocks, 4, LEN)
    pad_blocks = padding_mask.reshape(blocks, 4, LEN)
    zero_offsets = jnp.zeros((blocks, 4, LEN, VOCAB), jnp.float32)
    params = (embedding, mixer_weight, output_weight, mixer_gain, expand_weight, reduce_weight, feed_gain, final_gain)

    def objective(weights, offsets):

        def scan_step(carried, block_in):
            token_ids, pad_rows, offset_rows = block_in
            summed, losses = jax.checkpoint(block_loss)(weights, token_ids, pad_rows, offset_rows)
            return (carried + summed, losses)
        summed, losses = lax.scan(scan_step, jnp.zeros((), jnp.float32), (id_blocks, pad_blocks, offsets))
        return (summed, losses.reshape(-1))
    summed, pullback, item_loss = jax.vjp(objective, params, zero_offsets, has_aux=True)
    grads, logit_grad = pullback(jnp.ones((), jnp.float32))
    return (item_loss, logit_grad.reshape(tokens.shape[0], LEN, VOCAB), grads[0], grads[1], grads[2], grads[3], grads[4], grads[5], grads[6], grads[7])
```

```python
import functools

import jax
import jax.numpy as jnp
from jax import lax
from jax.experimental import pallas as pl
from jax.experimental.pallas import tpu as pltpu
from jax.sharding import PartitionSpec as P

D = 512
HEADS = 8
HD = 64
FF = 2048
VOCAB = 256
BAND = 30
LEN = 640
LAYERS = 2
CH = 128
CHUNKS = LEN // CH
REACH = 32
TILE = 512
F32 = jnp.float32
BF16 = jnp.bfloat16


def mm(left, right):
    return jnp.dot(left, right, preferred_element_type=F32)


def mm_nt(left, right):
    return lax.dot_general(left, right, (((1,), (1,)), ((), ())), preferred_element_type=F32)


def norm_forward(v, gain):
    scale = lax.rsqrt(jnp.mean(v * v, axis=-1, keepdims=True) + 1e-05)
    return v * scale * gain


def norm_backward(v, gain, dy):
    scale = lax.rsqrt(jnp.mean(v * v, axis=-1, keepdims=True) + 1e-05)
    normed = v * scale
    dgain = jnp.sum(dy * normed, axis=0, keepdims=True)
    dyg = dy * gain
    dv = scale * (dyg - normed * jnp.mean(dyg * normed, axis=-1, keepdims=True))
    return dv, dgain


def gelu_parts(u):
    c = 0.7978845608028654
    square = u * u
    t = jnp.tanh(u * (c + (c * 0.044715) * square))
    half = 0.5 * (1.0 + t)
    value = u * half
    slope = half + 0.5 * u * (1.0 - t * t) * (c + (3.0 * c * 0.044715) * square)
    return value, slope


def feature_parts(u):
    low_exp = jnp.exp(jnp.minimum(u, 0.0))
    first = jnp.where(u > 0.0, u + 1.0, low_exp)
    second = jnp.tanh(u)
    return first, low_exp, second


def iotas(rows, cols, row0=0):
    r = lax.broadcasted_iota(jnp.int32, (rows, cols), 0) + row0
    c = lax.broadcasted_iota(jnp.int32, (rows, cols), 1)
    return r, c


def near_part(i, key_rows, query_cols):
    row0 = -REACH if i > 0 else 0
    scores = mm(key_rows, query_cols) * 0.125
    r, c = iotas(CH - row0, CH, row0)
    ok = (r <= c) & (c - r < BAND)
    scores = jnp.where(ok, scores, -1e30)
    peak = jnp.max(scores, axis=0, keepdims=True)
    weights = jnp.exp(scores - peak)
    return weights / jnp.sum(weights, axis=0, keepdims=True)


def causal_rows(i, block):
    row0 = -REACH if i > 0 else 0
    r, c = iotas(CH - row0, CH, row0)
    return jnp.where(r <= c, block, 0.0)


def mixture_chunk(i, key_nat, key_feat2, query_masked, query_feat2):
    t0, t1 = i * CH, (i + 1) * CH
    r0 = t0 - REACH if i > 0 else 0
    far = mm(key_feat2[:t1], query_feat2[:, t0:t1])
    near = near_part(i, key_nat[r0:t1], query_masked[:, t0:t1])
    bottom = (causal_rows(i, far[r0:]) + near).astype(BF16)
    if r0 == 0:
        return bottom, near
    return jnp.concatenate([far[:r0].astype(BF16), bottom], axis=0), near


def query_features(qT, inv1, inv2):
    first, slope1, second = feature_parts(qT.astype(F32))
    first_b, second_b = first.astype(BF16), second.astype(BF16)
    scaled = jnp.concatenate([first_b.astype(F32) * inv1, second_b.astype(F32) * inv2], axis=0)
    high = scaled.astype(BF16)
    rest = (scaled - high.astype(F32)).astype(BF16)
    return first_b, slope1, second, jnp.concatenate([high, rest], axis=0)


def masked_pair(part, e):
    zero = jnp.zeros_like(part)
    return jnp.concatenate([part, zero] if e == 0 else [zero, part], axis=0)


def step_kernel(
    tok_ref, tgt_ref, val_ref, table_ref, gm_ref, gf_ref, gz_ref, wm_ref, wo_ref, we_ref, wr_ref,
    loss_ref, lg_ref, dtable_ref, dgm_ref, dgf_ref, dgz_ref, dwm_ref, dwo_ref, dwe_ref, dwrt_ref,
    x_ref, x1_ref, dx_ref, kv_ref, pT_ref, kf_ref, inv1_ref, cum_ref, oT_ref, hT_ref, g_ref, gT_ref,
    wide_ref, a1k_ref, m_ref, d_ref, ds_ref, doT_ref, do_ref, dpT_ref, part_ref, w_ref, yb_ref, acc_ref,
    stage_ref, sem_ref,
):
    inv2 = 1.0 / (lax.broadcasted_iota(jnp.int32, (1, LEN), 1).astype(F32) + 1.0)

    def emit(slot, wait_first, value, dst):
        def copy():
            return pltpu.make_async_copy(stage_ref.at[slot], dst, sem_ref.at[slot])

        if wait_first is True:
            copy().wait()
        elif wait_first is not False:
            pl.when(wait_first)(lambda: copy().wait())
        stage_ref[slot] = value.astype(BF16)
        copy().start()

    vocab_ids = lax.broadcasted_iota(jnp.int32, (LEN, VOCAB), 1)
    hot = (vocab_ids == tok_ref[...]).astype(F32).astype(BF16)
    x_ref[0] = mm_nt(hot, table_ref[...])
    r, c = iotas(LEN, LEN)
    upper = (r <= c).astype(F32).astype(BF16)
    wide_ref[...] = upper

    def attention_forward(l):
        x = x_ref[l]
        h = norm_forward(x, gm_ref[l]).astype(BF16)
        hT_ref[l] = h.T
        for j in range(3):
            part = mm(h, wm_ref[l, :, j * TILE:(j + 1) * TILE]).astype(BF16)
            if j > 0:
                kv_ref[l, :, (j - 1) * TILE:j * TILE] = part
            pT_ref[l, j * TILE:(j + 1) * TILE, :] = part.T
        kT = pT_ref[l, D:2 * D, :].astype(F32)
        a1k_ref[...] = feature_parts(kT)[0].astype(BF16)
        for i in range(CHUNKS):
            t0, t1 = i * CH, (i + 1) * CH
            cum_ref[l, :, t0:t1] = mm(a1k_ref[:, :t1], wide_ref[:t1, t0:t1])

        def pair(p, carry):
            base = pl.multiple_of(p * CH, CH)
            for e in range(2):
                row = pl.multiple_of(base + e * HD, HD)
                qT = pT_ref[l, pl.ds(row, HD), :]
                kT = pT_ref[l, pl.ds(pl.multiple_of(D + row, HD), HD), :]
                vT = pT_ref[l, pl.ds(pl.multiple_of(2 * D + row, HD), HD), :]
                first_k, _, second_k = feature_parts(kT.astype(F32))
                key_feat = jnp.concatenate([first_k.astype(BF16), second_k.astype(BF16)], axis=0).T
                kf_ref[l, :, pl.ds(pl.multiple_of(2 * row, CH), CH)] = key_feat
                first_q = feature_parts(qT.astype(F32))[0].astype(BF16).astype(F32)
                total = jnp.sum(first_q * cum_ref[l, pl.ds(row, HD), :], axis=0, keepdims=True)
                inv1 = 1.0 / (total + 1.0)
                inv1_ref[l, 2 * p + e] = inv1
                query_feat2 = query_features(qT, inv1, inv2)[3]
                key_feat2 = jnp.concatenate([key_feat, key_feat], axis=1)
                key_nat = kv_ref[l, :, pl.ds(base, CH)]
                query_masked = masked_pair(qT, e)
                for i in range(CHUNKS):
                    t0, t1 = i * CH, (i + 1) * CH
                    mixture, _ = mixture_chunk(i, key_nat, key_feat2, query_masked, query_feat2)
                    oT_ref[l, pl.ds(row, HD), t0:t1] = mm(vT[:, :t1], mixture).astype(BF16)
            return carry

        lax.fori_loop(0, HEADS // 2, pair, 0)
        o = oT_ref[l].T
        x1_ref[l] = x_ref[l] + mm(o, wo_ref[l])

    def feed_forward(l):
        x1 = x1_ref[l]
        g_ref[l] = norm_forward(x1, gf_ref[l]).astype(BF16)
        gT_ref[l] = g_ref[l].T
        x_ref[l + 1] = x1

        def tile(j, carry):
            col = pl.multiple_of(j * TILE, TILE)
            active = gelu_parts(mm(g_ref[l], we_ref[l, :, pl.ds(col, TILE)]))[0].astype(BF16)
            x_ref[l + 1] += mm(active, wr_ref[l, pl.ds(col, TILE), :])
            return carry

        lax.fori_loop(0, FF // TILE, tile, 0)

    def head():
        x = x_ref[LAYERS]
        z = norm_forward(x, gz_ref[...]).astype(BF16)
        logits = mm(z, table_ref[...])
        tgt_hot = (vocab_ids == tgt_ref[...]).astype(F32)
        val = val_ref[...]
        peak = jnp.max(logits, axis=-1, keepdims=True)
        grown = jnp.exp(logits - peak)
        total = jnp.sum(grown, axis=-1, keepdims=True)
        lse = peak + jnp.log(total)
        picked = jnp.sum(logits * tgt_hot, axis=-1, keepdims=True)
        cross = (lse - picked) * val
        loss = jnp.sum(cross, axis=0, keepdims=True) / jnp.sum(val, axis=0, keepdims=True)
        loss_ref[...] = jnp.broadcast_to(loss, loss_ref.shape)
        grad_b = ((grown / total - tgt_hot) * val).astype(BF16)
        lg_ref[...] = grad_b
        dtable_ref[...] = mm(z.T, grad_b)
        dv, dgain = norm_backward(x, gz_ref[...], mm_nt(grad_b, table_ref[...]))
        dgz_ref[...] = dgain
        dx_ref[...] = dv

    def feed_backward(l):
        yb = dx_ref[...].astype(BF16)
        yb_ref[...] = yb
        ybT = yb.T
        doT_ref[...] = ybT
        acc_ref[...] = jnp.zeros_like(acc_ref)

        def tile(j, carry):
            col = pl.multiple_of(j * TILE, TILE)
            slot = lax.rem(j, 2)
            later = (j >= 2) if l == LAYERS - 1 else True
            value, slope = gelu_parts(mm(g_ref[l], we_ref[l, :, pl.ds(col, TILE)]))
            emit(slot, later, mm(doT_ref[...], value.astype(BF16)), dwrt_ref.at[l, :, pl.ds(col, TILE)])
            dact = mm_nt(yb_ref[...], wr_ref[l, pl.ds(col, TILE), :])
            dhid = (dact * slope).astype(BF16)
            emit(2 + slot, later, mm(gT_ref[l], dhid), dwe_ref.at[l, :, pl.ds(col, TILE)])
            acc_ref[...] += mm_nt(dhid, we_ref[l, :, pl.ds(col, TILE)])
            return carry

        lax.fori_loop(0, FF // TILE, tile, 0)
        dv, dgain = norm_backward(x1_ref[l], gf_ref[l], acc_ref[...])
        dgf_ref[l] = dgain
        dx_ref[...] += dv

    def attention_backward(l):
        yb = dx_ref[...].astype(BF16)
        yb_ref[...] = yb
        emit(0, True, mm(oT_ref[l], yb), dwo_ref.at[l])
        do_ref[...] = mm_nt(yb, wo_ref[l]).astype(BF16)
        doT_ref[...] = do_ref[...].T

        def pair(p, carry):
            base = pl.multiple_of(p * CH, CH)
            for e in range(2):
                row = pl.multiple_of(base + e * HD, HD)
                qT = pT_ref[l, pl.ds(row, HD), :]
                kT = pT_ref[l, pl.ds(pl.multiple_of(D + row, HD), HD), :]
                doT = doT_ref[pl.ds(row, HD), :]
                inv1 = inv1_ref[l, 2 * p + e]
                first_q, slope1_q, second_q, query_feat2 = query_features(qT, inv1, inv2)
                first_k, slope1_k, second_k = feature_parts(kT.astype(F32))
                key_featT = jnp.concatenate([first_k.astype(BF16), second_k.astype(BF16)], axis=0)
                key_feat = kf_ref[l, :, pl.ds(pl.multiple_of(2 * row, CH), CH)]
                key_feat2 = jnp.concatenate([key_feat, key_feat], axis=1)
                key_nat = kv_ref[l, :, pl.ds(base, CH)]
                value_nat = kv_ref[l, :, pl.ds(pl.multiple_of(D + base, CH), CH)]
                query_masked = masked_pair(qT, e)
                do_masked = masked_pair(doT, e)
                far_q, near_q = [], []
                for i in range(CHUNKS):
                    t0, t1 = i * CH, (i + 1) * CH
                    r0 = t0 - REACH if i > 0 else 0
                    mixture, near = mixture_chunk(i, key_nat, key_feat2, query_masked, query_feat2)
                    m_ref[e, :t1, t0:t1] = mixture
                    dm = mm(value_nat[:t1], do_masked[:, t0:t1])
                    bottom = dm[r0:]
                    dm_b = causal_rows(i, bottom).astype(BF16)
                    if r0 > 0:
                        dm_b = jnp.concatenate([dm[:r0].astype(BF16), dm_b], axis=0)
                    d_ref[e, :t1, t0:t1] = dm_b
                    weighted = near * bottom
                    dsum = jnp.sum(weighted, axis=0, keepdims=True)
                    ds = ((weighted - near * dsum) * 0.125).astype(BF16)
                    far_q.append(mm(key_featT[:, :t1], dm_b))
                    if i > 0:
                        before = jnp.concatenate([jnp.zeros((CH - REACH, CH), BF16), ds[:REACH]], axis=0)
                        ds_ref[e, t0 - CH:t0, CH:] = before
                        ds = ds[REACH:]
                        near_q.append(mm(kT[:, t0 - CH:t1], jnp.concatenate([before, ds], axis=0)))
                    else:
                        near_q.append(mm(kT[:, t0:t1], ds))
                    ds_ref[e, t0:t1, :CH] = ds
                farT = jnp.concatenate(far_q, axis=1)
                y1, y2 = farT[:HD], farT[HD:]
                first_qf = first_q.astype(F32)
                m = inv1 * jnp.sum(first_qf * y1, axis=0, keepdims=True)
                cum = cum_ref[l, pl.ds(row, HD), :]
                dq = jnp.concatenate(near_q, axis=1)
                dq = dq + (inv1 * (y1 - m * cum)) * slope1_q + (inv2 * y2) * (1.0 - second_q * second_q)
                dpT_ref[pl.ds(row, HD), :] = dq.astype(BF16)
                w_ref[pl.ds(row, HD), :] = (first_qf * (m * inv1)).astype(BF16)
                for i in range(CHUNKS):
                    t0, t1 = i * CH, (i + 1) * CH
                    far = mm_nt(query_feat2[:, t0:], d_ref[e, t0:t1, t0:])
                    far = far[:CH] + far[CH:]
                    t2 = min(t1 + CH, LEN)
                    near = mm_nt(qT[:, t0:t2], ds_ref[e, t0:t1, :t2 - t0])
                    dk = near + far[:HD] * slope1_k[:, t0:t1]
                    dk = dk + far[HD:] * (1.0 - second_k[:, t0:t1] * second_k[:, t0:t1])
                    part_ref[pl.ds(row, HD), t0:t1] = dk
                    dv = mm_nt(doT[:, t0:], m_ref[e, t0:t1, t0:])
                    dpT_ref[pl.ds(pl.multiple_of(2 * D + row, HD), HD), t0:t1] = dv.astype(BF16)
            return carry

        lax.fori_loop(0, HEADS // 2, pair, 0)
        kT = pT_ref[l, D:2 * D, :].astype(F32)
        slope1_k = jnp.exp(jnp.minimum(kT, 0.0))
        for i in range(CHUNKS):
            t0, t1 = i * CH, (i + 1) * CH
            back = mm_nt(w_ref[:, t0:], wide_ref[t0:t1, t0:])
            dk = part_ref[:, t0:t1] - back * slope1_k[:, t0:t1]
            dpT_ref[D:2 * D, t0:t1] = dk.astype(BF16)
        for j in range(3):
            tile = mm_nt(hT_ref[l], dpT_ref[j * TILE:(j + 1) * TILE, :])
            emit(1 + j, True, tile, dwm_ref.at[l, :, j * TILE:(j + 1) * TILE])
        dh = mm(wm_ref[l], dpT_ref[...]).T
        dv, dgain = norm_backward(x_ref[l], gm_ref[l], dh)
        dgm_ref[l] = dgain
        dx_ref[...] += dv

    for l in range(LAYERS):
        attention_forward(l)
        feed_forward(l)
    head()
    for l in reversed(range(LAYERS)):
        feed_backward(l)
        attention_backward(l)
    dtable_ref[...] += mm(dx_ref[...].astype(BF16).T, hot)
    for slot in range(4):
        pltpu.make_async_copy(stage_ref.at[slot], dwo_ref.at[0], sem_ref.at[slot]).wait()


def local_step(tok, tgt, val, table, gm, gf, gz, wm, wo, we, wr):
    vmem = pl.BlockSpec(memory_space=pltpu.VMEM)
    hbm = pl.BlockSpec(memory_space=pl.ANY)
    shape = jax.ShapeDtypeStruct
    return pl.pallas_call(
        step_kernel,
        out_shape=(
            shape((8, 128), F32),
            shape((LEN, VOCAB), BF16),
            shape((D, VOCAB), F32),
            shape((LAYERS, 1, D), F32),
            shape((LAYERS, 1, D), F32),
            shape((1, D), F32),
            shape((LAYERS, D, 3 * D), BF16),
            shape((LAYERS, D, D), BF16),
            shape((LAYERS, D, FF), BF16),
            shape((LAYERS, D, FF), BF16),
        ),
        in_specs=[vmem] * 11,
        out_specs=(vmem,) * 6 + (hbm,) * 4,
        scratch_shapes=[
            pltpu.VMEM((LAYERS + 1, LEN, D), F32),
            pltpu.VMEM((LAYERS, LEN, D), F32),
            pltpu.VMEM((LEN, D), F32),
            pltpu.VMEM((LAYERS, LEN, 2 * D), BF16),
            pltpu.VMEM((LAYERS, 3 * D, LEN), BF16),
            pltpu.VMEM((LAYERS, LEN, 2 * D), BF16),
            pltpu.VMEM((LAYERS, HEADS, 1, LEN), F32),
            pltpu.VMEM((LAYERS, D, LEN), F32),
            pltpu.VMEM((LAYERS, D, LEN), BF16),
            pltpu.VMEM((LAYERS, D, LEN), BF16),
            pltpu.VMEM((LAYERS, LEN, D), BF16),
            pltpu.VMEM((LAYERS, D, LEN), BF16),
            pltpu.VMEM((LEN, LEN), BF16),
            pltpu.VMEM((D, LEN), BF16),
            pltpu.VMEM((2, LEN, LEN), BF16),
            pltpu.VMEM((2, LEN, LEN), BF16),
            pltpu.VMEM((2, LEN, 2 * CH), BF16),
            pltpu.VMEM((D, LEN), BF16),
            pltpu.VMEM((LEN, D), BF16),
            pltpu.VMEM((3 * D, LEN), BF16),
            pltpu.VMEM((D, LEN), F32),
            pltpu.VMEM((D, LEN), BF16),
            pltpu.VMEM((LEN, D), BF16),
            pltpu.VMEM((LEN, D), F32),
            pltpu.VMEM((4, D, TILE), BF16),
            pltpu.SemaphoreType.DMA((4,)),
        ],
        compiler_params=pltpu.CompilerParams(vmem_limit_bytes=63 * 1024 * 1024),
        cost_estimate=pl.CostEstimate(flops=40_000_000_000, bytes_accessed=40_000_000, transcendentals=0),
        name="local_step",
    )(tok, tgt, val, table, gm, gf, gz, wm, wo, we, wr)


def body(
    tokens,
    padding_mask,
    embedding,
    mixer_weight,
    output_weight,
    mixer_gain,
    expand_weight,
    reduce_weight,
    feed_gain,
    final_gain,
):
    segments = lax.axis_size("section")
    segment_index = lax.axis_index("section")
    item_count = tokens.shape[0]
    assert item_count == segments
    slice_width = embedding.shape[1]

    token_row = lax.dynamic_index_in_dim(tokens, segment_index, 0, keepdims=False)
    mask_row = lax.dynamic_index_in_dim(padding_mask, segment_index, 0, keepdims=False)
    target_row = jnp.concatenate([token_row[1:], jnp.zeros((1,), jnp.int32)])
    valid_row = jnp.concatenate([mask_row[1:], jnp.zeros((1,), jnp.int32)]).astype(F32)

    def gather(block, dim):
        return lax.all_gather(block.astype(BF16), "dp", axis=dim, tiled=True)

    table = lax.all_gather(gather(embedding, 0), "section", axis=1, tiled=True)
    gains = gather(jnp.concatenate([mixer_gain, feed_gain, final_gain[None]], axis=0), 1).astype(F32)
    wm = gather(mixer_weight, 1)
    wo = gather(output_weight, 1)
    we = gather(expand_weight, 1)
    wr = gather(reduce_weight, 1)
    loss, lg, dtable, dgm, dgf, dgz, dwm, dwo, dwe, dwrt = local_step(
        token_row[:, None], target_row[:, None], valid_row[:, None], table,
        gains[0:2, None], gains[2:4, None], gains[4:5], wm, wo, we, wr,
    )
    item_loss = lax.all_gather(loss[0, 0], "section")
    parts = lg.reshape(LEN, segments, slice_width).transpose(1, 0, 2)
    logit_grad = lax.all_to_all(parts, "section", 0, 0, tiled=True).astype(F32)

    def shard(grad, dim):
        part = lax.psum_scatter(grad.astype(BF16), "dp", scatter_dimension=dim, tiled=True)
        return lax.psum(part, "section").astype(F32)

    table_part = lax.psum_scatter(dtable.astype(BF16), "dp", scatter_dimension=0, tiled=True)
    table_grad = lax.psum_scatter(table_part, "section", scatter_dimension=1, tiled=True).astype(F32)
    gain_grads = lax.psum_scatter(
        jnp.concatenate([dgm[:, 0], dgf[:, 0], dgz], axis=0), "dp", scatter_dimension=1, tiled=True
    )
    gain_grads = lax.psum(gain_grads, "section")
    return (
        item_loss,
        logit_grad,
        table_grad,
        shard(dwm, 1),
        shard(dwo, 1),
        gain_grads[0:2],
        shard(dwe, 1),
        jnp.swapaxes(shard(dwrt, 2), 1, 2),
        gain_grads[2:4],
        gain_grads[4],
    )


def solution(mesh):
    placed = (
        P("dp", None),
        P("dp", None),
        P("dp", "section"),
        P(None, "dp", None),
        P(None, "dp", None),
        P(None, "dp"),
        P(None, "dp", None),
        P(None, "dp", None),
        P(None, "dp"),
        P("dp"),
    )
    return jax.shard_map(
        body,
        mesh=mesh,
        in_specs=placed,
        out_specs=(
            P("dp"),
            P("dp", None, "section"),
            P("dp", "section"),
            P(None, "dp", None),
            P(None, "dp", None),
            P(None, "dp"),
            P(None, "dp", None),
            P(None, "dp", None),
            P(None, "dp"),
            P("dp"),
        ),
        check_vma=False,
    )
```

```python
import functools

import jax
import jax.numpy as jnp
from jax import lax
from jax.experimental import pallas as pl
from jax.experimental.pallas import tpu as pltpu
from jax.sharding import PartitionSpec as P

D = 512
HEADS = 8
HD = 64
FF = 2048
VOCAB = 256
BAND = 30
LEN = 640
LAYERS = 2
CH = 128
CHUNKS = LEN // CH
REACH = 32
TILE = 512
F32 = jnp.float32
BF16 = jnp.bfloat16


def mm(left, right):
    return jnp.dot(left, right, preferred_element_type=F32)


def mm_nt(left, right):
    return lax.dot_general(left, right, (((1,), (1,)), ((), ())), preferred_element_type=F32)


def norm_forward(v, gain):
    scale = lax.rsqrt(jnp.mean(v * v, axis=-1, keepdims=True) + 1e-05)
    return v * scale * gain


def norm_backward(v, gain, dy):
    scale = lax.rsqrt(jnp.mean(v * v, axis=-1, keepdims=True) + 1e-05)
    normed = v * scale
    dgain = jnp.sum(dy * normed, axis=0, keepdims=True)
    dyg = dy * gain
    dv = scale * (dyg - normed * jnp.mean(dyg * normed, axis=-1, keepdims=True))
    return dv, dgain


def gelu_parts(u):
    c = 0.7978845608028654
    square = u * u
    t = jnp.tanh(u * (c + (c * 0.044715) * square))
    half = 0.5 * (1.0 + t)
    value = u * half
    slope = half + 0.5 * u * (1.0 - t * t) * (c + (3.0 * c * 0.044715) * square)
    return value, slope


def feature_parts(u):
    low_exp = jnp.exp(jnp.minimum(u, 0.0))
    first = jnp.where(u > 0.0, u + 1.0, low_exp)
    second = jnp.tanh(u)
    return first, low_exp, second


def iotas(rows, cols, row0=0):
    r = lax.broadcasted_iota(jnp.int32, (rows, cols), 0) + row0
    c = lax.broadcasted_iota(jnp.int32, (rows, cols), 1)
    return r, c


def near_part(i, key_rows, query_cols):
    row0 = -REACH if i > 0 else 0
    scores = mm(key_rows, query_cols) * 0.125
    r, c = iotas(CH - row0, CH, row0)
    ok = (r <= c) & (c - r < BAND)
    scores = jnp.where(ok, scores, -1e30)
    peak = jnp.max(scores, axis=0, keepdims=True)
    weights = jnp.exp(scores - peak)
    return weights / jnp.sum(weights, axis=0, keepdims=True)


def causal_rows(i, block):
    row0 = -REACH if i > 0 else 0
    r, c = iotas(CH - row0, CH, row0)
    return jnp.where(r <= c, block, 0.0)


def mixture_chunk(i, key_nat, key_feat2, query_masked, query_feat2):
    t0, t1 = i * CH, (i + 1) * CH
    r0 = t0 - REACH if i > 0 else 0
    far = mm(key_feat2[:t1], query_feat2[:, t0:t1])
    near = near_part(i, key_nat[r0:t1], query_masked[:, t0:t1])
    bottom = (causal_rows(i, far[r0:]) + near).astype(BF16)
    if r0 == 0:
        return bottom, near
    return jnp.concatenate([far[:r0].astype(BF16), bottom], axis=0), near


def query_features(qT, inv1, inv2):
    first, slope1, second = feature_parts(qT.astype(F32))
    first_b, second_b = first.astype(BF16), second.astype(BF16)
    scaled = jnp.concatenate([first_b.astype(F32) * inv1, second_b.astype(F32) * inv2], axis=0)
    high = scaled.astype(BF16)
    rest = (scaled - high.astype(F32)).astype(BF16)
    return first_b, slope1, second, jnp.concatenate([high, rest], axis=0)


def masked_pair(part, e):
    zero = jnp.zeros_like(part)
    return jnp.concatenate([part, zero] if e == 0 else [zero, part], axis=0)


class Links:
    def __init__(self, pieces, send_sem, recv_sem):
        self.pieces, self.send_sem, self.recv_sem = pieces, send_sem, recv_sem
        d = lax.axis_index("dp")
        core, x, y = d % 2, (d // 2) % 2, d // 4
        self.d = d
        self.core_n, self.x_n, self.y_n = d + 1 - 2 * core, d + 2 - 4 * x, d + 4 - 8 * y
        self.diag = self.x_n + 4 - 8 * y

    def copy(self, n, kind):
        ref, rows, split = self.pieces[n]
        d, core_n, x_n, y_n, diag = self.d, self.core_n, self.x_n, self.y_n, self.diag
        block = (d, d, y_n, x_n, d, x_n, y_n, diag, diag)[kind]
        target = (x_n, y_n, x_n, y_n, core_n, core_n, core_n, core_n, core_n)[kind]
        view = ref.at[pl.ds(pl.multiple_of(block * rows, rows), rows)]
        if kind in (2, 7):
            view = view.at[:, :split]
        if kind in (3, 8):
            view = view.at[:, split:]
        return pltpu.make_async_remote_copy(
            src_ref=view, dst_ref=view, send_sem=self.send_sem.at[n, kind], recv_sem=self.recv_sem.at[n, kind],
            device_id={"dp": target}, device_id_type=pl.DeviceIdType.MESH,
        )

    def own(self, *ns):
        for n in ns:
            for kind in (0, 1, 4):
                self.copy(n, kind).start()

    def first(self, *ns):
        for n in ns:
            self.copy(n, 0).wait_recv()
            self.copy(n, 3).start()
            self.copy(n, 1).wait_recv()
            self.copy(n, 2).start()
            self.copy(n, 5).start()
            self.copy(n, 6).start()

    def second(self, *ns):
        for n in ns:
            self.copy(n, 2).wait_recv()
            self.copy(n, 7).start()
            self.copy(n, 3).wait_recv()
            self.copy(n, 8).start()

    def ready(self, *ns):
        for n in ns:
            for kind in (4, 5, 6, 7, 8):
                self.copy(n, kind).wait_recv()

    def finish(self):
        for n in range(len(self.pieces)):
            for kind in range(9):
                self.copy(n, kind).wait_send()


def step_kernel(linked, *refs):
    names = (LINKED_IN if linked else PLAIN_IN) + (LINKED_OUT if linked else PLAIN_OUT)
    names += tuple(SCRATCH) + (tuple(LINKED_SCRATCH) if linked else ())
    step_body(linked, **dict(zip(names, refs, strict=True)))


def step_body(
    linked, tok, tgt, val, loss, lg, dtable, dgm, dgf, dgz, dwm, dwo, dwe, dwrt,
    x, x1, dx, kv, pT, kf, inv1s, cum, oT, hT, g, gT, wide, a1k, m, d, ds, doT, do, dpT, part, w, yb, acc, stage, sem,
    table=None, gm=None, gf=None, gz=None, wm=None, wo=None, we=None, wr=None,
    small=None, wm_s=None, wo_s=None, we_s=None, wr_s=None, tz=None, gains=None, lgs=None, losss=None,
    send_sem=None, recv_sem=None, zsend=None, zrecv=None,
):
    tok_ref, tgt_ref, val_ref, table_ref = tok, tgt, val, table
    gm_ref, gf_ref, gz_ref = gm, gf, gz
    wm_ref, wo_ref, we_ref, wr_ref = wm, wo, we, wr
    loss_ref, lg_ref, dtable_ref, dgm_ref, dgf_ref, dgz_ref = loss, lg, dtable, dgm, dgf, dgz
    dwm_ref, dwo_ref, dwe_ref, dwrt_ref = dwm, dwo, dwe, dwrt
    x_ref, x1_ref, dx_ref, kv_ref, pT_ref, kf_ref, inv1_ref, cum_ref = x, x1, dx, kv, pT, kf, inv1s, cum
    oT_ref, hT_ref, g_ref, gT_ref, wide_ref, a1k_ref, m_ref, d_ref, ds_ref = oT, hT, g, gT, wide, a1k, m, d, ds
    doT_ref, do_ref, dpT_ref, part_ref, w_ref, yb_ref, acc_ref = doT, do, dpT, part, w, yb, acc
    stage_ref, sem_ref = stage, sem
    r, c = iotas(LEN, LEN)
    upper = (r <= c).astype(F32).astype(BF16)

    if linked:
        zi = lax.axis_index("section")
        links = Links(
            [(table_ref, 64, 256)]
            + [
                entry
                for l in range(LAYERS)
                for entry in (
                    (wm_ref.at[l], 64, 3 * D // 2),
                    (wo_ref.at[l], 64, D // 2),
                    (we_ref.at[l], 64, FF // 2),
                    (wr_ref.at[l], 256, D // 2),
                )
            ],
            send_sem, recv_sem,
        )

        def along_z(n, k, src_of, dst):
            target = (zi + k) % 4
            return pltpu.make_async_remote_copy(
                src_ref=src_of(target), dst_ref=dst.at[zi], send_sem=zsend.at[n, k - 1], recv_sem=zrecv.at[n, k - 1],
                device_id={"section": target}, device_id_type=pl.DeviceIdType.MESH,
            )

        def table_copy(k):
            return along_z(0, k, lambda target: tz.at[zi], tz)

        def lg_copy(k):
            return along_z(1, k, lambda target: lgs.at[target], lg_ref)

        def loss_copy(k):
            return along_z(2, k, lambda target: losss, loss_ref)

        barrier = pltpu.get_barrier_semaphore()
        for target in (links.core_n, links.x_n, links.y_n):
            pl.semaphore_signal(barrier, inc=1, device_id={"dp": target}, device_id_type=pl.DeviceIdType.MESH)
        for k in (1, 2, 3):
            pl.semaphore_signal(barrier, inc=1, device_id={"section": (zi + k) % 4}, device_id_type=pl.DeviceIdType.MESH)
        pl.semaphore_wait(barrier, 6)

        own64 = pl.ds(pl.multiple_of(links.d * 64, 64), 64)
        own256 = pl.ds(pl.multiple_of(links.d * 256, 256), 256)
        small_b = small[...].astype(BF16)
        tz[zi] = small_b
        for k in (1, 2, 3):
            table_copy(k).start()
        wm_ref[0, own64] = wm_s[0].astype(BF16)
        links.own(1)
        wo_ref[0, own64] = wo_s[0].astype(BF16)
        we_ref[0, own64] = we_s[0].astype(BF16)
        wr_ref[0, own256] = wr_s[0].astype(BF16)
        for k in (1, 2, 3):
            table_copy(k).wait_recv()
        pad = jnp.zeros((64, 64), BF16)
        table_ref[own64, :] = jnp.concatenate([tz[i][:, :64] for i in range(4)] + [small_b[:, 64:], pad], axis=1)
        links.own(0, 2, 3)
        wide_ref[...] = upper
        wm_ref[1, own64] = wm_s[1].astype(BF16)
        wo_ref[1, own64] = wo_s[1].astype(BF16)
        we_ref[1, own64] = we_s[1].astype(BF16)
        wr_ref[1, own256] = wr_s[1].astype(BF16)
        links.first(1, 0)
        links.second(1, 0)
        links.own(4)
        links.ready(0)
        gains[...] = table_ref[:, 256:].astype(F32).T
        table_ref = table_ref.at[:, :256]
        gm_ref, gf_ref, gz_ref = [gains[i:i + 1] for i in range(2)], [gains[i:i + 1] for i in range(2, 4)], gains[4:5]
        links.ready(1)
    else:
        wide_ref[...] = upper
        gm_ref, gf_ref, gz_ref = [gm_ref[i] for i in range(2)], [gf_ref[i] for i in range(2)], gz_ref[...]

    def service(step, index=None):
        if not linked:
            return
        for at, act in SERVICE.get(step, {}).items():
            def run(act=act):
                for name, ns in act:
                    getattr(links, name)(*ns)
            if at is None:
                run()
            else:
                pl.when(index == at)(run)

    inv2 = 1.0 / (lax.broadcasted_iota(jnp.int32, (1, LEN), 1).astype(F32) + 1.0)

    def emit(slot, wait_first, value, dst):
        def copy():
            return pltpu.make_async_copy(stage_ref.at[slot], dst, sem_ref.at[slot])

        if wait_first is True:
            copy().wait()
        elif wait_first is not False:
            pl.when(wait_first)(lambda: copy().wait())
        stage_ref[slot] = value.astype(BF16)
        copy().start()

    vocab_ids = lax.broadcasted_iota(jnp.int32, (LEN, VOCAB), 1)
    hot = (vocab_ids == tok_ref[...]).astype(F32).astype(BF16)
    x_ref[0] = mm_nt(hot, table_ref[...])

    def attention_forward(l):
        x = x_ref[l]
        h = norm_forward(x, gm_ref[l]).astype(BF16)
        hT_ref[l] = h.T
        for j in range(3):
            part = mm(h, wm_ref[l, :, j * TILE:(j + 1) * TILE]).astype(BF16)
            if j > 0:
                kv_ref[l, :, (j - 1) * TILE:j * TILE] = part
            pT_ref[l, j * TILE:(j + 1) * TILE, :] = part.T
        service(("mixer", l))
        kT = pT_ref[l, D:2 * D, :].astype(F32)
        a1k_ref[...] = feature_parts(kT)[0].astype(BF16)
        for i in range(CHUNKS):
            t0, t1 = i * CH, (i + 1) * CH
            cum_ref[l, :, t0:t1] = mm(a1k_ref[:, :t1], wide_ref[:t1, t0:t1])

        def pair(p, carry):
            base = pl.multiple_of(p * CH, CH)
            for e in range(2):
                row = pl.multiple_of(base + e * HD, HD)
                qT = pT_ref[l, pl.ds(row, HD), :]
                kT = pT_ref[l, pl.ds(pl.multiple_of(D + row, HD), HD), :]
                vT = pT_ref[l, pl.ds(pl.multiple_of(2 * D + row, HD), HD), :]
                first_k, _, second_k = feature_parts(kT.astype(F32))
                key_feat = jnp.concatenate([first_k.astype(BF16), second_k.astype(BF16)], axis=0).T
                kf_ref[l, :, pl.ds(pl.multiple_of(2 * row, CH), CH)] = key_feat
                first_q = feature_parts(qT.astype(F32))[0].astype(BF16).astype(F32)
                total = jnp.sum(first_q * cum_ref[l, pl.ds(row, HD), :], axis=0, keepdims=True)
                inv1 = 1.0 / (total + 1.0)
                inv1_ref[l, 2 * p + e] = inv1
                query_feat2 = query_features(qT, inv1, inv2)[3]
                key_feat2 = jnp.concatenate([key_feat, key_feat], axis=1)
                key_nat = kv_ref[l, :, pl.ds(base, CH)]
                query_masked = masked_pair(qT, e)
                for i in range(CHUNKS):
                    t0, t1 = i * CH, (i + 1) * CH
                    mixture, _ = mixture_chunk(i, key_nat, key_feat2, query_masked, query_feat2)
                    oT_ref[l, pl.ds(row, HD), t0:t1] = mm(vT[:, :t1], mixture).astype(BF16)
            service(("pair", l), p)
            return carry

        lax.fori_loop(0, HEADS // 2, pair, 0)
        service(("output", l))
        o = oT_ref[l].T
        x1_ref[l] = x_ref[l] + mm(o, wo_ref[l])

    def feed_forward(l):
        x1 = x1_ref[l]
        g_ref[l] = norm_forward(x1, gf_ref[l]).astype(BF16)
        gT_ref[l] = g_ref[l].T
        x_ref[l + 1] = x1
        service(("feed", l))

        def tile(j, carry):
            col = pl.multiple_of(j * TILE, TILE)
            active = gelu_parts(mm(g_ref[l], we_ref[l, :, pl.ds(col, TILE)]))[0].astype(BF16)
            x_ref[l + 1] += mm(active, wr_ref[l, pl.ds(col, TILE), :])
            service(("tile", l), j)
            return carry

        lax.fori_loop(0, FF // TILE, tile, 0)

    def head():
        x = x_ref[LAYERS]
        z = norm_forward(x, gz_ref).astype(BF16)
        logits = mm(z, table_ref[...])
        tgt_hot = (vocab_ids == tgt_ref[...]).astype(F32)
        val = val_ref[...]
        peak = jnp.max(logits, axis=-1, keepdims=True)
        grown = jnp.exp(logits - peak)
        total = jnp.sum(grown, axis=-1, keepdims=True)
        lse = peak + jnp.log(total)
        picked = jnp.sum(logits * tgt_hot, axis=-1, keepdims=True)
        cross = (lse - picked) * val
        loss = jnp.sum(cross, axis=0, keepdims=True) / jnp.sum(val, axis=0, keepdims=True)
        loss = jnp.broadcast_to(loss, (8, 128))
        grad_b = ((grown / total - tgt_hot) * val).astype(BF16)
        if linked:
            losss[...] = loss
            for i in range(4):
                lgs[i] = grad_b[:, 64 * i:64 * i + 64]
            for k in (1, 2, 3):
                lg_copy(k).start()
                loss_copy(k).start()
            pltpu.make_async_copy(lgs.at[zi], lg_ref.at[zi], zsend.at[1, 3]).start()
            pltpu.make_async_copy(losss, loss_ref.at[zi], zsend.at[2, 3]).start()
        else:
            loss_ref[...] = loss
            lg_ref[...] = grad_b
        dtable_ref[...] = mm(z.T, grad_b)
        dv, dgain = norm_backward(x, gz_ref, mm_nt(grad_b, table_ref[...]))
        dgz_ref[...] = dgain
        dx_ref[...] = dv

    def feed_backward(l):
        yb = dx_ref[...].astype(BF16)
        yb_ref[...] = yb
        ybT = yb.T
        doT_ref[...] = ybT
        acc_ref[...] = jnp.zeros_like(acc_ref)

        def tile(j, carry):
            col = pl.multiple_of(j * TILE, TILE)
            slot = lax.rem(j, 2)
            later = (j >= 2) if l == LAYERS - 1 else True
            value, slope = gelu_parts(mm(g_ref[l], we_ref[l, :, pl.ds(col, TILE)]))
            emit(slot, later, mm(doT_ref[...], value.astype(BF16)), dwrt_ref.at[l, :, pl.ds(col, TILE)])
            dact = mm_nt(yb_ref[...], wr_ref[l, pl.ds(col, TILE), :])
            dhid = (dact * slope).astype(BF16)
            emit(2 + slot, later, mm(gT_ref[l], dhid), dwe_ref.at[l, :, pl.ds(col, TILE)])
            acc_ref[...] += mm_nt(dhid, we_ref[l, :, pl.ds(col, TILE)])
            return carry

        lax.fori_loop(0, FF // TILE, tile, 0)
        dv, dgain = norm_backward(x1_ref[l], gf_ref[l], acc_ref[...])
        dgf_ref[l] = dgain
        dx_ref[...] += dv

    def attention_backward(l):
        yb = dx_ref[...].astype(BF16)
        yb_ref[...] = yb
        emit(0, True, mm(oT_ref[l], yb), dwo_ref.at[l])
        do_ref[...] = mm_nt(yb, wo_ref[l]).astype(BF16)
        doT_ref[...] = do_ref[...].T

        def pair(p, carry):
            base = pl.multiple_of(p * CH, CH)
            for e in range(2):
                row = pl.multiple_of(base + e * HD, HD)
                qT = pT_ref[l, pl.ds(row, HD), :]
                kT = pT_ref[l, pl.ds(pl.multiple_of(D + row, HD), HD), :]
                doT = doT_ref[pl.ds(row, HD), :]
                inv1 = inv1_ref[l, 2 * p + e]
                first_q, slope1_q, second_q, query_feat2 = query_features(qT, inv1, inv2)
                first_k, slope1_k, second_k = feature_parts(kT.astype(F32))
                key_featT = jnp.concatenate([first_k.astype(BF16), second_k.astype(BF16)], axis=0)
                key_feat = kf_ref[l, :, pl.ds(pl.multiple_of(2 * row, CH), CH)]
                key_feat2 = jnp.concatenate([key_feat, key_feat], axis=1)
                key_nat = kv_ref[l, :, pl.ds(base, CH)]
                value_nat = kv_ref[l, :, pl.ds(pl.multiple_of(D + base, CH), CH)]
                query_masked = masked_pair(qT, e)
                do_masked = masked_pair(doT, e)
                far_q, near_q = [], []
                for i in range(CHUNKS):
                    t0, t1 = i * CH, (i + 1) * CH
                    r0 = t0 - REACH if i > 0 else 0
                    mixture, near = mixture_chunk(i, key_nat, key_feat2, query_masked, query_feat2)
                    m_ref[e, :t1, t0:t1] = mixture
                    dm = mm(value_nat[:t1], do_masked[:, t0:t1])
                    bottom = dm[r0:]
                    dm_b = causal_rows(i, bottom).astype(BF16)
                    if r0 > 0:
                        dm_b = jnp.concatenate([dm[:r0].astype(BF16), dm_b], axis=0)
                    d_ref[e, :t1, t0:t1] = dm_b
                    weighted = near * bottom
                    dsum = jnp.sum(weighted, axis=0, keepdims=True)
                    ds = ((weighted - near * dsum) * 0.125).astype(BF16)
                    far_q.append(mm(key_featT[:, :t1], dm_b))
                    if i > 0:
                        before = jnp.concatenate([jnp.zeros((CH - REACH, CH), BF16), ds[:REACH]], axis=0)
                        ds_ref[e, t0 - CH:t0, CH:] = before
                        ds = ds[REACH:]
                        near_q.append(mm(kT[:, t0 - CH:t1], jnp.concatenate([before, ds], axis=0)))
                    else:
                        near_q.append(mm(kT[:, t0:t1], ds))
                    ds_ref[e, t0:t1, :CH] = ds
                farT = jnp.concatenate(far_q, axis=1)
                y1, y2 = farT[:HD], farT[HD:]
                first_qf = first_q.astype(F32)
                m = inv1 * jnp.sum(first_qf * y1, axis=0, keepdims=True)
                cum = cum_ref[l, pl.ds(row, HD), :]
                dq = jnp.concatenate(near_q, axis=1)
                dq = dq + (inv1 * (y1 - m * cum)) * slope1_q + (inv2 * y2) * (1.0 - second_q * second_q)
                dpT_ref[pl.ds(row, HD), :] = dq.astype(BF16)
                w_ref[pl.ds(row, HD), :] = (first_qf * (m * inv1)).astype(BF16)
                for i in range(CHUNKS):
                    t0, t1 = i * CH, (i + 1) * CH
                    far = mm_nt(query_feat2[:, t0:], d_ref[e, t0:t1, t0:])
                    far = far[:CH] + far[CH:]
                    t2 = min(t1 + CH, LEN)
                    near = mm_nt(qT[:, t0:t2], ds_ref[e, t0:t1, :t2 - t0])
                    dk = near + far[:HD] * slope1_k[:, t0:t1]
                    dk = dk + far[HD:] * (1.0 - second_k[:, t0:t1] * second_k[:, t0:t1])
                    part_ref[pl.ds(row, HD), t0:t1] = dk
                    dv = mm_nt(doT[:, t0:], m_ref[e, t0:t1, t0:])
                    dpT_ref[pl.ds(pl.multiple_of(2 * D + row, HD), HD), t0:t1] = dv.astype(BF16)
            return carry

        lax.fori_loop(0, HEADS // 2, pair, 0)
        kT = pT_ref[l, D:2 * D, :].astype(F32)
        slope1_k = jnp.exp(jnp.minimum(kT, 0.0))
        for i in range(CHUNKS):
            t0, t1 = i * CH, (i + 1) * CH
            back = mm_nt(w_ref[:, t0:], wide_ref[t0:t1, t0:])
            dk = part_ref[:, t0:t1] - back * slope1_k[:, t0:t1]
            dpT_ref[D:2 * D, t0:t1] = dk.astype(BF16)
        for j in range(3):
            tile = mm_nt(hT_ref[l], dpT_ref[j * TILE:(j + 1) * TILE, :])
            emit(1 + j, True, tile, dwm_ref.at[l, :, j * TILE:(j + 1) * TILE])
        dh = mm(wm_ref[l], dpT_ref[...]).T
        dv, dgain = norm_backward(x_ref[l], gm_ref[l], dh)
        dgm_ref[l] = dgain
        dx_ref[...] += dv

    for l in range(LAYERS):
        service(("layer", l))
        attention_forward(l)
        feed_forward(l)
    head()
    for l in reversed(range(LAYERS)):
        feed_backward(l)
        attention_backward(l)
    dtable_ref[...] += mm(dx_ref[...].astype(BF16).T, hot)
    for slot in range(4):
        pltpu.make_async_copy(stage_ref.at[slot], dwo_ref.at[0], sem_ref.at[slot]).wait()
    if linked:
        pltpu.make_async_copy(lgs.at[zi], lg_ref.at[zi], zsend.at[1, 3]).wait()
        pltpu.make_async_copy(losss, loss_ref.at[zi], zsend.at[2, 3]).wait()
        for k in (1, 2, 3):
            table_copy(k).wait_send()
            lg_copy(k).wait()
            loss_copy(k).wait()
        links.finish()


SERVICE = {
    ("mixer", 0): {None: (("first", (2, 3)), ("own", (5,)))},
    ("pair", 0): {
        0: (("second", (2, 3)),),
        1: (("first", (4,)), ("own", (6, 7))),
        2: (("second", (4,)), ("ready", (2, 3))),
        3: (("first", (5,)),),
    },
    ("feed", 0): {None: (("ready", (4,)), ("second", (5,)), ("own", (8,)))},
    ("tile", 0): {1: (("first", (6, 7)),), 2: (("second", (6,)),), 3: (("second", (7,)),)},
    ("layer", 1): {None: (("ready", (5,)),)},
    ("mixer", 1): {None: (("first", (8,)),)},
    ("pair", 1): {1: (("second", (8,)),)},
    ("output", 1): {None: (("ready", (6,)),)},
    ("feed", 1): {None: (("ready", (7, 8)),)},
}
PLAIN_IN = ("tok", "tgt", "val", "table", "gm", "gf", "gz", "wm", "wo", "we", "wr")
PLAIN_OUT = ("loss", "lg", "dtable", "dgm", "dgf", "dgz", "dwm", "dwo", "dwe", "dwrt")
LINKED_IN = ("tok", "tgt", "val", "small", "wm_s", "wo_s", "we_s", "wr_s")
LINKED_OUT = PLAIN_OUT
SCRATCH = dict(
    x=pltpu.VMEM((LAYERS + 1, LEN, D), F32),
    x1=pltpu.VMEM((LAYERS, LEN, D), F32),
    dx=pltpu.VMEM((LEN, D), F32),
    kv=pltpu.VMEM((LAYERS, LEN, 2 * D), BF16),
    pT=pltpu.VMEM((LAYERS, 3 * D, LEN), BF16),
    kf=pltpu.VMEM((LAYERS, LEN, 2 * D), BF16),
    inv1s=pltpu.VMEM((LAYERS, HEADS, 1, LEN), F32),
    cum=pltpu.VMEM((LAYERS, D, LEN), F32),
    oT=pltpu.VMEM((LAYERS, D, LEN), BF16),
    hT=pltpu.VMEM((LAYERS, D, LEN), BF16),
    g=pltpu.VMEM((LAYERS, LEN, D), BF16),
    gT=pltpu.VMEM((LAYERS, D, LEN), BF16),
    wide=pltpu.VMEM((LEN, LEN), BF16),
    a1k=pltpu.VMEM((D, LEN), BF16),
    m=pltpu.VMEM((2, LEN, LEN), BF16),
    d=pltpu.VMEM((2, LEN, LEN), BF16),
    ds=pltpu.VMEM((2, LEN, 2 * CH), BF16),
    doT=pltpu.VMEM((D, LEN), BF16),
    do=pltpu.VMEM((LEN, D), BF16),
    dpT=pltpu.VMEM((3 * D, LEN), BF16),
    part=pltpu.VMEM((D, LEN), F32),
    w=pltpu.VMEM((D, LEN), BF16),
    yb=pltpu.VMEM((LEN, D), BF16),
    acc=pltpu.VMEM((LEN, D), F32),
    stage=pltpu.VMEM((4, D, TILE), BF16),
    sem=pltpu.SemaphoreType.DMA((4,)),
)
LINKED_SCRATCH = dict(
    table=pltpu.VMEM((D, 384), BF16),
    wm=pltpu.VMEM((LAYERS, D, 3 * D), BF16),
    wo=pltpu.VMEM((LAYERS, D, D), BF16),
    we=pltpu.VMEM((LAYERS, D, FF), BF16),
    wr=pltpu.VMEM((LAYERS, FF, D), BF16),
    tz=pltpu.VMEM((4, 64, 128), BF16),
    gains=pltpu.VMEM((128, D), F32),
    lgs=pltpu.VMEM((4, LEN, 64), BF16),
    losss=pltpu.VMEM((8, 128), F32),
    send_sem=pltpu.SemaphoreType.DMA((9, 9)),
    recv_sem=pltpu.SemaphoreType.DMA((9, 9)),
    zsend=pltpu.SemaphoreType.DMA((3, 4)),
    zrecv=pltpu.SemaphoreType.DMA((3, 4)),
)


def local_step(linked, *operands):
    vmem = pl.BlockSpec(memory_space=pltpu.VMEM)
    hbm = pl.BlockSpec(memory_space=pl.ANY)
    shape = jax.ShapeDtypeStruct
    scratch = dict(SCRATCH, **LINKED_SCRATCH) if linked else SCRATCH
    if linked:
        first_out = (shape((4, 8, 128), F32), shape((4, LEN, 64), BF16))
    else:
        first_out = (shape((8, 128), F32), shape((LEN, VOCAB), BF16))
    return pl.pallas_call(
        functools.partial(step_kernel, linked),
        out_shape=first_out
        + (
            shape((D, VOCAB), F32),
            shape((LAYERS, 1, D), F32),
            shape((LAYERS, 1, D), F32),
            shape((1, D), F32),
            shape((LAYERS, D, 3 * D), BF16),
            shape((LAYERS, D, D), BF16),
            shape((LAYERS, D, FF), BF16),
            shape((LAYERS, D, FF), BF16),
        ),
        in_specs=[vmem] * len(operands),
        out_specs=(hbm if linked else vmem,) * 2 + (vmem,) * 4 + (hbm,) * 4,
        scratch_shapes=list(scratch.values()),
        compiler_params=pltpu.CompilerParams(
            vmem_limit_bytes=63 * 1024 * 1024,
            collective_id=0 if linked else None,
            has_side_effects=linked,
        ),
        cost_estimate=pl.CostEstimate(flops=40_000_000_000, bytes_accessed=40_000_000, transcendentals=0),
        name="local_step",
    )(*operands)


def body(
    tokens,
    padding_mask,
    embedding,
    mixer_weight,
    output_weight,
    mixer_gain,
    expand_weight,
    reduce_weight,
    feed_gain,
    final_gain,
):
    segments = lax.axis_size("section")
    segment_index = lax.axis_index("section")
    item_count = tokens.shape[0]
    assert item_count == segments
    slice_width = embedding.shape[1]

    token_row = lax.dynamic_index_in_dim(tokens, segment_index, 0, keepdims=False)
    mask_row = lax.dynamic_index_in_dim(padding_mask, segment_index, 0, keepdims=False)
    target_row = jnp.concatenate([token_row[1:], jnp.zeros((1,), jnp.int32)])
    valid_row = jnp.concatenate([mask_row[1:], jnp.zeros((1,), jnp.int32)]).astype(F32)

    columns = (token_row[:, None], target_row[:, None], valid_row[:, None])
    linked = segments == 4 and lax.axis_size("dp") == 8
    if linked:
        small = jnp.concatenate(
            [embedding, mixer_gain.T, feed_gain.T, final_gain[:, None], jnp.zeros((embedding.shape[0], 59), F32)], axis=1
        )
        loss, lg, dtable, dgm, dgf, dgz, dwm, dwo, dwe, dwrt = local_step(
            True, *columns, small, mixer_weight, output_weight, expand_weight, reduce_weight
        )
        item_loss = loss[:, 0, 0]
        logit_grad = lg.astype(F32)
    else:

        def gather(block, dim):
            return lax.all_gather(block.astype(BF16), "dp", axis=dim, tiled=True)

        table = lax.all_gather(gather(embedding, 0), "section", axis=1, tiled=True)
        gains = gather(jnp.concatenate([mixer_gain, feed_gain, final_gain[None]], axis=0), 1).astype(F32)
        loss, lg, dtable, dgm, dgf, dgz, dwm, dwo, dwe, dwrt = local_step(
            False, *columns, table, gains[0:2, None], gains[2:4, None], gains[4:5],
            gather(mixer_weight, 1), gather(output_weight, 1), gather(expand_weight, 1), gather(reduce_weight, 1),
        )
        item_loss = lax.all_gather(loss[0, 0], "section")
        parts = lg.reshape(LEN, segments, slice_width).transpose(1, 0, 2)
        logit_grad = lax.all_to_all(parts, "section", 0, 0, tiled=True).astype(F32)

    def shard(grad, dim):
        part = lax.psum_scatter(grad.astype(BF16), "dp", scatter_dimension=dim, tiled=True)
        return lax.psum(part, "section").astype(F32)

    table_part = lax.psum_scatter(dtable.astype(BF16), "dp", scatter_dimension=0, tiled=True)
    table_grad = lax.psum_scatter(table_part, "section", scatter_dimension=1, tiled=True).astype(F32)
    gain_grads = lax.psum_scatter(
        jnp.concatenate([dgm[:, 0], dgf[:, 0], dgz], axis=0), "dp", scatter_dimension=1, tiled=True
    )
    gain_grads = lax.psum(gain_grads, "section")
    return (
        item_loss,
        logit_grad,
        table_grad,
        shard(dwm, 1),
        shard(dwo, 1),
        gain_grads[0:2],
        shard(dwe, 1),
        jnp.swapaxes(shard(dwrt, 2), 1, 2),
        gain_grads[2:4],
        gain_grads[4],
    )


def solution(mesh):
    placed = (
        P("dp", None),
        P("dp", None),
        P("dp", "section"),
        P(None, "dp", None),
        P(None, "dp", None),
        P(None, "dp"),
        P(None, "dp", None),
        P(None, "dp", None),
        P(None, "dp"),
        P("dp"),
    )
    return jax.shard_map(
        body,
        mesh=mesh,
        in_specs=placed,
        out_specs=(
            P("dp"),
            P("dp", None, "section"),
            P("dp", "section"),
            P(None, "dp", None),
            P(None, "dp", None),
            P(None, "dp"),
            P(None, "dp", None),
            P(None, "dp", None),
            P(None, "dp"),
            P("dp"),
        ),
        check_vma=False,
    )
```

```python
import functools

import jax
import jax.numpy as jnp
from jax import lax
from jax.experimental import pallas as pl
from jax.experimental.pallas import tpu as pltpu
from jax.sharding import PartitionSpec as P

D = 512
HEADS = 8
HD = 64
FF = 2048
VOCAB = 256
BAND = 30
LEN = 640
LAYERS = 2
CH = 128
CHUNKS = LEN // CH
REACH = 32
TILE = 512
BACK = 256
F32 = jnp.float32
BF16 = jnp.bfloat16


def mm(left, right):
    return jnp.dot(left, right, preferred_element_type=F32)


def mm_nt(left, right):
    return lax.dot_general(left, right, (((1,), (1,)), ((), ())), preferred_element_type=F32)


def norm_forward(v, gain):
    scale = lax.rsqrt(jnp.mean(v * v, axis=-1, keepdims=True) + 1e-05)
    return v * scale * gain


def norm_backward(v, gain, dy):
    scale = lax.rsqrt(jnp.mean(v * v, axis=-1, keepdims=True) + 1e-05)
    normed = v * scale
    dgain = jnp.sum(dy * normed, axis=0, keepdims=True)
    dyg = dy * gain
    dv = scale * (dyg - normed * jnp.mean(dyg * normed, axis=-1, keepdims=True))
    return dv, dgain


def gelu_parts(u):
    c = 0.7978845608028654
    square = u * u
    t = jnp.tanh(u * (c + (c * 0.044715) * square))
    half = 0.5 * (1.0 + t)
    value = u * half
    slope = half + 0.5 * u * (1.0 - t * t) * (c + (3.0 * c * 0.044715) * square)
    return value, slope


def feature_parts(u):
    low_exp = jnp.exp(jnp.minimum(u, 0.0))
    first = jnp.where(u > 0.0, u + 1.0, low_exp)
    second = jnp.tanh(u)
    return first, low_exp, second


def iotas(rows, cols, row0=0):
    r = lax.broadcasted_iota(jnp.int32, (rows, cols), 0) + row0
    c = lax.broadcasted_iota(jnp.int32, (rows, cols), 1)
    return r, c


def near_part(i, key_rows, query_cols):
    row0 = -REACH if i > 0 else 0
    scores = mm(key_rows, query_cols) * 0.125
    r, c = iotas(CH - row0, CH, row0)
    ok = (r <= c) & (c - r < BAND)
    scores = jnp.where(ok, scores, -1e30)
    peak = jnp.max(scores, axis=0, keepdims=True)
    weights = jnp.exp(scores - peak)
    return weights / jnp.sum(weights, axis=0, keepdims=True)


def causal_rows(i, block):
    row0 = -REACH if i > 0 else 0
    r, c = iotas(CH - row0, CH, row0)
    return jnp.where(r <= c, block, 0.0)


def mixture_chunk(i, key_nat, key_feat2, query_masked, query_feat2):
    t0, t1 = i * CH, (i + 1) * CH
    r0 = t0 - REACH if i > 0 else 0
    far = mm(key_feat2[:t1], query_feat2[:, t0:t1])
    near = near_part(i, key_nat[r0:t1], query_masked[:, t0:t1])
    bottom = (causal_rows(i, far[r0:]) + near).astype(BF16)
    if r0 == 0:
        return bottom, near
    return jnp.concatenate([far[:r0].astype(BF16), bottom], axis=0), near


def query_features(qT, inv1, inv2):
    first, slope1, second = feature_parts(qT.astype(F32))
    first_b, second_b = first.astype(BF16), second.astype(BF16)
    scaled = jnp.concatenate([first_b.astype(F32) * inv1, second_b.astype(F32) * inv2], axis=0)
    high = scaled.astype(BF16)
    rest = (scaled - high.astype(F32)).astype(BF16)
    return first_b, slope1, second, jnp.concatenate([high, rest], axis=0)


def masked_pair(part, e):
    zero = jnp.zeros_like(part)
    return jnp.concatenate([part, zero] if e == 0 else [zero, part], axis=0)


class Links:
    def __init__(self, pieces, send_sem, recv_sem):
        self.pieces, self.send_sem, self.recv_sem = pieces, send_sem, recv_sem
        d, z = lax.axis_index("dp"), lax.axis_index("section")
        core, x, y = d % 2, (d // 2) % 2, d // 4
        self.d, self.half = d, z % 2
        self.core_n, self.x_n, self.y_n, self.z_n = d + 1 - 2 * core, d + 2 - 4 * x, d + 4 - 8 * y, z + 1 - 2 * (z % 2)
        self.diag = self.x_n + 4 - 8 * y

    def columns(self, n, part):
        _, _, cols, cut, shared = self.pieces[n]
        if part == "all" or (part == "mine" and not shared):
            return slice(None)
        if not shared:
            return slice(0, cut) if part == "a" else slice(cut, cols)
        half, quarter = cols // 2, cols // 4
        start = half * (1 - self.half if part == "other" else self.half) + (quarter if part == "b" else 0)
        return pl.ds(pl.multiple_of(start, quarter), quarter if part in "ab" else half)

    def copy(self, n, kind):
        ref, rows = self.pieces[n][:2]
        core, x, y, z = {"dp": self.core_n}, {"dp": self.x_n}, {"dp": self.y_n}, {"section": self.z_n}
        block, part, target = (
            (self.d, "mine", x),
            (self.d, "mine", y),
            (self.y_n, "a", x),
            (self.x_n, "b", y),
            (self.d, "all", core),
            (self.x_n, "mine", core),
            (self.y_n, "mine", core),
            (self.diag, "a", core),
            (self.diag, "b", core),
            (self.x_n, "mine", z),
            (self.y_n, "mine", z),
            (self.diag, "mine", z),
            (self.x_n, "other", core),
            (self.y_n, "other", core),
            (self.diag, "other", core),
        )[kind]
        view = ref.at[pl.ds(pl.multiple_of(block * rows, rows), rows), self.columns(n, part)]
        return pltpu.make_async_remote_copy(
            src_ref=view, dst_ref=view, send_sem=self.send_sem.at[n, kind], recv_sem=self.recv_sem.at[n, kind],
            device_id=target, device_id_type=pl.DeviceIdType.MESH,
        )

    def own(self, *ns):
        for n in ns:
            for kind in (0, 1, 4):
                self.copy(n, kind).start()

    def first(self, *ns):
        for n in ns:
            shared = self.pieces[n][4]
            self.copy(n, 0).wait_recv()
            self.copy(n, 3).start()
            self.copy(n, 1).wait_recv()
            self.copy(n, 2).start()
            for kind in (9, 10, 5, 6) if shared else (5, 6):
                self.copy(n, kind).start()

    def second(self, *ns):
        for n in ns:
            shared = self.pieces[n][4]
            self.copy(n, 2).wait_recv()
            self.copy(n, 7).start()
            self.copy(n, 3).wait_recv()
            for kind in (11, 8) if shared else (8,):
                self.copy(n, kind).start()

    def third(self, *ns):
        for n in ns:
            for kind in (9, 10, 11):
                self.copy(n, kind).wait_recv()
                self.copy(n, kind + 3).start()

    def ready(self, *ns):
        for n in ns:
            for kind in (4, 5, 6, 7, 8) + ((12, 13, 14) if self.pieces[n][4] else ()):
                self.copy(n, kind).wait_recv()

    def finish(self):
        for n, piece in enumerate(self.pieces):
            for kind in range(15 if piece[4] else 9):
                self.copy(n, kind).wait_send()


class Sums:
    def __init__(self, links, pieces, send_sem, recv_sem, tile_send, tile_recv):
        self.links, self.pieces, self.send_sem, self.recv_sem = links, pieces, send_sem, recv_sem
        self.tile_send, self.tile_recv = tile_send, tile_recv
        d = links.d
        self.core, self.x, self.y = d % 2, (d // 2) % 2, d // 4
        self.z = lax.axis_index("section")
        self.inner = (self.z == 1) | (self.z == 2)
        self.outer = (self.z == 0) | (self.z == 3)

    def view(self, piece, ref, block, count, half=None):
        blocks = pl.ds(pl.multiple_of(block * piece.size, piece.size), count * piece.size)
        across = {None: slice(None), 0: slice(0, piece.split), 1: slice(piece.split, piece.across)}[half]
        return ref.at[across, blocks] if piece.by_columns else ref.at[blocks, across]

    def tile_copy(self, block):
        r = self.pieces["r0"]
        src = r.whole.at[:, pl.ds(pl.multiple_of((4 * (1 - self.core) + block) * r.size, r.size), r.size)]
        dst = r.whole_r1.at[:, pl.ds(pl.multiple_of(block * r.size, r.size), r.size)]
        return pltpu.make_async_remote_copy(
            src_ref=src, dst_ref=dst, send_sem=self.tile_send.at[block], recv_sem=self.tile_recv.at[block],
            device_id={"dp": self.links.core_n}, device_id_type=pl.DeviceIdType.MESH,
        )

    def copy(self, name, kind, l=None):
        piece = self.pieces[name]
        core, x, y, z, links = self.core, self.x, self.y, self.z, self.links
        mine = 4 * core

        def pair(block, to, at, count, half):
            return self.view(piece, piece.grad, block, count, half), self.view(piece, to, at, count, half)

        if kind == 0:
            src, dst = pair(4 * (1 - core), piece.r1, 0, 4, None)
        elif kind in (1, 2):
            src, dst = pair(mine + 2 * (kind - 1) + 1 - x, piece.r2, kind - 1, 1, 0)
        elif kind == 3:
            src, dst = pair(mine + 2 * (1 - y), piece.r2, 0, 2, 1)
        elif kind == 4:
            src, dst = pair(mine + 2 * (1 - y) + x, piece.r3, 0, 1, 0)
        elif kind == 5:
            src, dst = pair(mine + 2 * y + 1 - x, piece.r3, 0, 1, 1)
        else:
            src = piece.r3
            dst = piece.rz.at[kind - 6] if kind < 8 else piece.out(l)
        device = (
            {"dp": links.core_n}, {"dp": links.x_n}, {"dp": links.x_n}, {"dp": links.y_n}, {"dp": links.y_n}, {"dp": links.x_n},
            {"section": z + 1 - 2 * (z // 3)}, {"section": 3 - z}, {"section": 3 * (z // 2)},
        )[kind]
        return pltpu.make_async_remote_copy(
            src_ref=src, dst_ref=dst, send_sem=self.send_sem.at[piece.index, kind], recv_sem=self.recv_sem.at[piece.index, kind],
            device_id=device, device_id_type=pl.DeviceIdType.MESH,
        )

    def add(self, into, other):
        into[...] = (into[...].astype(F32) + other[...].astype(F32)).astype(BF16)

    def step(self, name, number, l):
        piece = self.pieces[name]
        grad, r1, r2, r3, rz = piece.grad, piece.r1, piece.r2, piece.r3, piece.rz
        mine = 4 * self.core
        own = mine + 2 * self.y + self.x
        tiles = name[0] == "r"
        if number == 1:
            self.copy(name, 0).start()
        elif number == 2:
            if not tiles:
                self.copy(name, 0).wait_recv()
            elif name == "r0":
                for block in range(4):
                    self.tile_copy(block).wait_recv()
            self.add(self.view(piece, grad, mine, 4), self.view(piece, r1, 0, 4))
            for kind in (1, 2, 3):
                self.copy(name, kind).start()
        elif number == 3:
            for kind in (1, 2):
                self.copy(name, kind).wait_recv()
                self.add(self.view(piece, grad, mine + 2 * (kind - 1) + self.x, 1, 0), self.view(piece, r2, kind - 1, 1, 0))
            self.copy(name, 3).wait_recv()
            self.copy(name, 4).start()
            self.add(self.view(piece, grad, mine + 2 * self.y, 2, 1), self.view(piece, r2, 0, 2, 1))
            self.copy(name, 5).start()
        elif number == 4:
            for half in (0, 1):
                self.copy(name, 4 + half).wait_recv()
                self.add(self.view(piece, r3, 0, 1, half), self.view(piece, grad, own, 1, half))

            @pl.when(self.outer)
            def _():
                self.copy(name, 6).start()

            if not tiles:
                self.copy(name, 0).wait_send()
            elif name == "r0":
                for block in range(4):
                    self.tile_copy(block).wait_send()
            for kind in range(1, 6):
                self.copy(name, kind).wait_send()
        elif number == 5:

            @pl.when(self.inner)
            def _():
                self.copy(name, 6).wait_recv()
                self.add(r3, rz.at[0])
                self.copy(name, 7).start()
        elif number == 6:

            @pl.when(self.inner)
            def _():
                self.copy(name, 7).wait()
                self.add(r3, rz.at[1])
                self.copy(name, 8, l).start()
                self.local(piece, l).start()
        elif number == 7:

            @pl.when(self.outer)
            def _():
                self.copy(name, 6).wait_send()
                self.copy(name, 8, l).wait_recv()

            @pl.when(self.inner)
            def _():
                self.copy(name, 8, l).wait_send()
                self.local(piece, l).wait()

    def local(self, piece, l):
        return pltpu.make_async_copy(piece.r3, piece.out(l), self.send_sem.at[piece.index, 9])


class Piece:
    def __init__(self, index, refs, size, across, split, out, by_columns=False, whole=None):
        self.index, self.size, self.across, self.split, self.out, self.by_columns = index, size, across, split, out, by_columns
        self.grad, self.r1, self.r2, self.r3, self.rz = refs
        self.whole, self.whole_r1 = whole or (None, None)


def sum_pieces(refs, out_m, out_o, out_e, out_r, out_t):
    names = ("grad_", "r1", "r2", "r3")

    def part(n, index, rz=True):
        views = [refs[name + n].at[index] for name in names]
        return views + [refs["rz" + n].at[(slice(None),) + index]]

    every = slice(None)
    pieces = {}
    for i in range(2):
        cols = slice(FF // 2 * i, FF // 2 * (i + 1))
        pieces["e%d" % i] = Piece(i, part("e", (every, cols)), 64, FF // 2, FF // 4, lambda l, cols=cols: out_e.at[l, :, cols])
    for i in range(2):
        rows = slice(D // 2 * i, D // 2 * (i + 1))
        pieces["r%d" % i] = Piece(
            2 + i, part("r", (rows, every)), 256, D // 2, D // 4, lambda l, rows=rows: out_r.at[l, rows], True,
            (refs["grad_r"], refs["r1r"]),
        )
    for i in range(4):
        cols = slice(384 * i, 384 * (i + 1))
        pieces["m%d" % i] = Piece(
            4 + i, part("m", (every, cols)), 64, 384, 128 * (1 + i % 2), lambda l, i=i: out_m.at[l, i]
        )
    pieces["o"] = Piece(8, part("o", (every, every)), 64, D, D // 2, lambda l: out_o.at[l])
    pieces["t"] = Piece(9, part("t", (every, every)), 64, 384, 128, lambda l: out_t)
    return pieces


def by_position(rows):
    size = rows.shape[0] // 8
    return jnp.concatenate([rows[size * i:size * (i + 1)] for i in (0, 2, 4, 6, 1, 3, 5, 7)], axis=0)


def step_kernel(linked, *refs):
    names = (LINKED_IN + LINKED_OUT) if linked else (PLAIN_IN + PLAIN_OUT)
    names += tuple(SCRATCH) + tuple(LINKED_SCRATCH if linked else PLAIN_SCRATCH)
    step_body(linked, **dict(zip(names, refs, strict=True)))


def step_body(
    linked, columns, loss, lg, x, x1, dx, kv, pT, kf, inv1s, cum, oT, hT, g, gT, wide, a1k, m, d, ds, doT, dpT, yb, acc,
    table=None, gm=None, gf=None, gz=None, wm=None, wo=None, we=None, wr=None, stage=None, stage_half=None, sem=None, sem_half=None,
    dtable=None, dgm=None, dgf=None, dgz=None, dwm=None, dwo=None, dwe=None, dwrt=None,
    small=None, wm_s=None, wo_s=None, we_s=None, wr_s=None, tz=None, gains=None, lgs=None, losss=None,
    send_sem=None, recv_sem=None, zsend=None, zrecv=None, load_sem=None, sum_send=None, sum_recv=None, tile_send=None, tile_recv=None,
    out_m=None, out_o=None, out_e=None, out_r=None, out_t=None, dgains=None, **sums_refs,
):
    table_ref = table
    gm_ref, gf_ref, gz_ref = gm, gf, gz
    wm_ref, wo_ref, we_ref, wr_ref = wm, wo, we, wr
    loss_ref, lg_ref, dtable_ref, dgm_ref, dgf_ref, dgz_ref = loss, lg, dtable, dgm, dgf, dgz
    dwm_ref, dwo_ref, dwe_ref, dwrt_ref = dwm, dwo, dwe, dwrt
    x_ref, x1_ref, dx_ref, kv_ref, pT_ref, kf_ref, inv1_ref, cum_ref = x, x1, dx, kv, pT, kf, inv1s, cum
    oT_ref, hT_ref, g_ref, gT_ref, wide_ref, a1k_ref, m_ref, d_ref, ds_ref = oT, hT, g, gT, wide, a1k, m, d, ds
    doT_ref, dpT_ref, w_ref, yb_ref, acc_ref = doT, dpT, a1k, yb, acc
    xs = [x_ref.at[0], x_ref.at[1], dx_ref]
    placed = by_position if linked else (lambda rows: rows)
    r, c = iotas(LEN, LEN)
    upper = (r <= c).astype(F32).astype(BF16)

    if linked:
        zi = lax.axis_index("section")
        links = Links(
            [(table_ref, 64, 384, 256, False)]
            + [
                entry
                for l in range(LAYERS)
                for entry in (
                    (wm_ref.at[l], 64, 3 * D, 3 * D // 2, SHARED[l][0]),
                    (wo_ref.at[l], 64, D, D // 2, SHARED[l][1]),
                    (we_ref.at[l], 64, FF, FF // 2, SHARED[l][2]),
                    (wr_ref.at[l], 256, D, D // 2, SHARED[l][3]),
                )
            ],
            send_sem, recv_sem,
        )

        def along_z(n, k, src_of, dst):
            target = (zi + k) % 4
            return pltpu.make_async_remote_copy(
                src_ref=src_of(target), dst_ref=dst.at[zi], send_sem=zsend.at[n, k - 1], recv_sem=zrecv.at[n, k - 1],
                device_id={"section": target}, device_id_type=pl.DeviceIdType.MESH,
            )

        def table_copy(k):
            return along_z(0, k, lambda target: tz.at[zi], tz)

        def lg_copy(k):
            return along_z(1, k, lambda target: lgs.at[target], lg_ref)

        def loss_copy(k):
            return along_z(2, k, lambda target: losss, loss_ref)

        loads = []
        for l in range(LAYERS):
            pairs = [(wm_s.at[l, :, TILE * j:TILE * (j + 1)], x1_ref.at[l, 64 * j:64 * (j + 1)]) for j in range(3)]
            pairs += [(wo_s.at[l], x1_ref.at[l, 192:256])]
            pairs += [(we_s.at[l, :, TILE * j:TILE * (j + 1)], x1_ref.at[l, 256 + 64 * j:320 + 64 * j]) for j in range(4)]
            pairs += [(wr_s.at[l], x_ref.at[1, 256 * l:256 * (l + 1)])]
            loads.append([pltpu.make_async_copy(src, dst, load_sem.at[l, i]) for i, (src, dst) in enumerate(pairs)])
            for load in loads[l]:
                load.start()

        def take(l, part):
            for i in {"m": (0, 1, 2), "o": (3,), "e": (4, 5, 6, 7), "r": (8,)}[part]:
                loads[l][i].wait()
            if part == "m":
                for j in range(3):
                    wm_ref[l, own64, TILE * j:TILE * (j + 1)] = x1_ref[l, 64 * j:64 * (j + 1)].astype(BF16)
            elif part == "o":
                wo_ref[l, own64] = x1_ref[l, 192:256].astype(BF16)
            elif part == "e":
                for j in range(4):
                    we_ref[l, own64, TILE * j:TILE * (j + 1)] = x1_ref[l, 256 + 64 * j:320 + 64 * j].astype(BF16)
            else:
                wr_ref[l, own256] = x_ref[1, 256 * l:256 * (l + 1)].astype(BF16)

        barrier = pltpu.get_barrier_semaphore()
        for target in (links.core_n, links.x_n, links.y_n):
            pl.semaphore_signal(barrier, inc=1, device_id={"dp": target}, device_id_type=pl.DeviceIdType.MESH)
        for k in (1, 2, 3):
            pl.semaphore_signal(barrier, inc=1, device_id={"section": (zi + k) % 4}, device_id_type=pl.DeviceIdType.MESH)
        pl.semaphore_wait(barrier, 6)

        own64 = pl.ds(pl.multiple_of(links.d * 64, 64), 64)
        own256 = pl.ds(pl.multiple_of(links.d * 256, 256), 256)
        small_b = small[...].astype(BF16)
        tz[zi] = small_b
        for k in (1, 2, 3):
            table_copy(k).start()
        take(0, "m")
        links.own(1)
        take(0, "o")
        for k in (1, 2, 3):
            table_copy(k).wait_recv()
        pad = jnp.zeros((64, 64), BF16)
        table_ref[own64, :] = jnp.concatenate([tz[i][:, :64] for i in range(4)] + [small_b[:, 64:], pad], axis=1)
        links.own(0, 2)
        take(0, "e")
        wide_ref[...] = upper
        links.first(1, 0)
        links.own(3)
        links.first(2)
        take(0, "r")
        links.own(4)
        for part in "moer":
            take(1, part)
        links.second(1, 0)
        links.ready(0)
        gains[...] = table_ref[:, 256:].astype(F32).T[:8]
        table_ref = table_ref.at[:, :256]
        gm_ref, gf_ref, gz_ref = [gains[i:i + 1] for i in range(2)], [gains[i:i + 1] for i in range(2, 4)], gains[4:5]
        sums = Sums(
            links, sum_pieces(sums_refs, out_m, out_o, out_e, out_r, out_t), sum_send, sum_recv, tile_send, tile_recv
        )
    else:
        wide_ref[...] = upper
        gm_ref, gf_ref, gz_ref = [gm_ref[i] for i in range(2)], [gf_ref[i] for i in range(2)], gz_ref[...]

    def service(step, index=None, only=lambda at: True):
        if not linked:
            return
        for at, acts in SERVICE.get(step, {}).items():
            if not only(at):
                continue

            def run(acts=acts):
                for act in acts:
                    if isinstance(act, str):
                        name, number, layer = act.split(".")
                        sums.step(name, int(number), int(layer))
                    else:
                        getattr(links, act[0])(*act[1:])

            if at is None:
                run()
            else:
                pl.when(index == at)(run)

    inv2 = 1.0 / (lax.broadcasted_iota(jnp.int32, (1, LEN), 1).astype(F32) + 1.0)

    def emit(slot, wait_first, value, dst):
        into, sems = (stage, sem) if dst.shape[1] == TILE else (stage_half, sem_half)

        def copy():
            return pltpu.make_async_copy(into.at[slot], dst, sems.at[slot])

        if wait_first is True:
            copy().wait()
        elif wait_first is not False:
            pl.when(wait_first)(lambda: copy().wait())
        into[slot] = value.astype(BF16)
        copy().start()

    def put_gain(row, value):
        if linked:
            dgains[row:row + 1] = value
        elif row < 2:
            dgm_ref[row] = value
        elif row < 4:
            dgf_ref[row - 2] = value
        else:
            dgz_ref[...] = value

    def by_rows(run, init=None):
        def some(i, carry):
            return run(pl.ds(pl.multiple_of(i * CH, CH), CH), carry)

        return lax.fori_loop(0, CHUNKS, some, init)

    def normed_rows(src, gain, dst, dstT):
        def some(rows, carry):
            block = norm_forward(src[rows], gain).astype(BF16)
            dst[rows] = block
            dstT[:, rows] = placed(block.T)
            return carry

        by_rows(some, 0)

    def back_rows(src, gain, row):
        def some(rows, dgain):
            dv, dg = norm_backward(src[rows], gain, acc_ref[rows])
            dx_ref[rows] += dv
            return dgain + dg

        put_gain(row, by_rows(some, jnp.zeros((1, D), F32)))

    vocab_ids = lax.broadcasted_iota(jnp.int32, (LEN, VOCAB), 1)
    hot = (vocab_ids == columns[:, 0:1]).astype(F32).astype(BF16)
    x_ref[0] = mm_nt(hot, table_ref[...])
    if linked:
        links.ready(1)

    def attention_forward(l):
        normed_rows(x_ref.at[l], gm_ref[l], yb_ref, hT_ref.at[l])
        h = yb_ref[...]
        for j in range(3):
            part = mm(h, wm_ref[l, :, j * TILE:(j + 1) * TILE]).astype(BF16)
            if j > 0:
                kv_ref[l, :, (j - 1) * TILE:j * TILE] = part
            pT_ref[l, j * TILE:(j + 1) * TILE, :] = part.T
        service(("mixer", l))
        kT = pT_ref[l, D:2 * D, :].astype(F32)
        a1k_ref[...] = feature_parts(kT)[0].astype(BF16)
        for i in range(CHUNKS):
            t0, t1 = i * CH, (i + 1) * CH
            cum_ref[l, :, t0:t1] = mm(a1k_ref[:, :t1], wide_ref[:t1, t0:t1])

        def pair(p, carry):
            base = pl.multiple_of(p * CH, CH)
            for e in range(2):
                row = pl.multiple_of(base + e * HD, HD)
                qT = pT_ref[l, pl.ds(row, HD), :]
                kT = pT_ref[l, pl.ds(pl.multiple_of(D + row, HD), HD), :]
                vT = pT_ref[l, pl.ds(pl.multiple_of(2 * D + row, HD), HD), :]
                first_k, _, second_k = feature_parts(kT.astype(F32))
                key_feat = jnp.concatenate([first_k.astype(BF16), second_k.astype(BF16)], axis=0).T
                kf_ref[l, :, pl.ds(pl.multiple_of(2 * row, CH), CH)] = key_feat
                first_q = feature_parts(qT.astype(F32))[0].astype(BF16).astype(F32)
                total = jnp.sum(first_q * cum_ref[l, pl.ds(row, HD), :], axis=0, keepdims=True)
                inv1 = 1.0 / (total + 1.0)
                inv1_ref[l, 2 * p + e] = inv1
                query_feat2 = query_features(qT, inv1, inv2)[3]
                key_feat2 = jnp.concatenate([key_feat, key_feat], axis=1)
                key_nat = kv_ref[l, :, pl.ds(base, CH)]
                query_masked = masked_pair(qT, e)
                for i in range(CHUNKS):
                    t0, t1 = i * CH, (i + 1) * CH
                    mixture, _ = mixture_chunk(i, key_nat, key_feat2, query_masked, query_feat2)
                    oT_ref[l, pl.ds(row, HD), t0:t1] = mm(vT[:, :t1], mixture).astype(BF16)
                service(("head", l), 2 * p + e, lambda at: at % 2 == e)
            return carry

        lax.fori_loop(0, HEADS // 2, pair, 0)
        service(("output", l))
        o = oT_ref[l].T
        x1_ref[l] = x_ref[l] + mm(o, wo_ref[l])

    def feed_forward(l):
        normed_rows(x1_ref.at[l], gf_ref[l], g_ref, gT_ref.at[l])
        xs[l + 1][...] = x1_ref[l]
        service(("feed", l))

        def tile(j, carry):
            col = pl.multiple_of(j * BACK, BACK)
            active = gelu_parts(mm(g_ref[...], we_ref[l, :, pl.ds(col, BACK)]))[0].astype(BF16)
            service(("gelu", l), j)
            xs[l + 1][...] += mm(active, wr_ref[l, pl.ds(col, BACK), :])
            service(("tile", l), j)
            return carry

        lax.fori_loop(0, FF // BACK, tile, 0)

    def head():
        zT_ref, grad_ref = doT_ref, yb_ref.at[:, :VOCAB]

        def some(rows, carry):
            dgain, cross_sum, val_sum = carry
            x = dx_ref[rows]
            z = norm_forward(x, gz_ref).astype(BF16)
            zT_ref[:, rows] = placed(z.T)
            logits = mm(z, table_ref[...])
            ids = lax.broadcasted_iota(jnp.int32, (CH, VOCAB), 1)
            tgt_hot = (ids == columns[rows, 1:2]).astype(F32)
            val = columns[rows, 2:3].astype(F32)
            peak = jnp.max(logits, axis=-1, keepdims=True)
            grown = jnp.exp(logits - peak)
            total = jnp.sum(grown, axis=-1, keepdims=True)
            lse = peak + jnp.log(total)
            picked = jnp.sum(logits * tgt_hot, axis=-1, keepdims=True)
            cross = (lse - picked) * val
            grad_b = ((grown / total - tgt_hot) * val).astype(BF16)
            grad_ref[rows, :] = grad_b
            if linked:
                for i in range(4):
                    lgs[i, rows, :] = grad_b[:, 64 * i:64 * i + 64]
            else:
                lg_ref[rows, :] = grad_b
            dv, dg = norm_backward(x, gz_ref, mm_nt(grad_b, table_ref[...]))
            dx_ref[rows] = dv
            return (
                dgain + dg,
                cross_sum + jnp.sum(cross, axis=0, keepdims=True),
                val_sum + jnp.sum(val, axis=0, keepdims=True),
            )

        nothing = jnp.zeros((1, 1), F32)
        dgain, cross_sum, val_sum = by_rows(some, (jnp.zeros((1, D), F32), nothing, nothing))
        put_gain(4, dgain)
        loss = jnp.broadcast_to(cross_sum / val_sum, (8, 128))
        if linked:
            losss[...] = loss
            for k in (1, 2, 3):
                lg_copy(k).start()
                loss_copy(k).start()
            pltpu.make_async_copy(lgs.at[zi], lg_ref.at[zi], zsend.at[1, 3]).start()
            pltpu.make_async_copy(losss, loss_ref.at[zi], zsend.at[2, 3]).start()
        else:
            loss_ref[...] = loss
        dtable_ref[...] = mm(zT_ref[...], grad_ref[...])

    def feed_backward(l):
        def some(rows, carry):
            yb = dx_ref[rows].astype(BF16)
            yb_ref[rows] = yb
            doT_ref[:, rows] = yb.T
            if l < LAYERS - 1:
                g_ref[rows] = norm_forward(x1_ref[l, rows], gf_ref[l]).astype(BF16)
            return carry

        by_rows(some, 0)
        acc_ref[...] = jnp.zeros_like(acc_ref)

        def tile(j, carry):
            col = pl.multiple_of(j * BACK, BACK)
            slot = lax.rem(j, 2)
            later = (j >= 2) if l == LAYERS - 1 else True
            value, slope = gelu_parts(mm(g_ref[...], we_ref[l, :, pl.ds(col, BACK)]))
            dreduce = mm(doT_ref[...], value.astype(BF16))
            if linked:
                place = pl.multiple_of(BACK * (lax.rem(j, 2) * 4 + lax.div(j, 2)), BACK)
                sums_refs["grad_r"][:, pl.ds(place, BACK)] = dreduce.astype(BF16)
                pl.when(lax.rem(j, 2) != sums.core)(lambda: sums.tile_copy(lax.div(j, 2)).start())
            else:
                emit(slot, later, dreduce, dwrt_ref.at[l, :, pl.ds(col, BACK)])
            dact = mm_nt(yb_ref[...], wr_ref[l, pl.ds(col, BACK), :])
            dhid = (dact * slope).astype(BF16)
            dexpand = mm(gT_ref[l], dhid)
            if linked:
                sums_refs["grad_e"][:, pl.ds(col, BACK)] = dexpand.astype(BF16)
            else:
                emit(2 + slot, later, dexpand, dwe_ref.at[l, :, pl.ds(col, BACK)])
            dnormed = mm_nt(dhid, we_ref[l, :, pl.ds(col, BACK)])

            acc_ref[...] += dnormed
            service(("back tile", l), j)
            return carry

        lax.fori_loop(0, FF // BACK, tile, 0)
        service(("back feed", l))
        back_rows(x1_ref.at[l], gf_ref[l], 2 + l)

    def attention_backward(l):
        yb_ref[...] = dx_ref[...].astype(BF16)
        yb = yb_ref[...]
        doutput = mm(placed(oT_ref[l]), yb)
        if linked:
            sums_refs["grad_o"][...] = doutput.astype(BF16)
        else:
            emit(0, l < LAYERS - 1, doutput, dwo_ref.at[l])
        service(("back output", l))
        doT_ref[...] = mm_nt(yb, wo_ref[l]).astype(BF16).T

        def pair(p, carry):
            base = pl.multiple_of(p * CH, CH)
            for e in range(2):
                row = pl.multiple_of(base + e * HD, HD)
                qT = pT_ref[l, pl.ds(row, HD), :]
                kT = pT_ref[l, pl.ds(pl.multiple_of(D + row, HD), HD), :]
                doT = doT_ref[pl.ds(row, HD), :]
                inv1 = inv1_ref[l, 2 * p + e]
                first_q, slope1_q, second_q, query_feat2 = query_features(qT, inv1, inv2)
                first_k, slope1_k, second_k = feature_parts(kT.astype(F32))
                key_featT = jnp.concatenate([first_k.astype(BF16), second_k.astype(BF16)], axis=0)
                key_feat = kf_ref[l, :, pl.ds(pl.multiple_of(2 * row, CH), CH)]
                key_feat2 = jnp.concatenate([key_feat, key_feat], axis=1)
                key_nat = kv_ref[l, :, pl.ds(base, CH)]
                value_nat = kv_ref[l, :, pl.ds(pl.multiple_of(D + base, CH), CH)]
                query_masked = masked_pair(qT, e)
                do_masked = masked_pair(doT, e)
                far_q, near_q = [], []
                for i in range(CHUNKS):
                    t0, t1 = i * CH, (i + 1) * CH
                    r0 = t0 - REACH if i > 0 else 0
                    mixture, near = mixture_chunk(i, key_nat, key_feat2, query_masked, query_feat2)
                    m_ref[:t1, t0:t1] = mixture
                    dm = mm(value_nat[:t1], do_masked[:, t0:t1])
                    bottom = dm[r0:]
                    dm_b = causal_rows(i, bottom).astype(BF16)
                    if r0 > 0:
                        dm_b = jnp.concatenate([dm[:r0].astype(BF16), dm_b], axis=0)
                    d_ref[:t1, t0:t1] = dm_b
                    weighted = near * bottom
                    dsum = jnp.sum(weighted, axis=0, keepdims=True)
                    ds = ((weighted - near * dsum) * 0.125).astype(BF16)
                    far_q.append(mm(key_featT[:, :t1], dm_b))
                    if i > 0:
                        before = jnp.concatenate([jnp.zeros((CH - REACH, CH), BF16), ds[:REACH]], axis=0)
                        ds_ref[t0 - CH:t0, CH:] = before
                        ds = ds[REACH:]
                        near_q.append(mm(kT[:, t0 - CH:t1], jnp.concatenate([before, ds], axis=0)))
                    else:
                        near_q.append(mm(kT[:, t0:t1], ds))
                    ds_ref[t0:t1, :CH] = ds
                farT = jnp.concatenate(far_q, axis=1)
                y1, y2 = farT[:HD], farT[HD:]
                first_qf = first_q.astype(F32)
                m = inv1 * jnp.sum(first_qf * y1, axis=0, keepdims=True)
                cum = cum_ref[l, pl.ds(row, HD), :]
                dq = jnp.concatenate(near_q, axis=1)
                dq = dq + (inv1 * (y1 - m * cum)) * slope1_q + (inv2 * y2) * (1.0 - second_q * second_q)
                dpT_ref[pl.ds(row, HD), :] = dq.astype(BF16)
                w_ref[pl.ds(row, HD), :] = (first_qf * (m * inv1)).astype(BF16)
                for i in range(CHUNKS):
                    t0, t1 = i * CH, (i + 1) * CH
                    far = mm_nt(query_feat2[:, t0:], d_ref[t0:t1, t0:])
                    back = mm_nt(w_ref[pl.ds(row, HD), t0:], wide_ref[t0:t1, t0:])
                    far = far[:CH] + far[CH:]
                    t2 = min(t1 + CH, LEN)
                    near = mm_nt(qT[:, t0:t2], ds_ref[t0:t1, :t2 - t0])
                    dk = near + (far[:HD] - back) * slope1_k[:, t0:t1]
                    dk = dk + far[HD:] * (1.0 - second_k[:, t0:t1] * second_k[:, t0:t1])
                    dpT_ref[pl.ds(pl.multiple_of(D + row, HD), HD), t0:t1] = dk.astype(BF16)
                    dv = mm_nt(doT[:, t0:], m_ref[t0:t1, t0:])
                    dpT_ref[pl.ds(pl.multiple_of(2 * D + row, HD), HD), t0:t1] = dv.astype(BF16)
                service(("back head", l), 2 * p + e, lambda at: at % 2 == e)
            if linked:
                for j in range(3):
                    block = mm_nt(hT_ref[l], dpT_ref[pl.ds(pl.multiple_of(j * D + base, CH), CH), :])
                    place = pl.multiple_of(3 * base + j * CH, CH)
                    sums_refs["grad_m"][:, pl.ds(place, CH)] = block.astype(BF16)
                service(("back pair", l), p)
            return carry

        lax.fori_loop(0, HEADS // 2, pair, 0)
        if not linked:
            for j in range(3):
                block = mm_nt(hT_ref[l], dpT_ref[j * TILE:(j + 1) * TILE, :])
                emit(1 + j, l < LAYERS - 1, block, dwm_ref.at[l, :, j * TILE:(j + 1) * TILE])
        for t0 in range(0, LEN, 256):
            t1 = min(t0 + 256, LEN)
            acc_ref[t0:t1] = mm(wm_ref[l], dpT_ref[:, t0:t1]).T
        service(("back mixer", l))
        back_rows(x_ref.at[l], gm_ref[l], l)
        service(("back layer", l))

    for l in range(LAYERS):
        service(("layer", l))
        attention_forward(l)
        feed_forward(l)
    head()
    for l in reversed(range(LAYERS)):
        feed_backward(l)
        attention_backward(l)
    dtable_sum = dtable_ref[...] + mm(placed(dx_ref[...].astype(BF16).T), hot)
    if linked:
        sums_refs["grad_t"][:, :VOCAB] = dtable_sum.astype(BF16)
        sums_refs["grad_t"][:, VOCAB:] = placed(jnp.concatenate([dgains[...], jnp.zeros((120, D), F32)], axis=0).T).astype(BF16)
        service(("end", 0))
        for k in (1, 2, 3):
            table_copy(k).wait_send()
            lg_copy(k).wait()
            loss_copy(k).wait()
        pltpu.make_async_copy(lgs.at[zi], lg_ref.at[zi], zsend.at[1, 3]).wait()
        pltpu.make_async_copy(losss, loss_ref.at[zi], zsend.at[2, 3]).wait()
        links.finish()
    else:
        dtable_ref[...] = dtable_sum
        for slot in range(4):
            pltpu.make_async_copy(stage.at[slot], dwo_ref.at[0], sem.at[slot]).wait()
            pltpu.make_async_copy(stage_half.at[slot], dwe_ref.at[0, :, :BACK], sem_half.at[slot]).wait()


SHARED = ((False, False, True, False), (False, False, True, False))
SERVICE = {
    ("mixer", 0): {None: (("first", 3),)},
    ("head", 0): {
        2: (("second", 3), ("own", 5), ("second", 2)),
        4: (("first", 4), ("ready", 2)),
        7: (("third", 3), ("first", 5), ("own", 6, 7)),
    },
    ("feed", 0): {None: (("ready", 3),)},
    ("gelu", 0): {0: (("second", 4), ("ready", 4))},
    ("tile", 0): {1: (("own", 8),), 3: (("first", 6),), 5: (("second", 5),), 7: (("first", 7),)},
    ("layer", 1): {None: (("ready", 5),)},
    ("mixer", 1): {None: (("second", 6),)},
    ("head", 1): {0: (("first", 8), ("second", 7)), 2: (("ready", 6),), 4: (("third", 7), ("second", 8))},
    ("feed", 1): {None: (("ready", 7),)},
    ("gelu", 1): {0: (("ready", 8),)},
    ("back tile", 1): {3: ("e0.1.1",)},
    ("back feed", 1): {None: ("e1.1.1",)},
    ("back output", 1): {None: ("o.1.1", "e0.2.1")},
    ("back head", 1): {
        0: ("r0.2.1",),
        1: ("r1.2.1", "e1.2.1"),
        2: ("e0.3.1",),
        3: ("r0.3.1", "o.2.1"),
        4: ("r1.3.1", "m0.2.1"),
        5: ("e1.3.1", "e0.4.1"),
        6: ("r0.4.1", "o.3.1"),
        7: ("r1.4.1", "e1.4.1", "m1.2.1", "m0.3.1"),
    },
    ("back pair", 1): {0: ("m0.1.1",), 1: ("m1.1.1",), 2: ("m2.1.1",), 3: ("m3.1.1",)},
    ("back mixer", 1): {None: ("m2.2.1",)},
    ("back layer", 1): {None: ("o.4.1", "m0.4.1", "e0.5.1")},
    ("back tile", 0): {
        0: ("m1.3.1", "r0.5.1"),
        1: ("m3.2.1", "r1.5.1"),
        2: ("m2.3.1", "e1.5.1"),
        3: ("e0.1.0", "o.5.1", "m0.5.1"),
        4: ("m1.4.1", "m3.3.1", "e0.6.1"),
        5: ("m2.4.1", "r0.6.1"),
        6: ("m3.4.1", "r1.6.1", "m1.5.1"),
        7: ("e1.6.1", "o.6.1", "m0.6.1"),
    },
    ("back feed", 0): {None: ("e1.1.0", "m2.5.1", "m3.5.1")},
    ("back output", 0): {None: ("o.1.0", "m1.6.1", "e0.7.1", "e0.2.0")},
    ("back head", 0): {
        0: ("r0.7.1", "r0.2.0", "m2.6.1"),
        1: ("r1.7.1", "r1.2.0", "e1.7.1", "e1.2.0", "m3.6.1", "o.7.1", "m0.7.1"),
        2: ("e0.3.0", "m1.7.1"),
        3: ("r0.3.0", "o.2.0", "m2.7.1"),
        4: ("r1.3.0", "m0.2.0", "m3.7.1"),
        5: ("e1.3.0", "e0.4.0"),
        6: ("r0.4.0", "o.3.0"),
        7: ("r1.4.0", "e1.4.0", "m1.2.0", "m0.3.0", "e0.5.0"),
    },
    ("back pair", 0): {0: ("m0.1.0",), 1: ("m1.1.0",), 2: ("m2.1.0",), 3: ("m3.1.0",)},
    ("back mixer", 0): {None: ("m2.2.0",)},
    ("back layer", 0): {None: ("o.4.0", "m0.4.0", "m1.3.0", "r0.5.0")},
    ("end", 0): {
        None: (
            "t.1.0", "m3.2.0", "m2.3.0", "r1.5.0", "e1.5.0", "t.2.0", "m1.4.0", "m0.5.0", "o.5.0", "m3.3.0", "m2.4.0", "e0.6.0",
            "t.3.0", "r0.6.0", "m1.5.0", "m3.4.0", "r1.6.0", "e1.6.0", "m2.5.0", "t.4.0", "m0.6.0", "o.6.0", "m3.5.0", "m1.6.0",
            "t.5.0", "m2.6.0", "m3.6.0", "t.6.0",
        )
        + tuple(n + ".7.0" for n in ("e0", "r0", "r1", "e1", "m0", "o", "m1", "m2", "m3", "t")),
    },
}
PLAIN_IN = ("columns", "table", "gm", "gf", "gz", "wm", "wo", "we", "wr")
PLAIN_OUT = ("loss", "lg", "dtable", "dgm", "dgf", "dgz", "dwm", "dwo", "dwe", "dwrt")
LINKED_IN = ("columns", "small", "wm_s", "wo_s", "we_s", "wr_s")
LINKED_OUT = ("loss", "lg", "out_m", "out_o", "out_e", "out_r", "out_t")
SCRATCH = dict(
    x=pltpu.VMEM((LAYERS, LEN, D), F32),
    x1=pltpu.VMEM((LAYERS, LEN, D), F32),
    dx=pltpu.VMEM((LEN, D), F32),
    kv=pltpu.VMEM((LAYERS, LEN, 2 * D), BF16),
    pT=pltpu.VMEM((LAYERS, 3 * D, LEN), BF16),
    kf=pltpu.VMEM((LAYERS, LEN, 2 * D), BF16),
    inv1s=pltpu.VMEM((LAYERS, HEADS, 1, LEN), F32),
    cum=pltpu.VMEM((LAYERS, D, LEN), F32),
    oT=pltpu.VMEM((LAYERS, D, LEN), BF16),
    hT=pltpu.VMEM((LAYERS, D, LEN), BF16),
    g=pltpu.VMEM((LEN, D), BF16),
    gT=pltpu.VMEM((LAYERS, D, LEN), BF16),
    wide=pltpu.VMEM((LEN, LEN), BF16),
    a1k=pltpu.VMEM((D, LEN), BF16),
    m=pltpu.VMEM((LEN, LEN), BF16),
    d=pltpu.VMEM((LEN, LEN), BF16),
    ds=pltpu.VMEM((LEN, 2 * CH), BF16),
    doT=pltpu.VMEM((D, LEN), BF16),
    dpT=pltpu.VMEM((3 * D, LEN), BF16),
    yb=pltpu.VMEM((LEN, D), BF16),
    acc=pltpu.VMEM((LEN, D), F32),
)
PLAIN_SCRATCH = dict(
    stage=pltpu.VMEM((4, D, TILE), BF16),
    stage_half=pltpu.VMEM((4, D, BACK), BF16),
    sem=pltpu.SemaphoreType.DMA((4,)),
    sem_half=pltpu.SemaphoreType.DMA((4,)),
)


def sum_buffers(n, rows, cols, along):
    def shape(blocks):
        return (rows * blocks // 8, cols) if along == 0 else (rows, cols * blocks // 8)

    return {
        "grad_" + n: pltpu.VMEM((rows, cols), BF16),
        "r1" + n: pltpu.VMEM(shape(4), BF16),
        "r2" + n: pltpu.VMEM(shape(2), BF16),
        "r3" + n: pltpu.VMEM(shape(1), BF16),
        "rz" + n: pltpu.VMEM((2,) + shape(1), BF16),
    }


LINKED_SCRATCH = dict(
    table=pltpu.VMEM((D, 384), BF16),
    wm=pltpu.VMEM((LAYERS, D, 3 * D), BF16),
    wo=pltpu.VMEM((LAYERS, D, D), BF16),
    we=pltpu.VMEM((LAYERS, D, FF), BF16),
    wr=pltpu.VMEM((LAYERS, FF, D), BF16),
    tz=pltpu.VMEM((4, 64, 128), BF16),
    gains=pltpu.VMEM((8, D), F32),
    lgs=pltpu.VMEM((4, LEN, 64), BF16),
    losss=pltpu.VMEM((8, 128), F32),
    send_sem=pltpu.SemaphoreType.DMA((9, 15)),
    recv_sem=pltpu.SemaphoreType.DMA((9, 15)),
    zsend=pltpu.SemaphoreType.DMA((3, 4)),
    zrecv=pltpu.SemaphoreType.DMA((3, 4)),
    load_sem=pltpu.SemaphoreType.DMA((LAYERS, 9)),
    sum_send=pltpu.SemaphoreType.DMA((10, 10)),
    sum_recv=pltpu.SemaphoreType.DMA((10, 9)),
    tile_send=pltpu.SemaphoreType.DMA((4,)),
    tile_recv=pltpu.SemaphoreType.DMA((4,)),
    dtable=pltpu.VMEM((D, VOCAB), F32),
    dgains=pltpu.VMEM((8, D), F32),
    **sum_buffers("m", D, 3 * D, 0),
    **sum_buffers("o", D, D, 0),
    **sum_buffers("e", D, FF, 0),
    **sum_buffers("r", D, FF, 1),
    **sum_buffers("t", D, 384, 0),
)


def local_step(linked, *operands):
    vmem = pl.BlockSpec(memory_space=pltpu.VMEM)
    hbm = pl.BlockSpec(memory_space=pl.ANY)
    shape = jax.ShapeDtypeStruct
    if linked:
        scratch = dict(SCRATCH, **LINKED_SCRATCH)
        in_specs = [vmem] * 2 + [hbm] * 4
        out_shape = (
            shape((4, 8, 128), F32),
            shape((4, LEN, 64), BF16),
            shape((LAYERS, 4, 64, 384), BF16),
            shape((LAYERS, 64, D), BF16),
            shape((LAYERS, 64, FF), BF16),
            shape((LAYERS, D, 256), BF16),
            shape((64, 384), BF16),
        )
        out_specs = (hbm,) * 7
    else:
        scratch = dict(SCRATCH, **PLAIN_SCRATCH)
        in_specs = [vmem] * len(operands)
        out_shape = (
            shape((8, 128), F32),
            shape((LEN, VOCAB), BF16),
            shape((D, VOCAB), F32),
            shape((LAYERS, 1, D), F32),
            shape((LAYERS, 1, D), F32),
            shape((1, D), F32),
            shape((LAYERS, D, 3 * D), BF16),
            shape((LAYERS, D, D), BF16),
            shape((LAYERS, D, FF), BF16),
            shape((LAYERS, D, FF), BF16),
        )
        out_specs = (vmem,) * 6 + (hbm,) * 4
    return pl.pallas_call(
        functools.partial(step_kernel, linked),
        out_shape=out_shape,
        in_specs=in_specs,
        out_specs=out_specs,
        scratch_shapes=list(scratch.values()),
        compiler_params=pltpu.CompilerParams(
            vmem_limit_bytes=64 * 1024 * 1024,
            collective_id=0 if linked else None,
            has_side_effects=linked,
        ),
        cost_estimate=pl.CostEstimate(flops=40_000_000_000, bytes_accessed=40_000_000, transcendentals=0),
        name="local_step",
    )(*operands)


def body(
    tokens,
    padding_mask,
    embedding,
    mixer_weight,
    output_weight,
    mixer_gain,
    expand_weight,
    reduce_weight,
    feed_gain,
    final_gain,
):
    segments = lax.axis_size("section")
    segment_index = lax.axis_index("section")
    item_count = tokens.shape[0]
    assert item_count == segments
    slice_width = embedding.shape[1]

    token_row = lax.dynamic_index_in_dim(tokens, segment_index, 0, keepdims=False)
    mask_row = lax.dynamic_index_in_dim(padding_mask, segment_index, 0, keepdims=False)
    zero = jnp.zeros((1,), jnp.int32)
    columns = jnp.stack(
        [token_row, jnp.concatenate([token_row[1:], zero]), jnp.concatenate([mask_row[1:], zero])], axis=1
    )
    if segments == 4 and lax.axis_size("dp") == 8:
        small = jnp.concatenate(
            [embedding, mixer_gain.T, feed_gain.T, final_gain[:, None], jnp.zeros((embedding.shape[0], 59), F32)], axis=1
        )
        loss, lg, dwm, dwo, dwe, dwrt, last = local_step(
            True, columns, small, mixer_weight, output_weight, expand_weight, reduce_weight
        )
        dwm = dwm.reshape(LAYERS, 4, 64, 3, CH).transpose(0, 2, 3, 1, 4).reshape(LAYERS, 64, 3 * D)
        table_grad = lax.dynamic_slice_in_dim(last[:, :VOCAB], segment_index * slice_width, slice_width, 1)
        gain_grads = last[:, VOCAB:VOCAB + 5].astype(F32).T
        return (
            loss[:, 0, 0],
            lg.astype(F32),
            table_grad.astype(F32),
            dwm.astype(F32),
            dwo.astype(F32),
            gain_grads[0:2],
            dwe.astype(F32),
            jnp.swapaxes(dwrt, 1, 2).astype(F32),
            gain_grads[2:4],
            gain_grads[4],
        )

    def gather(block, dim):
        return lax.all_gather(block.astype(BF16), "dp", axis=dim, tiled=True)

    table = lax.all_gather(gather(embedding, 0), "section", axis=1, tiled=True)
    gains = gather(jnp.concatenate([mixer_gain, feed_gain, final_gain[None]], axis=0), 1).astype(F32)
    loss, lg, dtable, dgm, dgf, dgz, dwm, dwo, dwe, dwrt = local_step(
        False, columns, table, gains[0:2, None], gains[2:4, None], gains[4:5],
        gather(mixer_weight, 1), gather(output_weight, 1), gather(expand_weight, 1), gather(reduce_weight, 1),
    )
    item_loss = lax.all_gather(loss[0, 0], "section")
    parts = lg.reshape(LEN, segments, slice_width).transpose(1, 0, 2)
    logit_grad = lax.all_to_all(parts, "section", 0, 0, tiled=True).astype(F32)

    def shard(grad, dim):
        part = lax.psum_scatter(grad.astype(BF16), "dp", scatter_dimension=dim, tiled=True)
        return lax.psum(part, "section").astype(F32)

    table_part = lax.psum_scatter(dtable.astype(BF16), "dp", scatter_dimension=0, tiled=True)
    table_grad = lax.psum_scatter(table_part, "section", scatter_dimension=1, tiled=True).astype(F32)
    gain_grads = lax.psum_scatter(
        jnp.concatenate([dgm[:, 0], dgf[:, 0], dgz], axis=0), "dp", scatter_dimension=1, tiled=True
    )
    gain_grads = lax.psum(gain_grads, "section")
    return (
        item_loss,
        logit_grad,
        table_grad,
        shard(dwm, 1),
        shard(dwo, 1),
        gain_grads[0:2],
        shard(dwe, 1),
        jnp.swapaxes(shard(dwrt, 2), 1, 2),
        gain_grads[2:4],
        gain_grads[4],
    )


def solution(mesh):
    placed = (
        P("dp", None),
        P("dp", None),
        P("dp", "section"),
        P(None, "dp", None),
        P(None, "dp", None),
        P(None, "dp"),
        P(None, "dp", None),
        P(None, "dp", None),
        P(None, "dp"),
        P("dp"),
    )
    return jax.shard_map(
        body,
        mesh=mesh,
        in_specs=placed,
        out_specs=(
            P("dp"),
            P("dp", None, "section"),
            P("dp", "section"),
            P(None, "dp", None),
            P(None, "dp", None),
            P(None, "dp"),
            P(None, "dp", None),
            P(None, "dp", None),
            P(None, "dp"),
            P("dp"),
        ),
        check_vma=False,
    )
```

```python
import functools

import jax
import jax.numpy as jnp
from jax import lax
from jax.experimental import pallas as pl
from jax.experimental.pallas import tpu as pltpu
from jax.sharding import PartitionSpec as P

D = 512
HEADS = 8
HD = 64
FF = 2048
VOCAB = 256
BAND = 30
LEN = 640
LAYERS = 2
CH = 128
CHUNKS = LEN // CH
REACH = 32
WIDE = tuple((t0, min(t0 + 256, LEN)) for t0 in range(0, LEN, 256))
TILE = 512
BACK = 256
F32 = jnp.float32
DP, SECTION = ("dp", "section")
BF16 = jnp.bfloat16


def mm(left, right):
    return jnp.dot(left, right, preferred_element_type=F32)


def mm_nt(left, right):
    return lax.dot_general(left, right, (((1,), (1,)), ((), ())), preferred_element_type=F32)


def norm_forward(v, gain):
    scale = lax.rsqrt(jnp.mean(v * v, axis=-1, keepdims=True) + 1e-05)
    return v * scale * gain


def norm_backward(v, gain, dy):
    scale = lax.rsqrt(jnp.mean(v * v, axis=-1, keepdims=True) + 1e-05)
    normed = v * scale
    dgain = jnp.sum(dy * normed, axis=0, keepdims=True)
    dyg = dy * gain
    dv = scale * (dyg - normed * jnp.mean(dyg * normed, axis=-1, keepdims=True))
    return dv, dgain


def gelu_parts(u):
    c = 0.7978845608028654
    square = u * u
    t = jnp.tanh(u * (c + (c * 0.044715) * square))
    half = 0.5 * (1.0 + t)
    value = u * half
    slope = half + 0.5 * u * (1.0 - t * t) * (c + (3.0 * c * 0.044715) * square)
    return value, slope


def feature_parts(u):
    low_exp = jnp.exp(jnp.minimum(u, 0.0))
    first = jnp.where(u > 0.0, u + 1.0, low_exp)
    second = jnp.tanh(u)
    return first, low_exp, second


def iotas(rows, cols, row0=0):
    r = lax.broadcasted_iota(jnp.int32, (rows, cols), 0) + row0
    c = lax.broadcasted_iota(jnp.int32, (rows, cols), 1)
    return r, c


def near_part(i, key_rows, query_cols):
    row0 = -REACH if i > 0 else 0
    scores = mm(key_rows, query_cols) * 0.125
    r, c = iotas(CH - row0, CH, row0)
    ok = (r <= c) & (c - r < BAND)
    scores = jnp.where(ok, scores, -1e30)
    peak = jnp.max(scores, axis=0, keepdims=True)
    weights = jnp.exp(scores - peak)
    return weights / jnp.sum(weights, axis=0, keepdims=True)


def causal_rows(i, block):
    row0 = -REACH if i > 0 else 0
    r, c = iotas(CH - row0, CH, row0)
    return jnp.where(r <= c, block, 0.0)


START, WAIT = range(2)


def every(copies, act):
    for copy in copies:
        if act == START:
            copy.start()
        else:
            copy.wait()


def halves(t0, t1, half):
    parts = []
    for i in range(t0 // CH, t1 // CH):
        part = half(i)
        if part.shape[0] < t1:
            part = jnp.concatenate([part, jnp.zeros((t1 - part.shape[0], CH), part.dtype)], axis=0)
        parts.append(part)
    return parts[0] if len(parts) == 1 else jnp.concatenate(parts, axis=1)


def first_row(i):
    return i * CH - REACH if i > 0 else 0


def mixture_block(t0, t1, key_nat, key_feat2, query_masked, query_feat2, near_ref):
    far = mm(key_feat2[:t1], query_feat2[:, t0:t1])

    def half(i):
        r0, end = first_row(i), (i + 1) * CH
        near = near_part(i, key_nat[r0:end], query_masked[:, i * CH:end])
        near_ref[i, :end - r0, :] = near
        column = far[:end, i * CH - t0:end - t0]
        bottom = (causal_rows(i, column[r0:]) + near).astype(BF16)
        if r0 == 0:
            return bottom
        return jnp.concatenate([column[:r0].astype(BF16), bottom], axis=0)

    return halves(t0, t1, half)


def query_features(qT, inv1, inv2):
    first, slope1, second = feature_parts(qT.astype(F32))
    first_b, second_b = first.astype(BF16), second.astype(BF16)
    scaled = jnp.concatenate([first_b.astype(F32) * inv1, second_b.astype(F32) * inv2], axis=0)
    high = scaled.astype(BF16)
    rest = (scaled - high.astype(F32)).astype(BF16)
    return first_b, slope1, second, jnp.concatenate([high, rest], axis=0)


def masked_pair(part, e):
    zero = jnp.zeros_like(part)
    return jnp.concatenate([part, zero] if e == 0 else [zero, part], axis=0)


ALL, MINE, MINE_A, MINE_B, OTHER = range(5)


class Links:
    def __init__(self, pieces, send_sem, recv_sem):
        self.pieces, self.send_sem, self.recv_sem = pieces, send_sem, recv_sem
        d, z = lax.axis_index(DP), lax.axis_index(SECTION)
        core, x, y = d % 2, (d // 2) % 2, d // 4
        self.d, self.half = d, z % 2
        self.core_n, self.x_n, self.y_n, self.z_n = d + 1 - 2 * core, d + 2 - 4 * x, d + 4 - 8 * y, z + 1 - 2 * (z % 2)
        self.diag = self.x_n + 4 - 8 * y

    def columns(self, n, part):
        _, _, cols, cut, shared = self.pieces[n]
        if part == ALL or (part == MINE and not shared):
            return slice(None)
        if not shared:
            return slice(0, cut) if part == MINE_A else slice(cut, cols)
        half, quarter = cols // 2, cols // 4
        start = half * (1 - self.half if part == OTHER else self.half) + (quarter if part == MINE_B else 0)
        return pl.ds(pl.multiple_of(start, quarter), quarter if part in (MINE_A, MINE_B) else half)

    def copy(self, n, kind):
        ref, rows = self.pieces[n][:2]
        core, x, y, z = {DP: self.core_n}, {DP: self.x_n}, {DP: self.y_n}, {SECTION: self.z_n}
        block, part, target = (
            (self.d, MINE, x),
            (self.d, MINE, y),
            (self.y_n, MINE_A, x),
            (self.x_n, MINE_B, y),
            (self.d, ALL, core),
            (self.x_n, MINE, core),
            (self.y_n, MINE, core),
            (self.diag, MINE_A, core),
            (self.diag, MINE_B, core),
            (self.x_n, MINE, z),
            (self.y_n, MINE, z),
            (self.diag, MINE, z),
            (self.x_n, OTHER, core),
            (self.y_n, OTHER, core),
            (self.diag, OTHER, core),
        )[kind]
        view = ref.at[pl.ds(pl.multiple_of(block * rows, rows), rows), self.columns(n, part)]
        return pltpu.make_async_remote_copy(
            src_ref=view, dst_ref=view, send_sem=self.send_sem.at[n, kind], recv_sem=self.recv_sem.at[n, kind],
            device_id=target, device_id_type=pl.DeviceIdType.MESH,
        )

    def own(self, *ns):
        for n in ns:
            for kind in (0, 1, 4):
                self.copy(n, kind).start()

    def first(self, *ns):
        for n in ns:
            shared = self.pieces[n][4]
            self.copy(n, 0).wait_recv()
            self.copy(n, 3).start()
            self.copy(n, 1).wait_recv()
            self.copy(n, 2).start()
            for kind in (9, 10, 5, 6) if shared else (5, 6):
                self.copy(n, kind).start()

    def second(self, *ns):
        for n in ns:
            shared = self.pieces[n][4]
            self.copy(n, 2).wait_recv()
            self.copy(n, 7).start()
            self.copy(n, 3).wait_recv()
            for kind in (11, 8) if shared else (8,):
                self.copy(n, kind).start()

    def third(self, *ns):
        for n in ns:
            for kind in (9, 10, 11):
                self.copy(n, kind).wait_recv()
                self.copy(n, kind + 3).start()

    def ready(self, *ns):
        for n in ns:
            for kind in (4, 5, 6, 7, 8) + ((12, 13, 14) if self.pieces[n][4] else ()):
                self.copy(n, kind).wait_recv()

    def finish(self):
        for n, piece in enumerate(self.pieces):
            for kind in range(15 if piece[4] else 9):
                self.copy(n, kind).wait_send()


class Sums:
    def __init__(self, links, pieces, send_sem, recv_sem, tile_send, tile_recv):
        self.links, self.pieces, self.send_sem, self.recv_sem = links, pieces, send_sem, recv_sem
        self.tile_send, self.tile_recv = tile_send, tile_recv
        d = links.d
        self.core, self.x, self.y = d % 2, (d // 2) % 2, d // 4
        self.z = lax.axis_index(SECTION)
        self.inner = (self.z == 1) | (self.z == 2)
        self.outer = (self.z == 0) | (self.z == 3)

    def view(self, piece, ref, block, count, half=None):
        blocks = pl.ds(pl.multiple_of(block * piece.size, piece.size), count * piece.size)
        across = {None: slice(None), 0: slice(0, piece.split), 1: slice(piece.split, piece.across)}[half]
        return ref.at[across, blocks] if piece.by_columns else ref.at[blocks, across]

    def tile_copy(self, block):
        r = self.pieces[R0]
        src = r.whole.at[:, pl.ds(pl.multiple_of((4 * (1 - self.core) + block) * r.size, r.size), r.size)]
        dst = r.whole_r1.at[:, pl.ds(pl.multiple_of(block * r.size, r.size), r.size)]
        return pltpu.make_async_remote_copy(
            src_ref=src, dst_ref=dst, send_sem=self.tile_send.at[block], recv_sem=self.tile_recv.at[block],
            device_id={DP: self.links.core_n}, device_id_type=pl.DeviceIdType.MESH,
        )

    def copy(self, name, kind, l=None):
        piece = self.pieces[name]
        core, x, y, z, links = self.core, self.x, self.y, self.z, self.links
        mine = 4 * core

        def pair(block, to, at, count, half):
            return self.view(piece, piece.grad, block, count, half), self.view(piece, to, at, count, half)

        if kind == 0:
            src, dst = pair(4 * (1 - core), piece.r1, 0, 4, None)
        elif kind in (1, 2):
            src, dst = pair(mine + 2 * (kind - 1) + 1 - x, piece.r2, kind - 1, 1, 0)
        elif kind == 3:
            src, dst = pair(mine + 2 * (1 - y), piece.r2, 0, 2, 1)
        elif kind == 4:
            src, dst = pair(mine + 2 * (1 - y) + x, piece.r3, 0, 1, 0)
        elif kind == 5:
            src, dst = pair(mine + 2 * y + 1 - x, piece.r3, 0, 1, 1)
        else:
            src = piece.r3
            dst = piece.rz.at[kind - 6] if kind < 8 else piece.out(l)
        device = (
            {DP: links.core_n}, {DP: links.x_n}, {DP: links.x_n}, {DP: links.y_n}, {DP: links.y_n}, {DP: links.x_n},
            {SECTION: z + 1 - 2 * (z // 3)}, {SECTION: 3 - z}, {SECTION: 3 * (z // 2)},
        )[kind]
        return pltpu.make_async_remote_copy(
            src_ref=src, dst_ref=dst, send_sem=self.send_sem.at[piece.index, kind], recv_sem=self.recv_sem.at[piece.index, kind],
            device_id=device, device_id_type=pl.DeviceIdType.MESH,
        )

    def add(self, into, other):
        into[...] = (into[...].astype(F32) + other[...].astype(F32)).astype(BF16)

    def step(self, name, number, l):
        piece = self.pieces[name]
        grad, r1, r2, r3, rz = piece.grad, piece.r1, piece.r2, piece.r3, piece.rz
        mine = 4 * self.core
        own = mine + 2 * self.y + self.x
        tiles = name in (R0, R1)
        if number == 1:
            self.copy(name, 0).start()
        elif number == 2:
            if not tiles:
                self.copy(name, 0).wait_recv()
            elif name == R0:
                for block in range(4):
                    self.tile_copy(block).wait_recv()
            self.add(self.view(piece, grad, mine, 4), self.view(piece, r1, 0, 4))
            for kind in (1, 2, 3):
                self.copy(name, kind).start()
        elif number == 3:
            for kind in (1, 2):
                self.copy(name, kind).wait_recv()
                self.add(self.view(piece, grad, mine + 2 * (kind - 1) + self.x, 1, 0), self.view(piece, r2, kind - 1, 1, 0))
            self.copy(name, 3).wait_recv()
            self.copy(name, 4).start()
            self.add(self.view(piece, grad, mine + 2 * self.y, 2, 1), self.view(piece, r2, 0, 2, 1))
            self.copy(name, 5).start()
        elif number == 4:
            for half in (0, 1):
                self.copy(name, 4 + half).wait_recv()
                self.add(self.view(piece, r3, 0, 1, half), self.view(piece, grad, own, 1, half))

            @pl.when(self.outer)
            def _():
                self.copy(name, 6).start()

            if not tiles:
                self.copy(name, 0).wait_send()
            elif name == R0:
                for block in range(4):
                    self.tile_copy(block).wait_send()
            for kind in range(1, 6):
                self.copy(name, kind).wait_send()
        elif number == 5:

            @pl.when(self.inner)
            def _():
                self.copy(name, 6).wait_recv()
                self.add(r3, rz.at[0])
                self.copy(name, 7).start()
        elif number == 6:

            @pl.when(self.inner)
            def _():
                self.copy(name, 7).wait()
                self.add(r3, rz.at[1])
                self.copy(name, 8, l).start()
                self.local(piece, l).start()
        elif number == 7:

            @pl.when(self.outer)
            def _():
                self.copy(name, 6).wait_send()
                self.copy(name, 8, l).wait_recv()

            @pl.when(self.inner)
            def _():
                self.copy(name, 8, l).wait_send()
                self.local(piece, l).wait()

    def local(self, piece, l):
        return pltpu.make_async_copy(piece.r3, piece.out(l), self.send_sem.at[piece.index, 9])


class Piece:
    def __init__(self, index, refs, size, across, split, out, by_columns=False, whole=None):
        self.index, self.size, self.across, self.split, self.out, self.by_columns = index, size, across, split, out, by_columns
        self.grad, self.r1, self.r2, self.r3, self.rz = refs
        self.whole, self.whole_r1 = whole or (None, None)


def sum_pieces(refs, out_m, out_o, out_e, out_r, out_t):
    def part(n, index):
        return [refs[name + n].at[index] for name in ("grad_", "r1", "r2", "r3")] + [refs["rz" + n].at[(slice(None),) + index]]

    every = slice(None)
    pieces = {}
    for i in range(2):
        cols = slice(FF // 2 * i, FF // 2 * (i + 1))
        pieces[E0 + i] = Piece(E0 + i, part("e", (every, cols)), 64, FF // 2, FF // 4, lambda l, cols=cols: out_e.at[l, :, cols])
    for i in range(2):
        rows = slice(D // 2 * i, D // 2 * (i + 1))
        pieces[R0 + i] = Piece(
            R0 + i, part("r", (rows, every)), 256, D // 2, D // 4, lambda l, rows=rows: out_r.at[l, rows], True,
            (refs["grad_r"], refs["r1r"]),
        )
    for i in range(4):
        cols = slice(384 * i, 384 * (i + 1))
        pieces[M0 + i] = Piece(
            M0 + i, part("m", (every, cols)), 64, 384, 128 * (1 + i % 2), lambda l, i=i: out_m.at[l, i]
        )
    pieces[O] = Piece(O, part("o", (every, every)), 64, D, D // 2, lambda l: out_o.at[l])
    pieces[T] = Piece(T, part("t", (every, every)), 64, 384, 128, lambda l: out_t)
    return pieces


def by_position(rows):
    size = rows.shape[0] // 8
    return jnp.concatenate([rows[size * i:size * (i + 1)] for i in (0, 2, 4, 6, 1, 3, 5, 7)], axis=0)


def step_kernel(linked, *refs):
    names = (LINKED_IN + LINKED_OUT) if linked else (PLAIN_IN + PLAIN_OUT)
    names += tuple(SCRATCH) + tuple(LINKED_SCRATCH if linked else PLAIN_SCRATCH)
    step_body(linked, **dict(zip(names, refs, strict=True)))


def step_body(
    linked, loss, lg, kept_m, kept_near, x, x1, dx, kv, pT, inv1s, cum, oT, hT, g, gT, wide, a1k, m, near, keep_sem, d, ds, doT, dpT, yb, acc,
    columns=None, table=None, gm=None, gf=None, gz=None, wm=None, wo=None, we=None, wr=None, stage=None, stage_half=None, sem=None, sem_half=None,
    dtable=None, dgm=None, dgf=None, dgz=None, dwm=None, dwo=None, dwe=None, dwrt=None,
    tokens=None, mask=None, emb=None, mgain=None, fgain=None, zgain=None, wm_s=None, wo_s=None, we_s=None, wr_s=None, tz=None, gains=None, lgs=None, losss=None,
    send_sem=None, recv_sem=None, zsend=None, zrecv=None, load_sem=None, sum_send=None, sum_recv=None, tile_send=None, tile_recv=None,
    out_m=None, out_o=None, out_e=None, out_r=None, out_t=None, dgains=None, **sums_refs,
):
    table_ref = table
    gm_ref, gf_ref, gz_ref = gm, gf, gz
    wm_ref, wo_ref, we_ref, wr_ref = wm, wo, we, wr
    loss_ref, lg_ref, dtable_ref, dgm_ref, dgf_ref, dgz_ref = loss, lg, dtable, dgm, dgf, dgz
    dwm_ref, dwo_ref, dwe_ref, dwrt_ref = dwm, dwo, dwe, dwrt
    x_ref, x1_ref, dx_ref, kv_ref, pT_ref, inv1_ref, cum_ref = x, x1, dx, kv, pT, inv1s, cum
    oT_ref, hT_ref, g_ref, gT_ref, wide_ref, a1k_ref, near_ref, m_ref, d_ref, ds_ref = oT, hT, g, gT, wide, a1k, near, m, d, ds
    doT_ref, dpT_ref, w_ref, yb_ref, acc_ref = doT, dpT, a1k, yb, acc
    xs = [x_ref.at[0], x_ref.at[1], dx_ref]
    placed = by_position if linked else (lambda rows: rows)
    r, c = iotas(LEN, LEN)
    upper = (r <= c).astype(F32).astype(BF16)

    if linked:
        zi = lax.axis_index(SECTION)
        links = Links(
            [(table_ref, 64, 384, 256, False)]
            + [
                entry
                for l in range(LAYERS)
                for entry in (
                    (wm_ref.at[l], 64, 3 * D, 3 * D // 2, SHARED[l][0]),
                    (wo_ref.at[l], 64, D, D // 2, SHARED[l][1]),
                    (we_ref.at[l], 64, FF, FF // 2, SHARED[l][2]),
                    (wr_ref.at[l], 256, D, D // 2, SHARED[l][3]),
                )
            ],
            send_sem, recv_sem,
        )

        def along_z(n, k, src_of, dst):
            target = (zi + k) % 4
            return pltpu.make_async_remote_copy(
                src_ref=src_of(target), dst_ref=dst.at[zi], send_sem=zsend.at[n, k - 1], recv_sem=zrecv.at[n, k - 1],
                device_id={SECTION: target}, device_id_type=pl.DeviceIdType.MESH,
            )

        def table_copy(k):
            return along_z(0, k, lambda target: tz.at[zi], tz)

        def lg_copy(k):
            return along_z(1, k, lambda target: lgs.at[target], lg_ref)

        def loss_copy(k):
            return along_z(2, k, lambda target: losss, loss_ref)

        loads = []
        for l in range(LAYERS):
            pairs = [(wm_s.at[l, :, TILE * j:TILE * (j + 1)], x1_ref.at[l, 64 * j:64 * (j + 1)]) for j in range(3)]
            pairs += [(wo_s.at[l], x1_ref.at[l, 192:256])]
            pairs += [(we_s.at[l, :, TILE * j:TILE * (j + 1)], x1_ref.at[l, 256 + 64 * j:320 + 64 * j]) for j in range(4)]
            pairs += [(wr_s.at[l], x_ref.at[1, 256 * l:256 * (l + 1)])]
            loads.append([pltpu.make_async_copy(src, dst, load_sem.at[l, i]) for i, (src, dst) in enumerate(pairs)])
            for load in loads[l]:
                load.start()

        def take(l, part):
            for i in {"m": (0, 1, 2), "o": (3,), "e": (4, 5, 6, 7), "r": (8,)}[part]:
                loads[l][i].wait()
            if part == "m":
                for j in range(3):
                    wm_ref[l, own64, TILE * j:TILE * (j + 1)] = x1_ref[l, 64 * j:64 * (j + 1)].astype(BF16)
            elif part == "o":
                wo_ref[l, own64] = x1_ref[l, 192:256].astype(BF16)
            elif part == "e":
                for j in range(4):
                    we_ref[l, own64, TILE * j:TILE * (j + 1)] = x1_ref[l, 256 + 64 * j:320 + 64 * j].astype(BF16)
            else:
                wr_ref[l, own256] = x_ref[1, 256 * l:256 * (l + 1)].astype(BF16)

        barrier = pltpu.get_barrier_semaphore()
        for target in (links.core_n, links.x_n, links.y_n):
            pl.semaphore_signal(barrier, inc=1, device_id={DP: target}, device_id_type=pl.DeviceIdType.MESH)
        for k in (1, 2, 3):
            pl.semaphore_signal(barrier, inc=1, device_id={SECTION: (zi + k) % 4}, device_id_type=pl.DeviceIdType.MESH)
        pl.semaphore_wait(barrier, 6)

        own64 = pl.ds(pl.multiple_of(links.d * 64, 64), 64)
        own256 = pl.ds(pl.multiple_of(links.d * 256, 256), 256)
        r, _ = iotas(8, 64)
        rows = [mgain[0:1], mgain[1:2], fgain[0:1], fgain[1:2], zgain[0:1]]
        gathered = sum(jnp.where(r == i, row, 0.0) for i, row in enumerate(rows))
        gathered = jnp.concatenate([gathered, jnp.zeros((8, 64), F32)], axis=1)
        gathered = jnp.concatenate([gathered, jnp.zeros((120, 128), F32)], axis=0).T[:64]
        small_b = (jnp.concatenate([emb[...], jnp.zeros((64, 64), F32)], axis=1) + pltpu.roll(gathered, 64, 1)).astype(BF16)
        tz[zi] = small_b
        for k in (1, 2, 3):
            table_copy(k).start()
        take(0, "m")
        links.own(1)
        r, c = iotas(8, LEN)
        ids = tokens[pl.ds(zi, 1), :].astype(F32)
        scored = mask[pl.ds(zi, 1), :].astype(F32)
        rows = [ids, pltpu.roll(ids, LEN - 1, 1), pltpu.roll(scored, LEN - 1, 1)]
        rows = sum(jnp.where((r == i) & ((c < LEN - 1) | (r == 0)), row, 0.0) for i, row in enumerate(rows))
        columns[...] = rows.T.astype(jnp.int32)
        take(0, "o")
        for k in (1, 2, 3):
            table_copy(k).wait_recv()
        pad = jnp.zeros((64, 64), BF16)
        table_ref[own64, :] = jnp.concatenate([tz[i][:, :64] for i in range(4)] + [small_b[:, 64:], pad], axis=1)
        links.own(0, 2)
        take(0, "e")
        wide_ref[...] = upper
        links.first(1, 0)
        links.own(3)
        links.first(2)
        take(0, "r")
        links.own(4)
        for part in "moer":
            take(1, part)
        links.second(1, 0)
        links.ready(0)
        gains[...] = table_ref[:, 256:].astype(F32).T[:8]
        table_ref = table_ref.at[:, :256]
        gm_ref, gf_ref, gz_ref = [gains[i:i + 1] for i in range(2)], [gains[i:i + 1] for i in range(2, 4)], gains[4:5]
        sums = Sums(
            links, sum_pieces(sums_refs, out_m, out_o, out_e, out_r, out_t), sum_send, sum_recv, tile_send, tile_recv
        )
    else:
        wide_ref[...] = upper
        gm_ref, gf_ref, gz_ref = [gm_ref[i] for i in range(2)], [gf_ref[i] for i in range(2)], gz_ref[...]

    def service(step, index=None, only=lambda at: True):
        if not linked:
            return
        for at, acts in SERVICE.get(step, {}).items():
            if not only(at):
                continue

            def run(acts=acts):
                for act in acts:
                    if isinstance(act[0], int):
                        sums.step(*act)
                    else:
                        act[0](links, *act[1:])

            if at is None:
                run()
            else:
                pl.when(index == at)(run)

    inv2 = 1.0 / (lax.broadcasted_iota(jnp.int32, (1, LEN), 1).astype(F32) + 1.0)

    def emit(slot, wait_first, value, dst):
        into, sems = (stage, sem) if dst.shape[1] == TILE else (stage_half, sem_half)

        def copy():
            return pltpu.make_async_copy(into.at[slot], dst, sems.at[slot])

        if wait_first is True:
            copy().wait()
        elif wait_first is not False:
            pl.when(wait_first)(lambda: copy().wait())
        into[slot] = value.astype(BF16)
        copy().start()

    def put_gain(row, value):
        if linked:
            dgains[row:row + 1] = value
        elif row < 2:
            dgm_ref[row] = value
        elif row < 4:
            dgf_ref[row - 2] = value
        else:
            dgz_ref[...] = value

    def by_rows(run, init=None):
        def some(i, carry):
            return run(pl.ds(pl.multiple_of(i * CH, CH), CH), carry)

        return lax.fori_loop(0, CHUNKS, some, init)

    def normed_rows(src, gain, dst, dstT):
        def some(rows, carry):
            block = norm_forward(src[rows], gain).astype(BF16)
            dst[rows] = block
            dstT[:, rows] = placed(block.T)
            return carry

        by_rows(some, 0)

    def back_rows(src, gain, row):
        def some(rows, dgain):
            dv, dg = norm_backward(src[rows], gain, acc_ref[rows])
            dx_ref[rows] += dv
            return dgain + dg

        put_gain(row, by_rows(some, jnp.zeros((1, D), F32)))

    vocab_ids = lax.broadcasted_iota(jnp.int32, (LEN, VOCAB), 1)
    hot = (vocab_ids == columns[:, 0:1]).astype(F32).astype(BF16)
    x_ref[0] = mm_nt(hot, table_ref[...])
    if linked:
        links.ready(1)

    def keep(l, h, e):
        return (
            pltpu.make_async_copy(m_ref.at[e], kept_m.at[l, h], keep_sem.at[e, 0]),
            pltpu.make_async_copy(near_ref.at[e], kept_near.at[l, h], keep_sem.at[e, 1]),
        )

    def fetch(l, h, e):
        return (
            pltpu.make_async_copy(kept_m.at[l, h], m_ref.at[e], keep_sem.at[e, 0]),
            pltpu.make_async_copy(kept_near.at[l, h], near_ref.at[e], keep_sem.at[e, 1]),
        )

    m_ref[...] = jnp.zeros_like(m_ref)
    near_ref[...] = jnp.zeros_like(near_ref)

    def attention_forward(l):
        normed_rows(x_ref.at[l], gm_ref[l], yb_ref, hT_ref.at[l])
        h = yb_ref[...]
        for j in range(3):
            part = mm(h, wm_ref[l, :, j * TILE:(j + 1) * TILE]).astype(BF16)
            if j > 0:
                kv_ref[l, :, (j - 1) * TILE:j * TILE] = part
            pT_ref[l, j * TILE:(j + 1) * TILE, :] = part.T
        service((MIXER, l))
        kT = pT_ref[l, D:2 * D, :].astype(F32)
        a1k_ref[...] = feature_parts(kT)[0].astype(BF16)
        for i in range(CHUNKS):
            t0, t1 = i * CH, (i + 1) * CH
            cum_ref[l, :, t0:t1] = mm(a1k_ref[:, :t1], wide_ref[:t1, t0:t1])

        def pair(p, carry):
            base = pl.multiple_of(p * CH, CH)
            for e in range(2):
                row = pl.multiple_of(base + e * HD, HD)
                if l == 0:
                    pl.when(p > 0)(lambda: every(keep(l, 0, e), WAIT))
                else:
                    for copy in keep(l, 0, e):
                        copy.wait()
                qT = pT_ref[l, pl.ds(row, HD), :]
                kT = pT_ref[l, pl.ds(pl.multiple_of(D + row, HD), HD), :]
                vT = pT_ref[l, pl.ds(pl.multiple_of(2 * D + row, HD), HD), :]
                first_k, _, second_k = feature_parts(kT.astype(F32))
                key_feat = jnp.concatenate([first_k.astype(BF16), second_k.astype(BF16)], axis=0).T
                first_q = feature_parts(qT.astype(F32))[0].astype(BF16).astype(F32)
                total = jnp.sum(first_q * cum_ref[l, pl.ds(row, HD), :], axis=0, keepdims=True)
                inv1 = 1.0 / (total + 1.0)
                inv1_ref[l, 2 * p + e] = inv1
                query_feat2 = query_features(qT, inv1, inv2)[3]
                key_feat2 = jnp.concatenate([key_feat, key_feat], axis=1)
                key_nat = kv_ref[l, :, pl.ds(base, CH)]
                query_masked = masked_pair(qT, e)
                for t0, t1 in WIDE:
                    mixture = mixture_block(t0, t1, key_nat, key_feat2, query_masked, query_feat2, near_ref.at[e])
                    m_ref[e, :t1, t0:t1] = mixture
                    oT_ref[l, pl.ds(row, HD), t0:t1] = mm(vT[:, :t1], mixture).astype(BF16)
                for copy in keep(l, 2 * p + e, e):
                    copy.start()
                service((HEAD, l), 2 * p + e, lambda at: at % 2 == e)
            return carry

        lax.fori_loop(0, HEADS // 2, pair, 0)
        service((OUTPUT, l))
        o = oT_ref[l].T
        x1_ref[l] = x_ref[l] + mm(o, wo_ref[l])

    def feed_forward(l):
        normed_rows(x1_ref.at[l], gf_ref[l], g_ref, gT_ref.at[l])
        xs[l + 1][...] = x1_ref[l]
        service((FEED, l))

        def tile(j, carry):
            col = pl.multiple_of(j * BACK, BACK)
            active = gelu_parts(mm(g_ref[...], we_ref[l, :, pl.ds(col, BACK)]))[0].astype(BF16)
            service((GELU, l), j)
            xs[l + 1][...] += mm(active, wr_ref[l, pl.ds(col, BACK), :])
            service((FEED_TILE, l), j)
            return carry

        lax.fori_loop(0, FF // BACK, tile, 0)

    def head():
        zT_ref, grad_ref = doT_ref, yb_ref.at[:, :VOCAB]

        def some(rows, carry):
            dgain, cross_sum, val_sum = carry
            x = dx_ref[rows]
            z = norm_forward(x, gz_ref).astype(BF16)
            zT_ref[:, rows] = placed(z.T)
            logits = mm(z, table_ref[...])
            ids = lax.broadcasted_iota(jnp.int32, (CH, VOCAB), 1)
            tgt_hot = (ids == columns[rows, 1:2]).astype(F32)
            val = columns[rows, 2:3].astype(F32)
            peak = jnp.max(logits, axis=-1, keepdims=True)
            grown = jnp.exp(logits - peak)
            total = jnp.sum(grown, axis=-1, keepdims=True)
            lse = peak + jnp.log(total)
            picked = jnp.sum(logits * tgt_hot, axis=-1, keepdims=True)
            cross = (lse - picked) * val
            grad_b = ((grown / total - tgt_hot) * val).astype(BF16)
            grad_ref[rows, :] = grad_b
            if linked:
                grad_bT = grad_b.T
                for i in range(4):
                    lgs[i, :, rows] = grad_bT[64 * i:64 * i + 64]
            else:
                lg_ref[rows, :] = grad_b
            dv, dg = norm_backward(x, gz_ref, mm_nt(grad_b, table_ref[...]))
            dx_ref[rows] = dv
            return (
                dgain + dg,
                cross_sum + jnp.sum(cross, axis=0, keepdims=True),
                val_sum + jnp.sum(val, axis=0, keepdims=True),
            )

        nothing = jnp.zeros((1, 1), F32)
        dgain, cross_sum, val_sum = by_rows(some, (jnp.zeros((1, D), F32), nothing, nothing))
        put_gain(4, dgain)
        loss = jnp.broadcast_to(cross_sum / val_sum, (8, 128))
        if linked:
            losss[...] = loss
            for k in (1, 2, 3):
                lg_copy(k).start()
                loss_copy(k).start()
            pltpu.make_async_copy(lgs.at[zi], lg_ref.at[zi], zsend.at[1, 3]).start()
            pltpu.make_async_copy(losss, loss_ref.at[zi], zsend.at[2, 3]).start()
        else:
            loss_ref[...] = loss
        dtable_ref[...] = mm(zT_ref[...], grad_ref[...])

    def feed_backward(l):
        def some(rows, carry):
            yb = dx_ref[rows].astype(BF16)
            yb_ref[rows] = yb
            doT_ref[:, rows] = yb.T
            if l < LAYERS - 1:
                g_ref[rows] = norm_forward(x1_ref[l, rows], gf_ref[l]).astype(BF16)
            return carry

        by_rows(some, 0)
        acc_ref[...] = jnp.zeros_like(acc_ref)

        def tile(j, carry):
            col = pl.multiple_of(j * BACK, BACK)
            slot = lax.rem(j, 2)
            later = (j >= 2) if l == LAYERS - 1 else True
            value, slope = gelu_parts(mm(g_ref[...], we_ref[l, :, pl.ds(col, BACK)]))
            dreduce = mm(doT_ref[...], value.astype(BF16))
            if linked:
                place = pl.multiple_of(BACK * (lax.rem(j, 2) * 4 + lax.div(j, 2)), BACK)
                sums_refs["grad_r"][:, pl.ds(place, BACK)] = dreduce.astype(BF16)
                pl.when(lax.rem(j, 2) != sums.core)(lambda: sums.tile_copy(lax.div(j, 2)).start())
            else:
                emit(slot, later, dreduce, dwrt_ref.at[l, :, pl.ds(col, BACK)])
            dact = mm_nt(yb_ref[...], wr_ref[l, pl.ds(col, BACK), :])
            dhid = (dact * slope).astype(BF16)
            dexpand = mm(gT_ref[l], dhid)
            if linked:
                sums_refs["grad_e"][:, pl.ds(col, BACK)] = dexpand.astype(BF16)
            else:
                emit(2 + slot, later, dexpand, dwe_ref.at[l, :, pl.ds(col, BACK)])
            dnormed = mm_nt(dhid, we_ref[l, :, pl.ds(col, BACK)])

            acc_ref[...] += dnormed
            service((BACK_TILE, l), j)
            return carry

        lax.fori_loop(0, FF // BACK, tile, 0)
        service((BACK_FEED, l))
        back_rows(x1_ref.at[l], gf_ref[l], 2 + l)

    def attention_backward(l):
        yb_ref[...] = dx_ref[...].astype(BF16)
        yb = yb_ref[...]
        doutput = mm(placed(oT_ref[l]), yb)
        if linked:
            sums_refs["grad_o"][...] = doutput.astype(BF16)
        else:
            emit(0, l < LAYERS - 1, doutput, dwo_ref.at[l])
        service((BACK_OUTPUT, l))
        doT_ref[...] = mm_nt(yb, wo_ref[l]).astype(BF16).T

        for e in range(2):
            for copy in fetch(l, e, e):
                copy.start()

        def pair(p, carry):
            base = pl.multiple_of(p * CH, CH)
            for e in range(2):
                row = pl.multiple_of(base + e * HD, HD)
                qT = pT_ref[l, pl.ds(row, HD), :]
                kT = pT_ref[l, pl.ds(pl.multiple_of(D + row, HD), HD), :]
                doT = doT_ref[pl.ds(row, HD), :]
                inv1 = inv1_ref[l, 2 * p + e]
                first_q, slope1_q, second_q, query_feat2 = query_features(qT, inv1, inv2)
                first_k, slope1_k, second_k = feature_parts(kT.astype(F32))
                key_featT = jnp.concatenate([first_k.astype(BF16), second_k.astype(BF16)], axis=0)
                value_nat = kv_ref[l, :, pl.ds(pl.multiple_of(D + base, CH), CH)]
                do_masked = masked_pair(doT, e)
                for copy in fetch(l, 2 * p + e, e):
                    copy.wait()
                far_q, near_q = [], []
                for t0, t1 in WIDE:
                    dm = mm(value_nat[:t1], do_masked[:, t0:t1])

                    def half(i):
                        r0, end = first_row(i), (i + 1) * CH
                        column = dm[:end, i * CH - t0:end - t0]
                        bottom = column[r0:]
                        near = near_ref[e, i, :end - r0, :]
                        weighted = near * bottom
                        dsum = jnp.sum(weighted, axis=0, keepdims=True)
                        ds = ((weighted - near * dsum) * 0.125).astype(BF16)
                        if i > 0:
                            before = jnp.concatenate([jnp.zeros((CH - REACH, CH), BF16), ds[:REACH]], axis=0)
                            ds_ref[end - 2 * CH:end - CH, CH:] = before
                            ds = ds[REACH:]
                            near_q.append(mm(kT[:, end - 2 * CH:end], jnp.concatenate([before, ds], axis=0)))
                        else:
                            near_q.append(mm(kT[:, :end], ds))
                        ds_ref[end - CH:end, :CH] = ds
                        lower = causal_rows(i, bottom).astype(BF16)
                        if r0 == 0:
                            return lower
                        return jnp.concatenate([column[:r0].astype(BF16), lower], axis=0)

                    dm_b = halves(t0, t1, half)
                    d_ref[:t1, t0:t1] = dm_b
                    far_q.append(mm(key_featT[:, :t1], dm_b))
                farT = jnp.concatenate(far_q, axis=1)
                y1, y2 = farT[:HD], farT[HD:]
                first_qf = first_q.astype(F32)
                m = inv1 * jnp.sum(first_qf * y1, axis=0, keepdims=True)
                cum = cum_ref[l, pl.ds(row, HD), :]
                dq = jnp.concatenate(near_q, axis=1)
                dq = dq + (inv1 * (y1 - m * cum)) * slope1_q + (inv2 * y2) * (1.0 - second_q * second_q)
                dpT_ref[pl.ds(row, HD), :] = dq.astype(BF16)
                w_ref[pl.ds(row, HD), :] = (first_qf * (m * inv1)).astype(BF16)
                for t0, t1 in WIDE:
                    far = mm_nt(query_feat2[:CH, t0:], d_ref[t0:t1, t0:])
                    back = mm_nt(w_ref[pl.ds(row, HD), t0:], wide_ref[t0:t1, t0:])
                    near_k = []
                    for u0 in range(t0, t1, CH):
                        u2 = min(u0 + 2 * CH, LEN)
                        near_k.append(mm_nt(qT[:, u0:u2], ds_ref[u0:u0 + CH, :u2 - u0]))
                    near = near_k[0] if len(near_k) == 1 else jnp.concatenate(near_k, axis=1)
                    dk = near + (far[:HD] - back) * slope1_k[:, t0:t1]
                    dk = dk + far[HD:] * (1.0 - second_k[:, t0:t1] * second_k[:, t0:t1])
                    dpT_ref[pl.ds(pl.multiple_of(D + row, HD), HD), t0:t1] = dk.astype(BF16)
                    dv = mm_nt(doT[:, t0:], m_ref[e, t0:t1, t0:])
                    dpT_ref[pl.ds(pl.multiple_of(2 * D + row, HD), HD), t0:t1] = dv.astype(BF16)
                pl.when(p < HEADS // 2 - 1)(lambda: every(fetch(l, 2 * p + e + 2, e), START))
                service((BACK_HEAD, l), 2 * p + e, lambda at: at % 2 == e)
            if linked:
                for j in range(3):
                    block = mm_nt(hT_ref[l], dpT_ref[pl.ds(pl.multiple_of(j * D + base, CH), CH), :])
                    place = pl.multiple_of(3 * base + j * CH, CH)
                    sums_refs["grad_m"][:, pl.ds(place, CH)] = block.astype(BF16)
                service((BACK_PAIR, l), p)
            return carry

        lax.fori_loop(0, HEADS // 2, pair, 0)
        if not linked:
            for j in range(3):
                block = mm_nt(hT_ref[l], dpT_ref[j * TILE:(j + 1) * TILE, :])
                emit(1 + j, l < LAYERS - 1, block, dwm_ref.at[l, :, j * TILE:(j + 1) * TILE])
        for t0 in range(0, LEN, 256):
            t1 = min(t0 + 256, LEN)
            acc_ref[t0:t1] = mm(wm_ref[l], dpT_ref[:, t0:t1]).T
        service((BACK_MIXER, l))
        back_rows(x_ref.at[l], gm_ref[l], l)
        service((BACK_LAYER, l))

    for l in range(LAYERS):
        service((LAYER, l))
        attention_forward(l)
        feed_forward(l)
    for e in range(2):
        for copy in keep(0, 0, e):
            copy.wait()
    head()
    for l in reversed(range(LAYERS)):
        feed_backward(l)
        attention_backward(l)
    dtable_sum = dtable_ref[...] + mm(placed(dx_ref[...].astype(BF16).T), hot)
    if linked:
        sums_refs["grad_t"][:, :VOCAB] = dtable_sum.astype(BF16)
        sums_refs["grad_t"][:, VOCAB:] = placed(jnp.concatenate([dgains[...], jnp.zeros((120, D), F32)], axis=0).T).astype(BF16)
        service((END, 0))
        for k in (1, 2, 3):
            table_copy(k).wait_send()
            lg_copy(k).wait()
            loss_copy(k).wait()
        pltpu.make_async_copy(lgs.at[zi], lg_ref.at[zi], zsend.at[1, 3]).wait()
        pltpu.make_async_copy(losss, loss_ref.at[zi], zsend.at[2, 3]).wait()
        links.finish()
    else:
        dtable_ref[...] = dtable_sum
        for slot in range(4):
            pltpu.make_async_copy(stage.at[slot], dwo_ref.at[0], sem.at[slot]).wait()
            pltpu.make_async_copy(stage_half.at[slot], dwe_ref.at[0, :, :BACK], sem_half.at[slot]).wait()


E0, E1, R0, R1, M0, M1, M2, M3, O, T = range(10)
MIXER, HEAD, FEED, GELU, FEED_TILE, LAYER, BACK_TILE, BACK_FEED, BACK_OUTPUT, BACK_HEAD, BACK_PAIR, BACK_MIXER, BACK_LAYER, END, OUTPUT = range(15)
SHARED = ((False, False, True, False), (False, False, True, False))
SERVICE = {
    (MIXER, 0): {
        None: ((Links.second, 2), (Links.first, 3),),
    },
    (HEAD, 0): {
        0: ((Links.own, 5),),
        4: ((Links.first, 4),),
        5: ((Links.second, 3),),
        7: ((Links.own, 6),),
    },
    (OUTPUT, 0): {
        None: ((Links.ready, 2),),
    },
    (FEED, 0): {
        None: ((Links.own, 7), (Links.third, 3), (Links.ready, 3),),
    },
    (GELU, 0): {
        0: ((Links.second, 4), (Links.ready, 4),),
    },
    (FEED_TILE, 0): {
        0: ((Links.first, 5), (Links.first, 6), (Links.own, 8),),
        5: ((Links.first, 7),),
    },
    (LAYER, 1): {
        None: ((Links.second, 5), (Links.ready, 5),),
    },
    (MIXER, 1): {
        None: ((Links.second, 6),),
    },
    (HEAD, 1): {
        1: ((Links.first, 8),),
        3: ((Links.second, 7),),
        7: ((Links.second, 8),),
    },
    (OUTPUT, 1): {
        None: ((Links.ready, 6),),
    },
    (FEED, 1): {
        None: ((Links.third, 7), (Links.ready, 7),),
    },
    (GELU, 1): {
        0: ((Links.ready, 8),),
    },
    (BACK_TILE, 1): {
        3: ((E0, 1, 1),),
        5: ((E0, 2, 1),),
    },
    (BACK_FEED, 1): {
        None: ((E1, 1, 1),),
    },
    (BACK_OUTPUT, 1): {
        None: ((O, 1, 1), (R0, 2, 1), (R1, 2, 1),),
    },
    (BACK_HEAD, 1): {
        0: ((E0, 3, 1), (E1, 2, 1), (O, 2, 1),),
        2: ((R0, 3, 1), (M0, 2, 1),),
        3: ((R1, 3, 1),),
        4: ((E0, 4, 1), (M1, 2, 1),),
        6: ((O, 3, 1), (M2, 2, 1),),
        7: ((E0, 5, 1), (R0, 4, 1), (M0, 3, 1),),
    },
    (BACK_PAIR, 1): {
        0: ((M0, 1, 1),),
        1: ((M1, 1, 1),),
        2: ((M2, 1, 1), (E1, 3, 1),),
        3: ((M3, 1, 1),),
    },
    (BACK_MIXER, 1): {
        None: ((R1, 4, 1), (M3, 2, 1),),
    },
    (BACK_LAYER, 1): {
        None: ((M1, 3, 1),),
    },
    (BACK_TILE, 0): {
        0: ((E0, 6, 1), (R0, 5, 1), (E1, 4, 1), (O, 4, 1), (M2, 3, 1),),
        1: ((M0, 4, 1), (M3, 3, 1), (R1, 5, 1), (M1, 4, 1),),
        2: ((M2, 4, 1),),
        3: ((E0, 1, 0), (R0, 6, 1), (E1, 5, 1), (E0, 7, 1), (M3, 4, 1),),
        4: ((O, 5, 1),),
        5: ((R1, 6, 1), (M0, 5, 1), (M1, 5, 1), (E0, 2, 0),),
        6: ((M2, 5, 1), (E1, 6, 1), (M3, 5, 1),),
        7: ((O, 6, 1), (R0, 7, 1),),
    },
    (BACK_FEED, 0): {
        None: ((E1, 1, 0),),
    },
    (BACK_OUTPUT, 0): {
        None: ((O, 1, 0), (M0, 6, 1), (R0, 2, 0), (M1, 6, 1),),
    },
    (BACK_HEAD, 0): {
        0: ((M2, 6, 1), (M3, 6, 1), (R1, 7, 1), (E0, 3, 0), (R1, 2, 0),),
        1: ((E1, 7, 1), (E1, 2, 0),),
        2: ((M0, 7, 1), (O, 7, 1), (R0, 3, 0), (E0, 4, 0), (M0, 2, 0), (O, 2, 0),),
        3: ((M1, 7, 1), (M2, 7, 1),),
        4: ((M3, 7, 1), (R1, 3, 0), (E0, 5, 0), (M1, 2, 0),),
        5: ((E1, 3, 0),),
        6: ((R0, 4, 0), (M2, 2, 0), (M0, 3, 0),),
        7: ((E0, 6, 0), (O, 3, 0),),
    },
    (BACK_PAIR, 0): {
        0: ((M0, 1, 0),),
        1: ((M1, 1, 0),),
        2: ((M2, 1, 0),),
        3: ((M3, 1, 0),),
    },
    (BACK_MIXER, 0): {
        None: ((R0, 5, 0), (R1, 4, 0), (M3, 2, 0), (M1, 3, 0),),
    },
    (END, 0): {
        None: (
            (T, 1, 0), (E1, 4, 0), (M2, 3, 0), (T, 2, 0), (M0, 4, 0), (R1, 5, 0), (O, 4, 0), (M3, 3, 0), (R0, 6, 0), (M1, 4, 0),
            (M2, 4, 0), (E1, 5, 0), (T, 3, 0), (M0, 5, 0), (M3, 4, 0), (O, 5, 0), (R1, 6, 0), (T, 4, 0), (M1, 5, 0), (M2, 5, 0),
            (E1, 6, 0), (M3, 5, 0), (M0, 6, 0), (T, 5, 0), (O, 6, 0), (M1, 6, 0), (M2, 6, 0), (M3, 6, 0), (T, 6, 0), (E0, 7, 0),
            (R0, 7, 0), (R1, 7, 0), (E1, 7, 0), (M0, 7, 0), (O, 7, 0), (M1, 7, 0), (M2, 7, 0), (M3, 7, 0), (T, 7, 0),
        ),
    },
}

PLAIN_IN = ("columns", "table", "gm", "gf", "gz", "wm", "wo", "we", "wr")
PLAIN_OUT = ("loss", "lg", "kept_m", "kept_near", "dtable", "dgm", "dgf", "dgz", "dwm", "dwo", "dwe", "dwrt")
LINKED_IN = ("tokens", "mask", "emb", "mgain", "fgain", "zgain", "wm_s", "wo_s", "we_s", "wr_s")
LINKED_OUT = ("loss", "lg", "kept_m", "kept_near", "out_m", "out_o", "out_e", "out_r", "out_t")
SCRATCH = dict(
    x=pltpu.VMEM((LAYERS, LEN, D), F32),
    x1=pltpu.VMEM((LAYERS, LEN, D), F32),
    dx=pltpu.VMEM((LEN, D), F32),
    kv=pltpu.VMEM((LAYERS, LEN, 2 * D), BF16),
    pT=pltpu.VMEM((LAYERS, 3 * D, LEN), BF16),
    inv1s=pltpu.VMEM((LAYERS, HEADS, 1, LEN), F32),
    cum=pltpu.VMEM((LAYERS, D, LEN), F32),
    oT=pltpu.VMEM((LAYERS, D, LEN), BF16),
    hT=pltpu.VMEM((LAYERS, D, LEN), BF16),
    g=pltpu.VMEM((LEN, D), BF16),
    gT=pltpu.VMEM((LAYERS, D, LEN), BF16),
    wide=pltpu.VMEM((LEN, LEN), BF16),
    a1k=pltpu.VMEM((D, LEN), BF16),
    m=pltpu.VMEM((2, LEN, LEN), BF16),
    near=pltpu.VMEM((2, CHUNKS, CH + REACH, CH), F32),
    keep_sem=pltpu.SemaphoreType.DMA((2, 2)),
    d=pltpu.VMEM((LEN, LEN), BF16),
    ds=pltpu.VMEM((LEN, 2 * CH), BF16),
    doT=pltpu.VMEM((D, LEN), BF16),
    dpT=pltpu.VMEM((3 * D, LEN), BF16),
    yb=pltpu.VMEM((LEN, D), BF16),
    acc=pltpu.VMEM((LEN, D), F32),
)
PLAIN_SCRATCH = dict(
    stage=pltpu.VMEM((4, D, TILE), BF16),
    stage_half=pltpu.VMEM((4, D, BACK), BF16),
    sem=pltpu.SemaphoreType.DMA((4,)),
    sem_half=pltpu.SemaphoreType.DMA((4,)),
)


def sum_buffers(n, rows, cols, along):
    def shape(blocks):
        return (rows * blocks // 8, cols) if along == 0 else (rows, cols * blocks // 8)

    return {
        "grad_" + n: pltpu.VMEM((rows, cols), BF16),
        "r1" + n: pltpu.VMEM(shape(4), BF16),
        "r2" + n: pltpu.VMEM(shape(2), BF16),
        "r3" + n: pltpu.VMEM(shape(1), BF16),
        "rz" + n: pltpu.VMEM((2,) + shape(1), BF16),
    }


LINKED_SCRATCH = dict(
    table=pltpu.VMEM((D, 384), BF16),
    wm=pltpu.VMEM((LAYERS, D, 3 * D), BF16),
    wo=pltpu.VMEM((LAYERS, D, D), BF16),
    we=pltpu.VMEM((LAYERS, D, FF), BF16),
    wr=pltpu.VMEM((LAYERS, FF, D), BF16),
    columns=pltpu.VMEM((LEN, 8), jnp.int32),
    tz=pltpu.VMEM((4, 64, 128), BF16),
    gains=pltpu.VMEM((8, D), F32),
    lgs=pltpu.VMEM((4, 64, LEN), BF16),
    losss=pltpu.VMEM((8, 128), F32),
    send_sem=pltpu.SemaphoreType.DMA((9, 15)),
    recv_sem=pltpu.SemaphoreType.DMA((9, 15)),
    zsend=pltpu.SemaphoreType.DMA((3, 4)),
    zrecv=pltpu.SemaphoreType.DMA((3, 4)),
    load_sem=pltpu.SemaphoreType.DMA((LAYERS, 9)),
    sum_send=pltpu.SemaphoreType.DMA((10, 10)),
    sum_recv=pltpu.SemaphoreType.DMA((10, 9)),
    tile_send=pltpu.SemaphoreType.DMA((4,)),
    tile_recv=pltpu.SemaphoreType.DMA((4,)),
    dtable=pltpu.VMEM((D, VOCAB), F32),
    dgains=pltpu.VMEM((8, D), F32),
    **sum_buffers("m", D, 3 * D, 0),
    **sum_buffers("o", D, D, 0),
    **sum_buffers("e", D, FF, 0),
    **sum_buffers("r", D, FF, 1),
    **sum_buffers("t", D, 384, 0),
)


def local_step(linked, *operands):
    vmem = pl.BlockSpec(memory_space=pltpu.VMEM)
    hbm = pl.BlockSpec(memory_space=pl.ANY)
    shape = jax.ShapeDtypeStruct
    kept = (shape((LAYERS, HEADS, LEN, LEN), BF16), shape((LAYERS, HEADS, CHUNKS, CH + REACH, CH), F32))
    if linked:
        scratch = dict(SCRATCH, **LINKED_SCRATCH)
        in_specs = [vmem] * 6 + [hbm] * 4
        out_shape = (
            shape((4, 8, 128), F32),
            shape((4, 64, LEN), BF16),
            *kept,
            shape((LAYERS, 4, 64, 384), BF16),
            shape((LAYERS, 64, D), BF16),
            shape((LAYERS, 64, FF), BF16),
            shape((LAYERS, D, 256), BF16),
            shape((64, 384), BF16),
        )
        out_specs = (hbm,) * 9
    else:
        scratch = dict(SCRATCH, **PLAIN_SCRATCH)
        in_specs = [vmem] * len(operands)
        out_shape = (
            shape((8, 128), F32),
            shape((LEN, VOCAB), BF16),
            *kept,
            shape((D, VOCAB), F32),
            shape((LAYERS, 1, D), F32),
            shape((LAYERS, 1, D), F32),
            shape((1, D), F32),
            shape((LAYERS, D, 3 * D), BF16),
            shape((LAYERS, D, D), BF16),
            shape((LAYERS, D, FF), BF16),
            shape((LAYERS, D, FF), BF16),
        )
        out_specs = (vmem,) * 2 + (hbm,) * 2 + (vmem,) * 4 + (hbm,) * 4
    return pl.pallas_call(
        functools.partial(step_kernel, linked),
        out_shape=out_shape,
        in_specs=in_specs,
        out_specs=out_specs,
        scratch_shapes=list(scratch.values()),
        compiler_params=pltpu.CompilerParams(
            vmem_limit_bytes=64 * 1024 * 1024,
            collective_id=0 if linked else None,
            has_side_effects=linked,
        ),
        cost_estimate=pl.CostEstimate(flops=40_000_000_000, bytes_accessed=40_000_000, transcendentals=0),
        name="local_step",
    )(*operands)


def finish_kernel(
    loss_in, lg_in, dwm_in, dwo_in, dwe_in, dwrt_in, last_in,
    out_loss, out_lg, out_table, out_m, out_o, out_mgain, out_e, out_r, out_fgain, out_zgain,
    loss, lg, dwm, dwo, dwe, dwrt, last, sem,
):
    pairs = ((loss_in, loss), (lg_in, lg), (dwm_in, dwm), (dwo_in, dwo), (dwe_in, dwe), (dwrt_in, dwrt), (last_in, last))
    copies = [pltpu.make_async_copy(src, dst, sem.at[i]) for i, (src, dst) in enumerate(pairs)]
    every(copies, START)
    every(copies, WAIT)
    z = lax.axis_index(SECTION)
    r, c = iotas(4, 128)
    out_loss[...] = jnp.sum(jnp.where(r == c, loss[:, 0, :], 0.0), axis=0, keepdims=True)
    out_lg[...] = lg[...].astype(F32)
    table = last[:, :VOCAB].astype(F32)
    out_table[...] = sum(jnp.where(z == i, table[:, 64 * i:64 * (i + 1)], 0.0) for i in range(4))
    gains = last[:, VOCAB:].astype(F32)
    gains = jnp.concatenate([gains, jnp.zeros((64, 128), F32)], axis=0).T
    out_mgain[...] = gains[0:2, :64]
    out_fgain[...] = gains[2:4, :64]
    out_zgain[...] = gains[4:5, :64]
    out_o[...] = dwo[...].astype(F32)
    out_e[...] = dwe[...].astype(F32)
    for l in range(LAYERS):
        out_r[l] = dwrt[l].astype(F32).T
        for p in range(4):
            for j in range(3):
                out_m[l, :, D * j + CH * p:D * j + CH * (p + 1)] = dwm[l, p, :, CH * j:CH * (j + 1)].astype(F32)


def finish(*operands):
    vmem = pl.BlockSpec(memory_space=pltpu.VMEM)
    shapes = (
        (1, 128), (4, 64, LEN), (64, 64), (LAYERS, 64, 3 * D), (LAYERS, 64, D), (LAYERS, 64), (LAYERS, 64, FF),
        (LAYERS, 256, D), (LAYERS, 64), (1, 64),
    )
    return pl.pallas_call(
        finish_kernel,
        out_shape=tuple(jax.ShapeDtypeStruct(shape, F32) for shape in shapes),
        in_specs=[pl.BlockSpec(memory_space=pl.ANY)] * len(operands),
        out_specs=(vmem,) * len(shapes),
        scratch_shapes=[pltpu.VMEM(operand.shape, operand.dtype) for operand in operands]
        + [pltpu.SemaphoreType.DMA((len(operands),))],
        compiler_params=pltpu.CompilerParams(vmem_limit_bytes=60 * 1024 * 1024),
        name="finish",
    )(*operands)


def body(
    tokens,
    padding_mask,
    embedding,
    mixer_weight,
    output_weight,
    mixer_gain,
    expand_weight,
    reduce_weight,
    feed_gain,
    final_gain,
):
    segments = lax.axis_size(SECTION)
    segment_index = lax.axis_index(SECTION)
    item_count = tokens.shape[0]
    assert item_count == segments
    slice_width = embedding.shape[1]

    if segments == 4 and lax.axis_size(DP) == 8:
        loss, lg, _, _, dwm, dwo, dwe, dwrt, last = local_step(
            True, tokens, padding_mask, embedding, mixer_gain, feed_gain, final_gain[None],
            mixer_weight, output_weight, expand_weight, reduce_weight,
        )
        loss, lg, table_grad, dwm, dwo, mixer_gain_grad, dwe, dwr, feed_gain_grad, final_gain_grad = finish(
            loss, lg, dwm, dwo, dwe, dwrt, last
        )
        return (
            loss[0, :4], jnp.swapaxes(lg, 1, 2), table_grad, dwm, dwo, mixer_gain_grad, dwe, dwr, feed_gain_grad, final_gain_grad[0]
        )

    token_row = lax.dynamic_index_in_dim(tokens, segment_index, 0, keepdims=False)
    mask_row = lax.dynamic_index_in_dim(padding_mask, segment_index, 0, keepdims=False)
    zero = jnp.zeros((1,), jnp.int32)
    columns = jnp.stack(
        [token_row, jnp.concatenate([token_row[1:], zero]), jnp.concatenate([mask_row[1:], zero])], axis=1
    )

    def gather(block, dim):
        return lax.all_gather(block.astype(BF16), DP, axis=dim, tiled=True)

    table = lax.all_gather(gather(embedding, 0), SECTION, axis=1, tiled=True)
    gains = gather(jnp.concatenate([mixer_gain, feed_gain, final_gain[None]], axis=0), 1).astype(F32)
    loss, lg, _, _, dtable, dgm, dgf, dgz, dwm, dwo, dwe, dwrt = local_step(
        False, columns, table, gains[0:2, None], gains[2:4, None], gains[4:5],
        gather(mixer_weight, 1), gather(output_weight, 1), gather(expand_weight, 1), gather(reduce_weight, 1),
    )
    item_loss = lax.all_gather(loss[0, 0], SECTION)
    parts = lg.reshape(LEN, segments, slice_width).transpose(1, 0, 2)
    logit_grad = lax.all_to_all(parts, SECTION, 0, 0, tiled=True).astype(F32)

    def shard(grad, dim):
        part = lax.psum_scatter(grad.astype(BF16), DP, scatter_dimension=dim, tiled=True)
        return lax.psum(part, SECTION).astype(F32)

    table_part = lax.psum_scatter(dtable.astype(BF16), DP, scatter_dimension=0, tiled=True)
    table_grad = lax.psum_scatter(table_part, SECTION, scatter_dimension=1, tiled=True).astype(F32)
    gain_grads = lax.psum_scatter(
        jnp.concatenate([dgm[:, 0], dgf[:, 0], dgz], axis=0), DP, scatter_dimension=1, tiled=True
    )
    gain_grads = lax.psum(gain_grads, SECTION)
    return (
        item_loss,
        logit_grad,
        table_grad,
        shard(dwm, 1),
        shard(dwo, 1),
        gain_grads[0:2],
        shard(dwe, 1),
        jnp.swapaxes(shard(dwrt, 2), 1, 2),
        gain_grads[2:4],
        gain_grads[4],
    )


def solution(mesh):
    placed = (
        P(DP, None),
        P(DP, None),
        P(DP, SECTION),
        P(None, DP, None),
        P(None, DP, None),
        P(None, DP),
        P(None, DP, None),
        P(None, DP, None),
        P(None, DP),
        P(DP),
    )
    return jax.shard_map(
        body,
        mesh=mesh,
        in_specs=placed,
        out_specs=(
            P(DP),
            P(DP, None, SECTION),
            P(DP, SECTION),
            P(None, DP, None),
            P(None, DP, None),
            P(None, DP),
            P(None, DP, None),
            P(None, DP, None),
            P(None, DP),
            P(DP),
        ),
        check_vma=False,
    )
```

```python
import functools

import jax
import jax.numpy as jnp
from jax import lax
from jax.experimental import pallas as pl
from jax.experimental.pallas import tpu as pltpu
from jax.sharding import PartitionSpec as P

D = 512
HEADS = 8
HD = 64
FF = 2048
VOCAB = 256
BAND = 30
LEN = 640
LAYERS = 2
CH = 128
CHUNKS = LEN // CH
REACH = 32
WIDE = tuple((t0, min(t0 + 256, LEN)) for t0 in range(0, LEN, 256))
TILE = 512
BACK = 256
F32 = jnp.float32
DP, SECTION = ("dp", "section")
BF16 = jnp.bfloat16


def mm(left, right):
    return jnp.dot(left, right, preferred_element_type=F32)


def mm_nt(left, right):
    return lax.dot_general(left, right, (((1,), (1,)), ((), ())), preferred_element_type=F32)


def norm_forward(v, gain):
    scale = lax.rsqrt(jnp.mean(v * v, axis=-1, keepdims=True) + 1e-05)
    return v * scale * gain


def norm_backward(v, gain, dy):
    scale = lax.rsqrt(jnp.mean(v * v, axis=-1, keepdims=True) + 1e-05)
    normed = v * scale
    dgain = jnp.sum(dy * normed, axis=0, keepdims=True)
    dyg = dy * gain
    dv = scale * (dyg - normed * jnp.mean(dyg * normed, axis=-1, keepdims=True))
    return dv, dgain


def gelu_parts(u):
    c = 0.7978845608028654
    square = u * u
    t = jnp.tanh(u * (c + (c * 0.044715) * square))
    half = 0.5 * (1.0 + t)
    value = u * half
    slope = half + 0.5 * u * (1.0 - t * t) * (c + (3.0 * c * 0.044715) * square)
    return value, slope


def feature_parts(u):
    low_exp = jnp.exp(jnp.minimum(u, 0.0))
    first = jnp.where(u > 0.0, u + 1.0, low_exp)
    second = jnp.tanh(u)
    return first, low_exp, second


def iotas(rows, cols, row0=0):
    r = lax.broadcasted_iota(jnp.int32, (rows, cols), 0) + row0
    c = lax.broadcasted_iota(jnp.int32, (rows, cols), 1)
    return r, c


def near_part(i, key_rows, query_cols):
    row0 = -REACH if i > 0 else 0
    scores = mm(key_rows, query_cols) * 0.125
    r, c = iotas(CH - row0, CH, row0)
    ok = (r <= c) & (c - r < BAND)
    scores = jnp.where(ok, scores, -1e30)
    peak = jnp.max(scores, axis=0, keepdims=True)
    weights = jnp.exp(scores - peak)
    return weights / jnp.sum(weights, axis=0, keepdims=True)


def causal_rows(i, block):
    row0 = -REACH if i > 0 else 0
    r, c = iotas(CH - row0, CH, row0)
    return jnp.where(r <= c, block, 0.0)


START, WAIT = range(2)


def every(copies, act):
    for copy in copies:
        if act == START:
            copy.start()
        else:
            copy.wait()


def halves(t0, t1, half):
    parts = []
    for i in range(t0 // CH, t1 // CH):
        part = half(i)
        if part.shape[0] < t1:
            part = jnp.concatenate([part, jnp.zeros((t1 - part.shape[0], CH), part.dtype)], axis=0)
        parts.append(part)
    return parts[0] if len(parts) == 1 else jnp.concatenate(parts, axis=1)


def first_row(i):
    return i * CH - REACH if i > 0 else 0


def mixture_block(t0, t1, key_nat, key_feat2, query_masked, query_feat2, near_ref):
    far = mm(key_feat2[:t1], query_feat2[:, t0:t1])

    def half(i):
        r0, end = first_row(i), (i + 1) * CH
        near = near_part(i, key_nat[r0:end], query_masked[:, i * CH:end])
        near_ref[i, :end - r0, :] = near
        column = far[:end, i * CH - t0:end - t0]
        bottom = (causal_rows(i, column[r0:]) + near).astype(BF16)
        if r0 == 0:
            return bottom
        return jnp.concatenate([column[:r0].astype(BF16), bottom], axis=0)

    return halves(t0, t1, half)


def query_features(qT, inv1, inv2):
    first, slope1, second = feature_parts(qT.astype(F32))
    first_b, second_b = first.astype(BF16), second.astype(BF16)
    scaled = jnp.concatenate([first_b.astype(F32) * inv1, second_b.astype(F32) * inv2], axis=0)
    high = scaled.astype(BF16)
    rest = (scaled - high.astype(F32)).astype(BF16)
    return first_b, slope1, second, jnp.concatenate([high, rest], axis=0)


def masked_pair(part, e):
    zero = jnp.zeros_like(part)
    return jnp.concatenate([part, zero] if e == 0 else [zero, part], axis=0)


ALL, MINE, MINE_A, MINE_B, OTHER = range(5)


class Links:
    def __init__(self, pieces, send_sem, recv_sem):
        self.pieces, self.send_sem, self.recv_sem = pieces, send_sem, recv_sem
        d, z = lax.axis_index(DP), lax.axis_index(SECTION)
        core, x, y = d % 2, (d // 2) % 2, d // 4
        self.d, self.half = d, z % 2
        self.core_n, self.x_n, self.y_n, self.z_n = d + 1 - 2 * core, d + 2 - 4 * x, d + 4 - 8 * y, z + 1 - 2 * (z % 2)
        self.diag = self.x_n + 4 - 8 * y

    def columns(self, n, part):
        _, _, cols, cut, shared = self.pieces[n]
        if part == ALL or (part == MINE and not shared):
            return slice(None)
        if not shared:
            return slice(0, cut) if part == MINE_A else slice(cut, cols)
        half, quarter = cols // 2, cols // 4
        start = half * (1 - self.half if part == OTHER else self.half) + (quarter if part == MINE_B else 0)
        return pl.ds(pl.multiple_of(start, quarter), quarter if part in (MINE_A, MINE_B) else half)

    def copy(self, n, kind):
        ref, rows = self.pieces[n][:2]
        core, x, y, z = {DP: self.core_n}, {DP: self.x_n}, {DP: self.y_n}, {SECTION: self.z_n}
        block, part, target = (
            (self.d, MINE, x),
            (self.d, MINE, y),
            (self.y_n, MINE_A, x),
            (self.x_n, MINE_B, y),
            (self.d, ALL, core),
            (self.x_n, MINE, core),
            (self.y_n, MINE, core),
            (self.diag, MINE_A, core),
            (self.diag, MINE_B, core),
            (self.x_n, MINE, z),
            (self.y_n, MINE, z),
            (self.diag, MINE, z),
            (self.x_n, OTHER, core),
            (self.y_n, OTHER, core),
            (self.diag, OTHER, core),
        )[kind]
        view = ref.at[pl.ds(pl.multiple_of(block * rows, rows), rows), self.columns(n, part)]
        return pltpu.make_async_remote_copy(
            src_ref=view, dst_ref=view, send_sem=self.send_sem.at[n, kind], recv_sem=self.recv_sem.at[n, kind],
            device_id=target, device_id_type=pl.DeviceIdType.MESH,
        )

    def own(self, *ns):
        for n in ns:
            for kind in (0, 1, 4):
                self.copy(n, kind).start()

    def first(self, *ns):
        for n in ns:
            shared = self.pieces[n][4]
            self.copy(n, 0).wait_recv()
            self.copy(n, 3).start()
            self.copy(n, 1).wait_recv()
            self.copy(n, 2).start()
            for kind in (9, 10, 5, 6) if shared else (5, 6):
                self.copy(n, kind).start()

    def second(self, *ns):
        for n in ns:
            shared = self.pieces[n][4]
            self.copy(n, 2).wait_recv()
            self.copy(n, 7).start()
            self.copy(n, 3).wait_recv()
            for kind in (11, 8) if shared else (8,):
                self.copy(n, kind).start()

    def third(self, *ns):
        for n in ns:
            for kind in (9, 10, 11):
                self.copy(n, kind).wait_recv()
                self.copy(n, kind + 3).start()

    def ready(self, *ns):
        for n in ns:
            for kind in (4, 5, 6, 7, 8) + ((12, 13, 14) if self.pieces[n][4] else ()):
                self.copy(n, kind).wait_recv()

    def finish(self):
        for n, piece in enumerate(self.pieces):
            for kind in range(15 if piece[4] else 9):
                self.copy(n, kind).wait_send()


class Sums:
    def __init__(self, links, pieces, send_sem, recv_sem, tile_send, tile_recv):
        self.links, self.pieces, self.send_sem, self.recv_sem = links, pieces, send_sem, recv_sem
        self.tile_send, self.tile_recv = tile_send, tile_recv
        d = links.d
        self.core, self.x, self.y = d % 2, (d // 2) % 2, d // 4
        self.z = lax.axis_index(SECTION)
        self.inner = (self.z == 1) | (self.z == 2)
        self.outer = (self.z == 0) | (self.z == 3)

    def view(self, piece, ref, block, count, half=None):
        blocks = pl.ds(pl.multiple_of(block * piece.size, piece.size), count * piece.size)
        across = {None: slice(None), 0: slice(0, piece.split), 1: slice(piece.split, piece.across)}[half]
        return ref.at[across, blocks] if piece.by_columns else ref.at[blocks, across]

    def tile_copy(self, block):
        r = self.pieces[R0]
        src = r.whole.at[:, pl.ds(pl.multiple_of((4 * (1 - self.core) + block) * r.size, r.size), r.size)]
        dst = r.whole_r1.at[:, pl.ds(pl.multiple_of(block * r.size, r.size), r.size)]
        return pltpu.make_async_remote_copy(
            src_ref=src, dst_ref=dst, send_sem=self.tile_send.at[block], recv_sem=self.tile_recv.at[block],
            device_id={DP: self.links.core_n}, device_id_type=pl.DeviceIdType.MESH,
        )

    def copy(self, name, kind, l=0):
        piece = self.pieces[name]
        core, x, y, z, links = self.core, self.x, self.y, self.z, self.links
        mine = 4 * core

        def pair(block, to, at, count, half):
            return self.view(piece, piece.grad, block, count, half), self.view(piece, to, at, count, half)

        if kind == 0:
            src, dst = pair(4 * (1 - core), piece.r1, 0, 4, None)
        elif kind in (1, 2):
            src, dst = pair(mine + 2 * (kind - 1) + 1 - x, piece.r2, kind - 1, 1, 0)
        elif kind == 3:
            src, dst = pair(mine + 2 * (1 - y), piece.r2, 0, 2, 1)
        elif kind == 4:
            src, dst = pair(mine + 2 * (1 - y) + x, piece.r3[l], 0, 1, 0)
        elif kind == 5:
            src, dst = pair(mine + 2 * y + 1 - x, piece.r3[l], 0, 1, 1)
        else:
            src = piece.r3[l]
            dst = piece.rz.at[kind - 6] if kind < 8 else piece.out(l)
        device = (
            {DP: links.core_n}, {DP: links.x_n}, {DP: links.x_n}, {DP: links.y_n}, {DP: links.y_n}, {DP: links.x_n},
            {SECTION: z + 1 - 2 * (z // 3)}, {SECTION: 3 - z}, {SECTION: 3 * (z // 2)},
        )[kind]
        return pltpu.make_async_remote_copy(
            src_ref=src, dst_ref=dst, send_sem=self.send_sem.at[piece.index, kind], recv_sem=self.recv_sem.at[piece.index, kind],
            device_id=device, device_id_type=pl.DeviceIdType.MESH,
        )

    def tile_parts(self, block):
        y, x = block // 2, block % 2
        copies = []
        for name in (R0, R1):
            piece = self.pieces[name]
            for half, kind, to, at in ((0, 1 + y, {DP: self.links.x_n}, y), (1, 3 + 7 * x, {DP: self.links.y_n}, x)):
                copies.append(pltpu.make_async_remote_copy(
                    src_ref=self.view(piece, piece.grad, 4 * self.core + block, 1, half), dst_ref=self.view(piece, piece.r2, at, 1, half),
                    send_sem=self.send_sem.at[piece.index, kind], recv_sem=self.recv_sem.at[piece.index, kind],
                    device_id=to, device_id_type=pl.DeviceIdType.MESH,
                ))
        return copies

    def tile_step(self, block):
        self.tile_copy(block).wait_recv()
        r = self.pieces[R0]
        mine = pl.ds(pl.multiple_of((4 * self.core + block) * r.size, r.size), r.size)
        self.add(r.whole.at[:, mine], r.whole_r1.at[:, r.size * block:r.size * (block + 1)])
        first0, second0, first1, second1 = self.tile_parts(block)

        @pl.when(self.x != block % 2)
        def _():
            first0.start()
            first1.start()

        @pl.when(self.y != block // 2)
        def _():
            second0.start()
            second1.start()

    def add(self, into, other):
        into[...] = (into[...].astype(F32) + other[...].astype(F32)).astype(BF16)

    def step(self, name, number, l):
        piece = self.pieces[name]
        grad, r1, r2, r3, rz = piece.grad, piece.r1, piece.r2, piece.r3[l], piece.rz
        mine = 4 * self.core
        own = mine + 2 * self.y + self.x
        tiles = name in (R0, R1)
        if number == 1:
            self.copy(name, 0, l).start()
        elif number == 2 and tiles:
            if name == R0:
                self.tile_step(3)
        elif number == 2:
            self.copy(name, 0, l).wait_recv()
            self.add(self.view(piece, grad, mine, 4), self.view(piece, r1, 0, 4))
            for kind in (1, 2, 3):
                self.copy(name, kind, l).start()
        elif number == 3:
            for kind in (1, 2):
                self.copy(name, kind, l).wait_recv()
                self.add(self.view(piece, grad, mine + 2 * (kind - 1) + self.x, 1, 0), self.view(piece, r2, kind - 1, 1, 0))
            if tiles:
                for i in range(2):
                    self.half_block(name, i).wait_recv()
            else:
                self.copy(name, 3, l).wait_recv()
            self.add(self.view(piece, grad, mine + 2 * self.y, 2, 1), self.view(piece, r2, 0, 2, 1))
            self.copy(name, 4, l).start()
            self.copy(name, 5, l).start()
        elif number == 4:
            for half in (0, 1):
                self.copy(name, 4 + half, l).wait_recv()
                self.add(self.view(piece, r3, 0, 1, half), self.view(piece, grad, own, 1, half))

            @pl.when(self.outer)
            def _():
                self.copy(name, 6, l).start()

            if not tiles:
                self.copy(name, 0, l).wait_send()
            elif name == R0:
                for block in range(4):
                    self.tile_copy(block).wait_send()
            for kind in (1, 2, 4, 5):
                self.copy(name, kind, l).wait_send()
            if tiles:
                for i in range(2):
                    self.half_block(name, i).wait_send()
            else:
                self.copy(name, 3, l).wait_send()
        elif number == 5:

            @pl.when(self.inner)
            def _():
                self.copy(name, 6, l).wait_recv()
                self.add(r3, rz.at[0])
                self.copy(name, 7, l).start()
        elif number == 6:

            @pl.when(self.inner)
            def _():
                self.copy(name, 7, l).wait()
                self.add(r3, rz.at[1])
                self.copy(name, 8, l).start()
                self.local(piece, l).start()
        elif number == 7:

            @pl.when(self.outer)
            def _():
                self.copy(name, 6, l).wait_send()
                self.copy(name, 8, l).wait_recv()

            @pl.when(self.inner)
            def _():
                self.copy(name, 8, l).wait_send()
                self.local(piece, l).wait()

    def half_block(self, name, x):
        piece = self.pieces[name]
        view = self.view(piece, piece.r2, x, 1, 1)
        return pltpu.make_async_remote_copy(
            src_ref=view, dst_ref=view,
            send_sem=self.send_sem.at[piece.index, 3 + 7 * x], recv_sem=self.recv_sem.at[piece.index, 3 + 7 * x],
            device_id={DP: self.links.y_n}, device_id_type=pl.DeviceIdType.MESH,
        )

    def local(self, piece, l):
        return pltpu.make_async_copy(piece.r3[l], piece.out(l), self.send_sem.at[piece.index, 9])


class Piece:
    def __init__(self, index, refs, size, across, split, out, by_columns=False, whole=None):
        self.index, self.size, self.across, self.split, self.out, self.by_columns = index, size, across, split, out, by_columns
        self.grad, self.r1, self.r2, self.r3, self.rz = refs
        self.whole, self.whole_r1 = whole or (None, None)


def sum_pieces(refs, out_m, out_o, out_e, out_r, out_t):
    def part(n, index):
        views = [refs[name + n].at[index] for name in ("grad_", "r1", "r2")]
        views.append([refs["r3" + n].at[(l,) + index] for l in range(1 if n == "t" else LAYERS)])
        return views + [refs["rz" + n].at[(slice(None),) + index]]

    every = slice(None)
    pieces = {}
    for i in range(2):
        cols = slice(FF // 2 * i, FF // 2 * (i + 1))
        pieces[E0 + i] = Piece(E0 + i, part("e", (every, cols)), 64, FF // 2, FF // 4, lambda l, cols=cols: out_e.at[l, :, cols])
    for i in range(2):
        rows = slice(D // 2 * i, D // 2 * (i + 1))
        pieces[R0 + i] = Piece(
            R0 + i, part("r", (rows, every)), 256, D // 2, D // 4, lambda l, rows=rows: out_r.at[l, rows], True,
            (refs["grad_r"], refs["r1r"]),
        )
    for i in range(4):
        cols = slice(384 * i, 384 * (i + 1))
        pieces[M0 + i] = Piece(
            M0 + i, part("m", (every, cols)), 64, 384, 128 * (1 + i % 2), lambda l, i=i: out_m.at[l, i]
        )
    pieces[O] = Piece(O, part("o", (every, every)), 64, D, D // 2, lambda l: out_o.at[l])
    pieces[T] = Piece(T, part("t", (every, every)), 64, 384, 128, lambda l: out_t)
    return pieces


def by_position(rows):
    size = rows.shape[0] // 8
    return jnp.concatenate([rows[size * i:size * (i + 1)] for i in (0, 2, 4, 6, 1, 3, 5, 7)], axis=0)


def step_kernel(linked, *refs):
    names = (LINKED_IN + LINKED_OUT) if linked else (PLAIN_IN + PLAIN_OUT)
    names += tuple(SCRATCH) + tuple(LINKED_SCRATCH if linked else PLAIN_SCRATCH)
    step_body(linked, **dict(zip(names, refs, strict=True)))


def step_body(
    linked, loss, lg, kept_m, kept_near, x, x1, dx, keys, values, pT, inv1s, cum, oT, hT, g, gT, wide, a1k, m, near, keep_sem, d, ds, doT, dpT, yb, acc,
    columns=None, table=None, gm=None, gf=None, gz=None, wm=None, wo=None, we=None, wr=None, stage=None, stage_half=None, sem=None, sem_half=None,
    dtable=None, dgm=None, dgf=None, dgz=None, dwm=None, dwo=None, dwe=None, dwrt=None,
    tokens=None, mask=None, emb=None, mgain=None, fgain=None, zgain=None, wm_s=None, wo_s=None, we_s=None, wr_s=None, tz=None, gains=None, lgs=None, losss=None,
    send_sem=None, recv_sem=None, zsend=None, zrecv=None, load_sem=None, sum_send=None, sum_recv=None, tile_send=None, tile_recv=None,
    out_m=None, out_o=None, out_e=None, out_r=None, out_t=None, dgains=None, **sums_refs,
):
    table_ref = table
    gm_ref, gf_ref, gz_ref = gm, gf, gz
    wm_ref, wo_ref, we_ref, wr_ref = wm, wo, we, wr
    loss_ref, lg_ref, dtable_ref, dgm_ref, dgf_ref, dgz_ref = loss, lg, dtable, dgm, dgf, dgz
    dwm_ref, dwo_ref, dwe_ref, dwrt_ref = dwm, dwo, dwe, dwrt
    x_ref, x1_ref, dx_ref, pT_ref, inv1_ref, cum_ref = x, x1, dx, pT, inv1s, cum
    oT_ref, hT_ref, g_ref, gT_ref, wide_ref, a1k_ref, near_ref, m_ref, d_ref, ds_ref = oT, hT, g, gT, wide, a1k, near, m, d, ds
    doT_ref, dpT_ref, w_ref, yb_ref, acc_ref = doT, dpT, a1k, yb, acc
    xs = [x_ref.at[0], x_ref.at[1], dx_ref]
    placed = by_position if linked else (lambda rows: rows)
    r, c = iotas(2 * CH, 2 * CH)
    upper = (r <= c).astype(F32).astype(BF16)

    if linked:
        zi = lax.axis_index(SECTION)
        links = Links(
            [(table_ref, 64, 384, 256, False)]
            + [
                entry
                for l in range(LAYERS)
                for entry in (
                    (wm_ref.at[l], 64, 3 * D, 3 * D // 2, SHARED[l][0]),
                    (wo_ref.at[l], 64, D, D // 2, SHARED[l][1]),
                    (we_ref.at[l], 64, FF, FF // 2, SHARED[l][2]),
                    (wr_ref.at[l], 256, D, D // 2, SHARED[l][3]),
                )
            ],
            send_sem, recv_sem,
        )

        def along_z(n, k, src_of, dst):
            target = (zi + k) % 4
            return pltpu.make_async_remote_copy(
                src_ref=src_of(target), dst_ref=dst.at[zi], send_sem=zsend.at[n, k - 1], recv_sem=zrecv.at[n, k - 1],
                device_id={SECTION: target}, device_id_type=pl.DeviceIdType.MESH,
            )

        def table_copy(k):
            return along_z(0, k, lambda target: tz.at[zi], tz)

        def lg_copy(k):
            return along_z(1, k, lambda target: lgs.at[target], lg_ref)

        def loss_copy(k):
            return along_z(2, k, lambda target: losss, loss_ref)

        loads = []
        for l in range(LAYERS):
            pairs = [(wm_s.at[l, :, TILE * j:TILE * (j + 1)], x1_ref.at[l, 64 * j:64 * (j + 1)]) for j in range(3)]
            pairs += [(wo_s.at[l], x1_ref.at[l, 192:256])]
            pairs += [(we_s.at[l, :, TILE * j:TILE * (j + 1)], x1_ref.at[l, 256 + 64 * j:320 + 64 * j]) for j in range(4)]
            pairs += [(wr_s.at[l], x_ref.at[1, 256 * l:256 * (l + 1)])]
            loads.append([pltpu.make_async_copy(src, dst, load_sem.at[l, i]) for i, (src, dst) in enumerate(pairs)])
            for load in loads[l]:
                load.start()

        def take(l, part):
            for i in {"m": (0, 1, 2), "o": (3,), "e": (4, 5, 6, 7), "r": (8,)}[part]:
                loads[l][i].wait()
            if part == "m":
                for j in range(3):
                    wm_ref[l, own64, TILE * j:TILE * (j + 1)] = x1_ref[l, 64 * j:64 * (j + 1)].astype(BF16)
            elif part == "o":
                wo_ref[l, own64] = x1_ref[l, 192:256].astype(BF16)
            elif part == "e":
                for j in range(4):
                    we_ref[l, own64, TILE * j:TILE * (j + 1)] = x1_ref[l, 256 + 64 * j:320 + 64 * j].astype(BF16)
            else:
                wr_ref[l, own256] = x_ref[1, 256 * l:256 * (l + 1)].astype(BF16)

        barrier = pltpu.get_barrier_semaphore()
        for target in (links.core_n, links.x_n, links.y_n):
            pl.semaphore_signal(barrier, inc=1, device_id={DP: target}, device_id_type=pl.DeviceIdType.MESH)
        for k in (1, 2, 3):
            pl.semaphore_signal(barrier, inc=1, device_id={SECTION: (zi + k) % 4}, device_id_type=pl.DeviceIdType.MESH)
        pl.semaphore_wait(barrier, 6)

        own64 = pl.ds(pl.multiple_of(links.d * 64, 64), 64)
        own256 = pl.ds(pl.multiple_of(links.d * 256, 256), 256)
        r, _ = iotas(8, 64)
        rows = [mgain[0:1], mgain[1:2], fgain[0:1], fgain[1:2], zgain[0:1]]
        gathered = sum(jnp.where(r == i, row, 0.0) for i, row in enumerate(rows))
        gathered = jnp.concatenate([gathered, jnp.zeros((8, 64), F32)], axis=1)
        gathered = jnp.concatenate([gathered, jnp.zeros((120, 128), F32)], axis=0).T[:64]
        small_b = (jnp.concatenate([emb[...], jnp.zeros((64, 64), F32)], axis=1) + pltpu.roll(gathered, 64, 1)).astype(BF16)
        tz[zi] = small_b
        for k in (1, 2, 3):
            table_copy(k).start()
        take(0, "m")
        links.own(1)
        r, c = iotas(8, LEN)
        ids = tokens[pl.ds(zi, 1), :].astype(F32)
        scored = mask[pl.ds(zi, 1), :].astype(F32)
        rows = [ids, pltpu.roll(ids, LEN - 1, 1), pltpu.roll(scored, LEN - 1, 1)]
        rows = sum(jnp.where((r == i) & ((c < LEN - 1) | (r == 0)), row, 0.0) for i, row in enumerate(rows))
        columns[...] = rows.T.astype(jnp.int32)
        take(0, "o")
        for k in (1, 2, 3):
            table_copy(k).wait_recv()
        pad = jnp.zeros((64, 64), BF16)
        table_ref[own64, :] = jnp.concatenate([tz[i][:, :64] for i in range(4)] + [small_b[:, 64:], pad], axis=1)
        links.own(0, 2)
        take(0, "e")
        wide_ref[...] = upper
        links.first(1, 0)
        links.own(3)
        links.first(2)
        take(0, "r")
        links.own(4)
        for part in "moer":
            take(1, part)
        links.second(1, 0)
        links.ready(0)
        gains[...] = table_ref[:, 256:].astype(F32).T[:8]
        table_ref = table_ref.at[:, :256]
        gm_ref, gf_ref, gz_ref = [gains[i:i + 1] for i in range(2)], [gains[i:i + 1] for i in range(2, 4)], gains[4:5]
        sums = Sums(
            links, sum_pieces(sums_refs, out_m, out_o, out_e, out_r, out_t), sum_send, sum_recv, tile_send, tile_recv
        )
    else:
        wide_ref[...] = upper
        gm_ref, gf_ref, gz_ref = [gm_ref[i] for i in range(2)], [gf_ref[i] for i in range(2)], gz_ref[...]

    def service(step, index=None, only=lambda at: True):
        if not linked:
            return
        for at, acts in SERVICE.get(step, {}).items():
            if not only(at):
                continue

            def run(acts=acts):
                for act in acts:
                    if isinstance(act[0], int):
                        sums.step(*act)
                    elif act[0] is Sums.tile_step:
                        sums.tile_step(act[1])
                    else:
                        act[0](links, *act[1:])

            if at is None:
                run()
            else:
                pl.when(index == at)(run)

    inv2 = 1.0 / (lax.broadcasted_iota(jnp.int32, (1, LEN), 1).astype(F32) + 1.0)

    def emit(slot, wait_first, value, dst, pool=0):
        into, sems = (stage, sem) if pool == 0 else (stage_half, sem_half)

        def copy():
            return pltpu.make_async_copy(into.at[slot], dst, sems.at[slot])

        if wait_first is True:
            copy().wait()
        elif wait_first is not False:
            pl.when(wait_first)(lambda: copy().wait())
        into[slot] = value.astype(BF16)
        copy().start()

    def put_gain(row, value):
        if linked:
            dgains[row:row + 1] = value
        elif row < 2:
            dgm_ref[row] = value
        elif row < 4:
            dgf_ref[row - 2] = value
        else:
            dgz_ref[...] = value

    def by_rows(run, init=None):
        for i in range(CHUNKS):
            init = run(slice(i * CH, (i + 1) * CH), init)
        return init

    def normed_rows(src, gain, dst, dstT):
        def some(rows, carry):
            block = norm_forward(src[rows], gain).astype(BF16)
            dst[rows] = block
            dstT[:, rows] = placed(block.T)
            return carry

        by_rows(some, 0)

    def back_rows(src, gain, row):
        def some(rows, dgain):
            dv, dg = norm_backward(src[rows], gain, acc_ref[rows])
            dx_ref[rows] += dv
            return dgain + dg

        put_gain(row, by_rows(some, jnp.zeros((1, D), F32)))

    vocab_ids = lax.broadcasted_iota(jnp.int32, (LEN, VOCAB), 1)
    hot = (vocab_ids == columns[:, 0:1]).astype(F32).astype(BF16)
    x_ref[0] = mm_nt(hot, table_ref[...])
    if linked:
        links.ready(1)

    def keep(l, h, e):
        return (
            pltpu.make_async_copy(m_ref.at[e], kept_m.at[l, h], keep_sem.at[e, 0]),
            pltpu.make_async_copy(near_ref.at[e], kept_near.at[l, h], keep_sem.at[e, 1]),
        )

    def fetch(l, h, e):
        return (
            pltpu.make_async_copy(kept_m.at[l, h], m_ref.at[e], keep_sem.at[e, 0]),
            pltpu.make_async_copy(kept_near.at[l, h], near_ref.at[e], keep_sem.at[e, 1]),
        )

    m_ref[...] = jnp.zeros_like(m_ref)
    near_ref[...] = jnp.zeros_like(near_ref)

    def key_sums(l):
        a1k_ref[...] = feature_parts(pT_ref[l, D:2 * D, :].astype(F32))[0].astype(BF16)
        for t0, t1 in WIDE:
            total = mm(a1k_ref[:, t0:t1], wide_ref[:t1 - t0, :t1 - t0])
            cum_ref[:, t0:t1] = total if t0 == 0 else total + cum_ref[:, t0 - 1:t0]

    def attention_forward(l):
        normed_rows(x_ref.at[l], gm_ref[l], yb_ref, hT_ref.at[l])
        h = yb_ref[...]
        for j in range(3):
            part = mm(h, wm_ref[l, :, j * TILE:(j + 1) * TILE]).astype(BF16)
            if j == 1:
                keys[...] = part
            if j == 2:
                values[l] = part
            pT_ref[l, j * TILE:(j + 1) * TILE, :] = part.T
        service((MIXER, l))
        key_sums(l)

        def pair(p, carry):
            base = pl.multiple_of(p * CH, CH)
            for e in range(2):
                row = pl.multiple_of(base + e * HD, HD)
                if l == 0:
                    pl.when(p > 0)(lambda: every(keep(l, 0, e), WAIT))
                else:
                    for copy in keep(l, 0, e):
                        copy.wait()
                qT = pT_ref[l, pl.ds(row, HD), :]
                kT = pT_ref[l, pl.ds(pl.multiple_of(D + row, HD), HD), :]
                vT = pT_ref[l, pl.ds(pl.multiple_of(2 * D + row, HD), HD), :]
                first_k, _, second_k = feature_parts(kT.astype(F32))
                key_feat = jnp.concatenate([first_k.astype(BF16), second_k.astype(BF16)], axis=0).T
                first_q = feature_parts(qT.astype(F32))[0].astype(BF16).astype(F32)
                total = jnp.sum(first_q * cum_ref[pl.ds(row, HD), :], axis=0, keepdims=True)
                inv1 = 1.0 / (total + 1.0)
                inv1_ref[l, 2 * p + e] = inv1
                query_feat2 = query_features(qT, inv1, inv2)[3]
                key_feat2 = jnp.concatenate([key_feat, key_feat], axis=1)
                key_nat = keys[:, pl.ds(base, CH)]
                query_masked = masked_pair(qT, e)
                for t0, t1 in WIDE:
                    mixture = mixture_block(t0, t1, key_nat, key_feat2, query_masked, query_feat2, near_ref.at[e])
                    m_ref[e, :t1, t0:t1] = mixture
                    oT_ref[l, pl.ds(row, HD), t0:t1] = mm(vT[:, :t1], mixture).astype(BF16)
                for copy in keep(l, 2 * p + e, e):
                    copy.start()
                service((HEAD, l), 2 * p + e, lambda at: at % 2 == e)
            return carry

        lax.fori_loop(0, HEADS // 2, pair, 0)
        service((OUTPUT, l))
        o = oT_ref[l].T
        x1_ref[l] = x_ref[l] + mm(o, wo_ref[l])

    def feed_forward(l):
        normed_rows(x1_ref.at[l], gf_ref[l], g_ref, gT_ref.at[l])
        xs[l + 1][...] = x1_ref[l]
        service((FEED, l))

        def tile(j, carry):
            col = pl.multiple_of(j * TILE, TILE)
            active = gelu_parts(mm(g_ref[...], we_ref[l, :, pl.ds(col, TILE)]))[0].astype(BF16)
            service((GELU, l), j)
            xs[l + 1][...] += mm(active, wr_ref[l, pl.ds(col, TILE), :])
            service((FEED_TILE, l), j)
            return carry

        lax.fori_loop(0, FF // TILE, tile, 0)

    def head():
        zT_ref, grad_ref = doT_ref, yb_ref.at[:, :VOCAB]

        def some(rows, carry):
            dgain, cross_sum, val_sum = carry
            x = dx_ref[rows]
            z = norm_forward(x, gz_ref).astype(BF16)
            zT_ref[:, rows] = placed(z.T)
            logits = mm(z, table_ref[...])
            ids = lax.broadcasted_iota(jnp.int32, (CH, VOCAB), 1)
            tgt_hot = (ids == columns[rows, 1:2]).astype(F32)
            val = columns[rows, 2:3].astype(F32)
            peak = jnp.max(logits, axis=-1, keepdims=True)
            grown = jnp.exp(logits - peak)
            total = jnp.sum(grown, axis=-1, keepdims=True)
            lse = peak + jnp.log(total)
            picked = jnp.sum(logits * tgt_hot, axis=-1, keepdims=True)
            cross = (lse - picked) * val
            grad_b = ((grown / total - tgt_hot) * val).astype(BF16)
            grad_ref[rows, :] = grad_b
            if linked:
                grad_bT = grad_b.T
                for i in range(4):
                    lgs[i, :, rows] = grad_bT[64 * i:64 * i + 64]
            else:
                lg_ref[rows, :] = grad_b
            dv, dg = norm_backward(x, gz_ref, mm_nt(grad_b, table_ref[...]))
            dx_ref[rows] = dv
            return (
                dgain + dg,
                cross_sum + jnp.sum(cross, axis=0, keepdims=True),
                val_sum + jnp.sum(val, axis=0, keepdims=True),
            )

        nothing = jnp.zeros((1, 1), F32)
        dgain, cross_sum, val_sum = by_rows(some, (jnp.zeros((1, D), F32), nothing, nothing))
        put_gain(4, dgain)
        loss = jnp.broadcast_to(cross_sum / val_sum, (8, 128))
        if linked:
            losss[...] = loss
            for k in (1, 2, 3):
                lg_copy(k).start()
                loss_copy(k).start()
            pltpu.make_async_copy(lgs.at[zi], lg_ref.at[zi], zsend.at[1, 3]).start()
            pltpu.make_async_copy(losss, loss_ref.at[zi], zsend.at[2, 3]).start()
        else:
            loss_ref[...] = loss
        dtable_head = mm(zT_ref[...], grad_ref[...])
        if linked:
            sums_refs["grad_t"][:, :VOCAB] = dtable_head.astype(BF16)
        else:
            dtable_ref[...] = dtable_head

    def feed_backward(l):
        def some(rows, carry):
            yb = dx_ref[rows].astype(BF16)
            yb_ref[rows] = yb
            doT_ref[:, rows] = yb.T
            if l < LAYERS - 1:
                g_ref[rows] = norm_forward(x1_ref[l, rows], gf_ref[l]).astype(BF16)
            return carry

        by_rows(some, 0)
        acc_ref[...] = jnp.zeros_like(acc_ref)

        def tile(j, carry):
            col = pl.multiple_of(j * TILE, TILE)
            slot = lax.rem(j, 2)
            later = (j >= 2) if l == LAYERS - 1 else True
            value, slope = gelu_parts(mm(g_ref[...], we_ref[l, :, pl.ds(col, TILE)]))
            dreduce = mm(doT_ref[...], value.astype(BF16))
            if linked:
                for i in range(2):
                    place = pl.multiple_of(BACK * j + FF // 2 * i, BACK)
                    sums_refs["grad_r"][:, pl.ds(place, BACK)] = dreduce[:, BACK * i:BACK * (i + 1)].astype(BF16)
                sums.tile_copy(j).start()
            else:
                emit(slot, later, dreduce, dwrt_ref.at[l, :, pl.ds(col, TILE)], 1)
            dact = mm_nt(yb_ref[...], wr_ref[l, pl.ds(col, TILE), :])
            dhid = (dact * slope).astype(BF16)
            dexpand = mm(gT_ref[l], dhid)
            if linked:
                sums_refs["grad_e"][:, pl.ds(col, TILE)] = dexpand.astype(BF16)
            else:
                emit(2 + slot, later, dexpand, dwe_ref.at[l, :, pl.ds(col, TILE)], 1)
            dnormed = mm_nt(dhid, we_ref[l, :, pl.ds(col, TILE)])

            acc_ref[...] += dnormed
            service((BACK_TILE, l), j)
            return carry

        lax.fori_loop(0, FF // TILE, tile, 0)
        service((BACK_FEED, l))
        back_rows(x1_ref.at[l], gf_ref[l], 2 + l)

    def attention_backward(l):
        if l < LAYERS - 1:
            key_sums(l)
        yb_ref[...] = dx_ref[...].astype(BF16)
        yb = yb_ref[...]
        doutput = mm(placed(oT_ref[l]), yb)
        if linked:
            sums_refs["grad_o"][...] = doutput.astype(BF16)
        else:
            emit(0, l < LAYERS - 1, doutput, dwo_ref.at[l])
        service((BACK_OUTPUT, l))
        doT_ref[...] = mm_nt(yb, wo_ref[l]).astype(BF16).T

        for e in range(2):
            for copy in fetch(l, e, e):
                copy.start()

        def pair(p, carry):
            base = pl.multiple_of(p * CH, CH)
            for e in range(2):
                row = pl.multiple_of(base + e * HD, HD)
                qT = pT_ref[l, pl.ds(row, HD), :]
                kT = pT_ref[l, pl.ds(pl.multiple_of(D + row, HD), HD), :]
                doT = doT_ref[pl.ds(row, HD), :]
                inv1 = inv1_ref[l, 2 * p + e]
                first_q, slope1_q, second_q, query_feat2 = query_features(qT, inv1, inv2)
                first_k, slope1_k, second_k = feature_parts(kT.astype(F32))
                key_featT = jnp.concatenate([first_k.astype(BF16), second_k.astype(BF16)], axis=0)
                value_nat = values[l, :, pl.ds(base, CH)]
                do_masked = masked_pair(doT, e)
                for copy in fetch(l, 2 * p + e, e):
                    copy.wait()
                far_q, near_q = [], []
                for t0, t1 in WIDE:
                    dm = mm(value_nat[:t1], do_masked[:, t0:t1])

                    def half(i):
                        r0, end = first_row(i), (i + 1) * CH
                        column = dm[:end, i * CH - t0:end - t0]
                        bottom = column[r0:]
                        near = near_ref[e, i, :end - r0, :]
                        weighted = near * bottom
                        dsum = jnp.sum(weighted, axis=0, keepdims=True)
                        ds = ((weighted - near * dsum) * 0.125).astype(BF16)
                        if i > 0:
                            before = jnp.concatenate([jnp.zeros((CH - REACH, CH), BF16), ds[:REACH]], axis=0)
                            ds_ref[end - 2 * CH:end - CH, CH:] = before
                            ds = ds[REACH:]
                            near_q.append(mm(kT[:, end - 2 * CH:end], jnp.concatenate([before, ds], axis=0)))
                        else:
                            near_q.append(mm(kT[:, :end], ds))
                        ds_ref[end - CH:end, :CH] = ds
                        lower = causal_rows(i, bottom).astype(BF16)
                        if r0 == 0:
                            return lower
                        return jnp.concatenate([column[:r0].astype(BF16), lower], axis=0)

                    dm_b = halves(t0, t1, half)
                    d_ref[:t1, t0:t1] = dm_b
                    far_q.append(mm(key_featT[:, :t1], dm_b))
                farT = jnp.concatenate(far_q, axis=1)
                y1, y2 = farT[:HD], farT[HD:]
                first_qf = first_q.astype(F32)
                m = inv1 * jnp.sum(first_qf * y1, axis=0, keepdims=True)
                cum = cum_ref[pl.ds(row, HD), :]
                dq = jnp.concatenate(near_q, axis=1)
                dq = dq + (inv1 * (y1 - m * cum)) * slope1_q + (inv2 * y2) * (1.0 - second_q * second_q)
                dpT_ref[pl.ds(row, HD), :] = dq.astype(BF16)
                w_ref[pl.ds(row, HD), :] = (first_qf * (m * inv1)).astype(BF16)
                after = 0.0
                for t0, t1 in reversed(WIDE):
                    far = mm_nt(query_feat2[:CH, t0:], d_ref[t0:t1, t0:])
                    back = mm_nt(w_ref[pl.ds(row, HD), t0:t1], wide_ref[:t1 - t0, :t1 - t0]) + after
                    after = back[:, :1]
                    near_k = []
                    for u0 in range(t0, t1, CH):
                        u2 = min(u0 + 2 * CH, LEN)
                        near_k.append(mm_nt(qT[:, u0:u2], ds_ref[u0:u0 + CH, :u2 - u0]))
                    near = near_k[0] if len(near_k) == 1 else jnp.concatenate(near_k, axis=1)
                    dk = near + (far[:HD] - back) * slope1_k[:, t0:t1]
                    dk = dk + far[HD:] * (1.0 - second_k[:, t0:t1] * second_k[:, t0:t1])
                    dpT_ref[pl.ds(pl.multiple_of(D + row, HD), HD), t0:t1] = dk.astype(BF16)
                    dv = mm_nt(doT[:, t0:], m_ref[e, t0:t1, t0:])
                    dpT_ref[pl.ds(pl.multiple_of(2 * D + row, HD), HD), t0:t1] = dv.astype(BF16)
                pl.when(p < HEADS // 2 - 1)(lambda: every(fetch(l, 2 * p + e + 2, e), START))
                service((BACK_HEAD, l), 2 * p + e, lambda at: at % 2 == e)
            if linked:
                for j in range(3):
                    block = mm_nt(hT_ref[l], dpT_ref[pl.ds(pl.multiple_of(j * D + base, CH), CH), :])
                    place = pl.multiple_of(3 * base + j * CH, CH)
                    sums_refs["grad_m"][:, pl.ds(place, CH)] = block.astype(BF16)
                service((BACK_PAIR, l), p)
            return carry

        lax.fori_loop(0, HEADS // 2, pair, 0)
        if not linked:
            for j in range(3):
                block = mm_nt(hT_ref[l], dpT_ref[j * TILE:(j + 1) * TILE, :])
                emit(1 + j, l < LAYERS - 1, block, dwm_ref.at[l, :, j * TILE:(j + 1) * TILE])
        for t0 in range(0, LEN, 256):
            t1 = min(t0 + 256, LEN)
            acc_ref[t0:t1] = mm(wm_ref[l], dpT_ref[:, t0:t1]).T
        service((BACK_MIXER, l))
        back_rows(x_ref.at[l], gm_ref[l], l)
        service((BACK_LAYER, l))

    for l in range(LAYERS):
        service((LAYER, l))
        attention_forward(l)
        feed_forward(l)
    for e in range(2):
        for copy in keep(0, 0, e):
            copy.wait()
    head()
    for l in reversed(range(LAYERS)):
        feed_backward(l)
        attention_backward(l)
    dtable_head = sums_refs["grad_t"][:, :VOCAB].astype(F32) if linked else dtable_ref[...]
    dtable_sum = dtable_head + mm(placed(dx_ref[...].astype(BF16).T), hot)
    if linked:
        sums_refs["grad_t"][:, :VOCAB] = dtable_sum.astype(BF16)
        sums_refs["grad_t"][:, VOCAB:] = placed(jnp.concatenate([dgains[...], jnp.zeros((120, D), F32)], axis=0).T).astype(BF16)
        service((END, 0))
        for k in (1, 2, 3):
            table_copy(k).wait_send()
            lg_copy(k).wait()
            loss_copy(k).wait()
        pltpu.make_async_copy(lgs.at[zi], lg_ref.at[zi], zsend.at[1, 3]).wait()
        pltpu.make_async_copy(losss, loss_ref.at[zi], zsend.at[2, 3]).wait()
        links.finish()
    else:
        dtable_ref[...] = dtable_sum
        for slot in range(4):
            pltpu.make_async_copy(stage.at[slot], dwo_ref.at[0], sem.at[slot]).wait()
            pltpu.make_async_copy(stage_half.at[slot], dwe_ref.at[0, :, :TILE], sem_half.at[slot]).wait()


E0, E1, R0, R1, M0, M1, M2, M3, O, T = range(10)
MIXER, HEAD, FEED, GELU, FEED_TILE, LAYER, BACK_TILE, BACK_FEED, BACK_OUTPUT, BACK_HEAD, BACK_PAIR, BACK_MIXER, BACK_LAYER, END, OUTPUT = range(15)
SHARED = ((False, False, True, False), (False, False, True, False))
SERVICE = {
    (MIXER, 0): {
        None: ((Links.second, 2), (Links.first, 3), (Links.own, 5),),
    },
    (HEAD, 0): {
        3: ((Links.first, 4),),
        4: ((Links.second, 3),),
        5: ((Links.own, 6),),
        7: ((Links.own, 7),),
    },
    (OUTPUT, 0): {
        None: ((Links.ready, 2),),
    },
    (FEED, 0): {
        None: ((Links.first, 5), (Links.third, 3), (Links.ready, 3),),
    },
    (GELU, 0): {
        0: ((Links.second, 4), (Links.ready, 4),),
    },
    (FEED_TILE, 0): {
        0: ((Links.first, 6), (Links.own, 8),),
        1: ((Links.first, 7),),
        3: ((Links.second, 5),),
    },
    (LAYER, 1): {
        None: ((Links.ready, 5),),
    },
    (MIXER, 1): {
        None: ((Links.second, 6),),
    },
    (HEAD, 1): {
        1: ((Links.first, 8),),
        2: ((Links.second, 7),),
        6: ((Links.second, 8),),
        7: ((Links.third, 7),),
    },
    (OUTPUT, 1): {
        None: ((Links.ready, 6),),
    },
    (FEED, 1): {
        None: ((Links.ready, 7),),
    },
    (GELU, 1): {
        0: ((Links.ready, 8),),
    },
    (BACK_TILE, 1): {
        1: ((E0, 1, 1), (Sums.tile_step, 0),),
        2: ((Sums.tile_step, 1), (E0, 2, 1),),
        3: ((Sums.tile_step, 2),),
    },
    (BACK_FEED, 1): {
        None: ((E1, 1, 1),),
    },
    (BACK_OUTPUT, 1): {
        None: ((O, 1, 1),),
    },
    (BACK_HEAD, 1): {
        0: ((E1, 2, 1), (R0, 2, 1), (R1, 2, 1), (O, 2, 1),),
        1: ((E0, 3, 1),),
        2: ((M0, 2, 1),),
        3: ((E1, 3, 1),),
        4: ((R0, 3, 1), (R1, 3, 1), (M1, 2, 1),),
        5: ((E0, 4, 1), (O, 3, 1),),
        6: ((M0, 3, 1), (M2, 2, 1), (E1, 4, 1),),
        7: ((R0, 4, 1),),
    },
    (BACK_PAIR, 1): {
        0: ((M0, 1, 1),),
        1: ((M1, 1, 1),),
        2: ((M2, 1, 1),),
        3: ((M3, 1, 1),),
    },
    (BACK_MIXER, 1): {
        None: ((E0, 5, 1), (R1, 4, 1), (M3, 2, 1),),
    },
    (BACK_LAYER, 1): {
        None: ((M1, 3, 1),),
    },
    (BACK_TILE, 0): {
        0: ((E1, 5, 1), (M0, 4, 1), (O, 4, 1), (M2, 3, 1), (M1, 4, 1), (M3, 3, 1),),
        1: ((E0, 1, 0), (Sums.tile_step, 0), (E0, 6, 1), (R0, 5, 1),),
        2: ((Sums.tile_step, 1), (E1, 6, 1), (R1, 5, 1), (M0, 5, 1), (M2, 4, 1), (M3, 4, 1), (E0, 2, 0),),
        3: ((Sums.tile_step, 2), (R0, 6, 1), (M1, 5, 1), (O, 5, 1),),
    },
    (BACK_FEED, 0): {
        None: ((E1, 1, 0),),
    },
    (BACK_OUTPUT, 0): {
        None: ((O, 1, 0), (M2, 5, 1), (M3, 5, 1), (E0, 7, 1),),
    },
    (BACK_HEAD, 0): {
        0: ((R1, 6, 1), (E1, 7, 1), (E1, 2, 0), (M0, 6, 1), (R0, 2, 0), (R1, 2, 0), (O, 2, 0),),
        1: ((M1, 6, 1), (E0, 3, 0),),
        2: ((M2, 6, 1), (R0, 7, 1), (M0, 2, 0),),
        3: ((M3, 6, 1), (E1, 3, 0),),
        4: ((R1, 7, 1), (M0, 7, 1), (R0, 3, 0), (R1, 3, 0), (M1, 2, 0),),
        5: ((M1, 7, 1), (E0, 4, 0), (O, 7, 1), (O, 3, 0),),
        6: ((M2, 7, 1), (M3, 7, 1), (M0, 3, 0), (E1, 4, 0), (M2, 2, 0),),
        7: ((E0, 5, 0), (R0, 4, 0),),
    },
    (BACK_PAIR, 0): {
        0: ((M0, 1, 0), (O, 6, 1),),
        1: ((M1, 1, 0),),
        2: ((M2, 1, 0),),
        3: ((M3, 1, 0),),
    },
    (BACK_MIXER, 0): {
        None: ((R1, 4, 0), (M3, 2, 0),),
    },
    (BACK_LAYER, 0): {
        None: ((E1, 5, 0), (M1, 3, 0), (O, 4, 0),),
    },
    (END, 0): {
        None: (
            (T, 1, 0), (M0, 4, 0), (M2, 3, 0), (T, 2, 0), (E0, 6, 0), (M3, 3, 0), (R0, 5, 0), (M1, 4, 0), (M2, 4, 0),
            (E1, 6, 0), (R1, 5, 0), (T, 3, 0), (M3, 4, 0), (O, 5, 0), (M0, 5, 0), (R0, 6, 0), (T, 4, 0), (M1, 5, 0), (M2, 5, 0),
            (R1, 6, 0), (M3, 5, 0), (T, 5, 0), (O, 6, 0), (M0, 6, 0), (M1, 6, 0), (M2, 6, 0), (M3, 6, 0), (T, 6, 0), (E0, 7, 0),
            (E1, 7, 0), (R0, 7, 0), (R1, 7, 0), (O, 7, 0), (M0, 7, 0), (M1, 7, 0), (M2, 7, 0), (M3, 7, 0), (T, 7, 0),
        ),
    },
}

PLAIN_IN = ("columns", "table", "gm", "gf", "gz", "wm", "wo", "we", "wr")
PLAIN_OUT = ("loss", "lg", "kept_m", "kept_near", "dtable", "dgm", "dgf", "dgz", "dwm", "dwo", "dwe", "dwrt")
LINKED_IN = ("tokens", "mask", "emb", "mgain", "fgain", "zgain", "wm_s", "wo_s", "we_s", "wr_s")
LINKED_OUT = ("loss", "lg", "kept_m", "kept_near", "out_m", "out_o", "out_e", "out_r", "out_t")
SCRATCH = dict(
    x=pltpu.VMEM((LAYERS, LEN, D), F32),
    x1=pltpu.VMEM((LAYERS, LEN, D), F32),
    dx=pltpu.VMEM((LEN, D), F32),
    keys=pltpu.VMEM((LEN, D), BF16),
    values=pltpu.VMEM((LAYERS, LEN, D), BF16),
    pT=pltpu.VMEM((LAYERS, 3 * D, LEN), BF16),
    inv1s=pltpu.VMEM((LAYERS, HEADS, 1, LEN), F32),
    cum=pltpu.VMEM((D, LEN), F32),
    oT=pltpu.VMEM((LAYERS, D, LEN), BF16),
    hT=pltpu.VMEM((LAYERS, D, LEN), BF16),
    g=pltpu.VMEM((LEN, D), BF16),
    gT=pltpu.VMEM((LAYERS, D, LEN), BF16),
    wide=pltpu.VMEM((2 * CH, 2 * CH), BF16),
    a1k=pltpu.VMEM((D, LEN), BF16),
    m=pltpu.VMEM((2, LEN, LEN), BF16),
    near=pltpu.VMEM((2, CHUNKS, CH + REACH, CH), F32),
    keep_sem=pltpu.SemaphoreType.DMA((2, 2)),
    d=pltpu.VMEM((LEN, LEN), BF16),
    ds=pltpu.VMEM((LEN, 2 * CH), BF16),
    doT=pltpu.VMEM((D, LEN), BF16),
    dpT=pltpu.VMEM((3 * D, LEN), BF16),
    yb=pltpu.VMEM((LEN, D), BF16),
    acc=pltpu.VMEM((LEN, D), F32),
)
PLAIN_SCRATCH = dict(
    stage=pltpu.VMEM((4, D, TILE), BF16),
    stage_half=pltpu.VMEM((4, D, TILE), BF16),
    sem=pltpu.SemaphoreType.DMA((4,)),
    sem_half=pltpu.SemaphoreType.DMA((4,)),
)


def sum_buffers(n, rows, cols, along):
    def shape(blocks):
        return (rows * blocks // 8, cols) if along == 0 else (rows, cols * blocks // 8)

    return {
        "grad_" + n: pltpu.VMEM((rows, cols), BF16),
        "r1" + n: pltpu.VMEM(shape(4), BF16),
        "r2" + n: pltpu.VMEM(shape(2), BF16),
        "r3" + n: pltpu.VMEM((1 if n == "t" else LAYERS,) + shape(1), BF16),
        "rz" + n: pltpu.VMEM((2,) + shape(1), BF16),
    }


LINKED_SCRATCH = dict(
    table=pltpu.VMEM((D, 384), BF16),
    wm=pltpu.VMEM((LAYERS, D, 3 * D), BF16),
    wo=pltpu.VMEM((LAYERS, D, D), BF16),
    we=pltpu.VMEM((LAYERS, D, FF), BF16),
    wr=pltpu.VMEM((LAYERS, FF, D), BF16),
    columns=pltpu.VMEM((LEN, 8), jnp.int32),
    tz=pltpu.VMEM((4, 64, 128), BF16),
    gains=pltpu.VMEM((8, D), F32),
    lgs=pltpu.VMEM((4, 64, LEN), BF16),
    losss=pltpu.VMEM((8, 128), F32),
    send_sem=pltpu.SemaphoreType.DMA((9, 15)),
    recv_sem=pltpu.SemaphoreType.DMA((9, 15)),
    zsend=pltpu.SemaphoreType.DMA((3, 4)),
    zrecv=pltpu.SemaphoreType.DMA((3, 4)),
    load_sem=pltpu.SemaphoreType.DMA((LAYERS, 9)),
    sum_send=pltpu.SemaphoreType.DMA((10, 11)),
    sum_recv=pltpu.SemaphoreType.DMA((10, 11)),
    tile_send=pltpu.SemaphoreType.DMA((4,)),
    tile_recv=pltpu.SemaphoreType.DMA((4,)),
    dgains=pltpu.VMEM((8, D), F32),
    **sum_buffers("m", D, 3 * D, 0),
    **sum_buffers("o", D, D, 0),
    **sum_buffers("e", D, FF, 0),
    **sum_buffers("r", D, FF, 1),
    **sum_buffers("t", D, 384, 0),
)


def local_step(linked, *operands):
    vmem = pl.BlockSpec(memory_space=pltpu.VMEM)
    hbm = pl.BlockSpec(memory_space=pl.ANY)
    shape = jax.ShapeDtypeStruct
    kept = (shape((LAYERS, HEADS, LEN, LEN), BF16), shape((LAYERS, HEADS, CHUNKS, CH + REACH, CH), F32))
    if linked:
        scratch = dict(SCRATCH, **LINKED_SCRATCH)
        in_specs = [vmem] * 6 + [hbm] * 4
        out_shape = (
            shape((4, 8, 128), F32),
            shape((4, 64, LEN), BF16),
            *kept,
            shape((LAYERS, 4, 64, 384), BF16),
            shape((LAYERS, 64, D), BF16),
            shape((LAYERS, 64, FF), BF16),
            shape((LAYERS, D, 256), BF16),
            shape((64, 384), BF16),
        )
        out_specs = (hbm,) * 9
    else:
        scratch = dict(SCRATCH, **PLAIN_SCRATCH)
        in_specs = [vmem] * len(operands)
        out_shape = (
            shape((8, 128), F32),
            shape((LEN, VOCAB), BF16),
            *kept,
            shape((D, VOCAB), F32),
            shape((LAYERS, 1, D), F32),
            shape((LAYERS, 1, D), F32),
            shape((1, D), F32),
            shape((LAYERS, D, 3 * D), BF16),
            shape((LAYERS, D, D), BF16),
            shape((LAYERS, D, FF), BF16),
            shape((LAYERS, D, FF), BF16),
        )
        out_specs = (vmem,) * 2 + (hbm,) * 2 + (vmem,) * 4 + (hbm,) * 4
    return pl.pallas_call(
        functools.partial(step_kernel, linked),
        out_shape=out_shape,
        in_specs=in_specs,
        out_specs=out_specs,
        scratch_shapes=list(scratch.values()),
        compiler_params=pltpu.CompilerParams(
            vmem_limit_bytes=64 * 1024 * 1024,
            collective_id=0 if linked else None,
            has_side_effects=linked,
        ),
        cost_estimate=pl.CostEstimate(flops=40_000_000_000, bytes_accessed=40_000_000, transcendentals=0),
        name="local_step",
    )(*operands)


def finish_kernel(
    loss_in, lg_in, dwm_in, dwo_in, dwe_in, dwrt_in, last_in,
    out_loss, out_lg, out_table, out_m, out_o, out_mgain, out_e, out_r, out_fgain, out_zgain,
    loss, lg, dwm, dwo, dwe, dwrt, last, sem,
):
    pairs = ((loss_in, loss), (lg_in, lg), (dwm_in, dwm), (dwo_in, dwo), (dwe_in, dwe), (dwrt_in, dwrt), (last_in, last))
    copies = [pltpu.make_async_copy(src, dst, sem.at[i]) for i, (src, dst) in enumerate(pairs)]
    every(copies, START)
    every(copies, WAIT)
    z = lax.axis_index(SECTION)
    r, c = iotas(4, 128)
    out_loss[...] = jnp.sum(jnp.where(r == c, loss[:, 0, :], 0.0), axis=0, keepdims=True)
    out_lg[...] = lg[...].astype(F32)
    table = last[:, :VOCAB].astype(F32)
    out_table[...] = sum(jnp.where(z == i, table[:, 64 * i:64 * (i + 1)], 0.0) for i in range(4))
    gains = last[:, VOCAB:].astype(F32)
    gains = jnp.concatenate([gains, jnp.zeros((64, 128), F32)], axis=0).T
    out_mgain[...] = gains[0:2, :64]
    out_fgain[...] = gains[2:4, :64]
    out_zgain[...] = gains[4:5, :64]
    out_o[...] = dwo[...].astype(F32)
    out_e[...] = dwe[...].astype(F32)
    for l in range(LAYERS):
        out_r[l] = dwrt[l].astype(F32).T
        for p in range(4):
            for j in range(3):
                out_m[l, :, D * j + CH * p:D * j + CH * (p + 1)] = dwm[l, p, :, CH * j:CH * (j + 1)].astype(F32)


def finish(*operands):
    vmem = pl.BlockSpec(memory_space=pltpu.VMEM)
    shapes = (
        (1, 128), (4, 64, LEN), (64, 64), (LAYERS, 64, 3 * D), (LAYERS, 64, D), (LAYERS, 64), (LAYERS, 64, FF),
        (LAYERS, 256, D), (LAYERS, 64), (1, 64),
    )
    return pl.pallas_call(
        finish_kernel,
        out_shape=tuple(jax.ShapeDtypeStruct(shape, F32) for shape in shapes),
        in_specs=[pl.BlockSpec(memory_space=pl.ANY)] * len(operands),
        out_specs=(vmem,) * len(shapes),
        scratch_shapes=[pltpu.VMEM(operand.shape, operand.dtype) for operand in operands]
        + [pltpu.SemaphoreType.DMA((len(operands),))],
        compiler_params=pltpu.CompilerParams(vmem_limit_bytes=60 * 1024 * 1024),
        name="finish",
    )(*operands)


def body(
    tokens,
    padding_mask,
    embedding,
    mixer_weight,
    output_weight,
    mixer_gain,
    expand_weight,
    reduce_weight,
    feed_gain,
    final_gain,
):
    segments = lax.axis_size(SECTION)
    segment_index = lax.axis_index(SECTION)
    item_count = tokens.shape[0]
    assert item_count == segments
    slice_width = embedding.shape[1]

    if segments == 4 and lax.axis_size(DP) == 8:
        loss, lg, _, _, dwm, dwo, dwe, dwrt, last = local_step(
            True, tokens, padding_mask, embedding, mixer_gain, feed_gain, final_gain[None],
            mixer_weight, output_weight, expand_weight, reduce_weight,
        )
        loss, lg, table_grad, dwm, dwo, mixer_gain_grad, dwe, dwr, feed_gain_grad, final_gain_grad = finish(
            loss, lg, dwm, dwo, dwe, dwrt, last
        )
        return (
            loss[0, :4], jnp.swapaxes(lg, 1, 2), table_grad, dwm, dwo, mixer_gain_grad, dwe, dwr, feed_gain_grad, final_gain_grad[0]
        )

    token_row = lax.dynamic_index_in_dim(tokens, segment_index, 0, keepdims=False)
    mask_row = lax.dynamic_index_in_dim(padding_mask, segment_index, 0, keepdims=False)
    zero = jnp.zeros((1,), jnp.int32)
    columns = jnp.stack(
        [token_row, jnp.concatenate([token_row[1:], zero]), jnp.concatenate([mask_row[1:], zero])], axis=1
    )

    def gather(block, dim):
        return lax.all_gather(block.astype(BF16), DP, axis=dim, tiled=True)

    table = lax.all_gather(gather(embedding, 0), SECTION, axis=1, tiled=True)
    gains = gather(jnp.concatenate([mixer_gain, feed_gain, final_gain[None]], axis=0), 1).astype(F32)
    loss, lg, _, _, dtable, dgm, dgf, dgz, dwm, dwo, dwe, dwrt = local_step(
        False, columns, table, gains[0:2, None], gains[2:4, None], gains[4:5],
        gather(mixer_weight, 1), gather(output_weight, 1), gather(expand_weight, 1), gather(reduce_weight, 1),
    )
    item_loss = lax.all_gather(loss[0, 0], SECTION)
    parts = lg.reshape(LEN, segments, slice_width).transpose(1, 0, 2)
    logit_grad = lax.all_to_all(parts, SECTION, 0, 0, tiled=True).astype(F32)

    def shard(grad, dim):
        part = lax.psum_scatter(grad.astype(BF16), DP, scatter_dimension=dim, tiled=True)
        return lax.psum(part, SECTION).astype(F32)

    table_part = lax.psum_scatter(dtable.astype(BF16), DP, scatter_dimension=0, tiled=True)
    table_grad = lax.psum_scatter(table_part, SECTION, scatter_dimension=1, tiled=True).astype(F32)
    gain_grads = lax.psum_scatter(
        jnp.concatenate([dgm[:, 0], dgf[:, 0], dgz], axis=0), DP, scatter_dimension=1, tiled=True
    )
    gain_grads = lax.psum(gain_grads, SECTION)
    return (
        item_loss,
        logit_grad,
        table_grad,
        shard(dwm, 1),
        shard(dwo, 1),
        gain_grads[0:2],
        shard(dwe, 1),
        jnp.swapaxes(shard(dwrt, 2), 1, 2),
        gain_grads[2:4],
        gain_grads[4],
    )


def solution(mesh):
    placed = (
        P(DP, None),
        P(DP, None),
        P(DP, SECTION),
        P(None, DP, None),
        P(None, DP, None),
        P(None, DP),
        P(None, DP, None),
        P(None, DP, None),
        P(None, DP),
        P(DP),
    )
    return jax.shard_map(
        body,
        mesh=mesh,
        in_specs=placed,
        out_specs=(
            P(DP),
            P(DP, None, SECTION),
            P(DP, SECTION),
            P(None, DP, None),
            P(None, DP, None),
            P(None, DP),
            P(None, DP, None),
            P(None, DP, None),
            P(None, DP),
            P(DP),
        ),
        check_vma=False,
    )
```

```python
import functools

import jax
import jax.numpy as jnp
from jax import lax
from jax.experimental import pallas as pl
from jax.experimental.pallas import tpu as pltpu
from jax.sharding import PartitionSpec as P

D = 512
HEADS = 8
HD = 64
FF = 2048
VOCAB = 256
BAND = 30
LEN = 640
LAYERS = 2
CH = 128
CHUNKS = LEN // CH
REACH = 32
WIDE = tuple((t0, min(t0 + 256, LEN)) for t0 in range(0, LEN, 256))
TILE = 512
BACK = 256
F32 = jnp.float32
DP, SECTION = ("dp", "section")
BF16 = jnp.bfloat16


def mm(left, right):
    return jnp.dot(left, right, preferred_element_type=F32)


def mm_nt(left, right):
    return lax.dot_general(left, right, (((1,), (1,)), ((), ())), preferred_element_type=F32)


def norm_forward(v, gain):
    scale = lax.rsqrt(jnp.mean(v * v, axis=-1, keepdims=True) + 1e-05)
    return v * scale * gain


def norm_backward(v, gain, dy):
    scale = lax.rsqrt(jnp.mean(v * v, axis=-1, keepdims=True) + 1e-05)
    normed = v * scale
    dgain = jnp.sum(dy * normed, axis=0, keepdims=True)
    dyg = dy * gain
    dv = scale * (dyg - normed * jnp.mean(dyg * normed, axis=-1, keepdims=True))
    return dv, dgain


def gelu_parts(u):
    c = 0.7978845608028654
    square = u * u
    t = jnp.tanh(u * (c + (c * 0.044715) * square))
    half = 0.5 * (1.0 + t)
    value = u * half
    slope = half + 0.5 * u * (1.0 - t * t) * (c + (3.0 * c * 0.044715) * square)
    return value, slope


def feature_parts(u):
    low_exp = jnp.exp(jnp.minimum(u, 0.0))
    first = jnp.where(u > 0.0, u + 1.0, low_exp)
    second = jnp.tanh(u)
    return first, low_exp, second


def iotas(rows, cols, row0=0):
    r = lax.broadcasted_iota(jnp.int32, (rows, cols), 0) + row0
    c = lax.broadcasted_iota(jnp.int32, (rows, cols), 1)
    return r, c


def near_part(i, key_rows, query_cols):
    row0 = -REACH if i > 0 else 0
    scores = mm(key_rows, query_cols) * 0.125
    r, c = iotas(CH - row0, CH, row0)
    ok = (r <= c) & (c - r < BAND)
    scores = jnp.where(ok, scores, -1e30)
    peak = jnp.max(scores, axis=0, keepdims=True)
    weights = jnp.exp(scores - peak)
    return weights / jnp.sum(weights, axis=0, keepdims=True)


def causal_rows(i, block):
    row0 = -REACH if i > 0 else 0
    r, c = iotas(CH - row0, CH, row0)
    return jnp.where(r <= c, block, 0.0)


START, WAIT = range(2)


def every(copies, act):
    for copy in copies:
        if act == START:
            copy.start()
        else:
            copy.wait()


def halves(t0, t1, half):
    parts = []
    for i in range(t0 // CH, t1 // CH):
        part = half(i)
        if part.shape[0] < t1:
            part = jnp.concatenate([part, jnp.zeros((t1 - part.shape[0], CH), part.dtype)], axis=0)
        parts.append(part)
    return parts[0] if len(parts) == 1 else jnp.concatenate(parts, axis=1)


def first_row(i):
    return i * CH - REACH if i > 0 else 0


def mixture_block(t0, t1, key_nat, key_feat2, query_masked, query_feat2, near_ref):
    far = mm(key_feat2[:t1], query_feat2[:, t0:t1])

    def half(i):
        r0, end = first_row(i), (i + 1) * CH
        near = near_part(i, key_nat[r0:end], query_masked[:, i * CH:end])
        near_ref[i, :end - r0, :] = near
        column = far[:end, i * CH - t0:end - t0]
        bottom = (causal_rows(i, column[r0:]) + near).astype(BF16)
        if r0 == 0:
            return bottom
        return jnp.concatenate([column[:r0].astype(BF16), bottom], axis=0)

    return halves(t0, t1, half)


def query_features(qT, inv1, inv2):
    first, slope1, second = feature_parts(qT.astype(F32))
    first_b, second_b = first.astype(BF16), second.astype(BF16)
    scaled = jnp.concatenate([first_b.astype(F32) * inv1, second_b.astype(F32) * inv2], axis=0)
    high = scaled.astype(BF16)
    rest = (scaled - high.astype(F32)).astype(BF16)
    return first_b, slope1, second, jnp.concatenate([high, rest], axis=0)


def masked_pair(part, e):
    zero = jnp.zeros_like(part)
    return jnp.concatenate([part, zero] if e == 0 else [zero, part], axis=0)


ALL, MINE, MINE_A, MINE_B, OTHER = range(5)


class Links:
    def __init__(self, pieces, send_sem, recv_sem):
        self.pieces, self.send_sem, self.recv_sem = pieces, send_sem, recv_sem
        d, z = lax.axis_index(DP), lax.axis_index(SECTION)
        core, x, y = d % 2, (d // 2) % 2, d // 4
        self.d, self.half = d, z % 2
        self.core_n, self.x_n, self.y_n, self.z_n = d + 1 - 2 * core, d + 2 - 4 * x, d + 4 - 8 * y, z + 1 - 2 * (z % 2)
        self.diag = self.x_n + 4 - 8 * y

    def columns(self, n, part):
        _, _, cols, cut, shared = self.pieces[n]
        if part == ALL or (part == MINE and not shared):
            return slice(None)
        if not shared:
            return slice(0, cut) if part == MINE_A else slice(cut, cols)
        half, quarter = cols // 2, cols // 4
        start = half * (1 - self.half if part == OTHER else self.half) + (quarter if part == MINE_B else 0)
        return pl.ds(pl.multiple_of(start, quarter), quarter if part in (MINE_A, MINE_B) else half)

    def copy(self, n, kind):
        ref, rows = self.pieces[n][:2]
        core, x, y, z = {DP: self.core_n}, {DP: self.x_n}, {DP: self.y_n}, {SECTION: self.z_n}
        block, part, target = (
            (self.d, MINE, x),
            (self.d, MINE, y),
            (self.y_n, MINE_A, x),
            (self.x_n, MINE_B, y),
            (self.d, ALL, core),
            (self.x_n, MINE, core),
            (self.y_n, MINE, core),
            (self.diag, MINE_A, core),
            (self.diag, MINE_B, core),
            (self.x_n, MINE, z),
            (self.y_n, MINE, z),
            (self.diag, MINE, z),
            (self.x_n, OTHER, core),
            (self.y_n, OTHER, core),
            (self.diag, OTHER, core),
        )[kind]
        view = ref.at[pl.ds(pl.multiple_of(block * rows, rows), rows), self.columns(n, part)]
        return pltpu.make_async_remote_copy(
            src_ref=view, dst_ref=view, send_sem=self.send_sem.at[n, kind], recv_sem=self.recv_sem.at[n, kind],
            device_id=target, device_id_type=pl.DeviceIdType.MESH,
        )

    def own(self, *ns):
        for n in ns:
            for kind in (0, 1, 4):
                self.copy(n, kind).start()

    def first(self, *ns):
        for n in ns:
            shared = self.pieces[n][4]
            self.copy(n, 0).wait_recv()
            self.copy(n, 3).start()
            self.copy(n, 1).wait_recv()
            self.copy(n, 2).start()
            for kind in (9, 10, 5, 6) if shared else (5, 6):
                self.copy(n, kind).start()

    def second(self, *ns):
        for n in ns:
            shared = self.pieces[n][4]
            self.copy(n, 2).wait_recv()
            self.copy(n, 7).start()
            self.copy(n, 3).wait_recv()
            for kind in (11, 8) if shared else (8,):
                self.copy(n, kind).start()

    def third(self, *ns):
        for n in ns:
            for kind in (9, 10, 11):
                self.copy(n, kind).wait_recv()
                self.copy(n, kind + 3).start()

    def ready(self, *ns):
        for n in ns:
            for kind in (4, 5, 6, 7, 8) + ((12, 13, 14) if self.pieces[n][4] else ()):
                self.copy(n, kind).wait_recv()

    def finish(self):
        for n, piece in enumerate(self.pieces):
            for kind in range(15 if piece[4] else 9):
                self.copy(n, kind).wait_send()


class Sums:
    def __init__(self, links, pieces, send_sem, recv_sem, tile_send, tile_recv):
        self.links, self.pieces, self.send_sem, self.recv_sem = links, pieces, send_sem, recv_sem
        self.tile_send, self.tile_recv = tile_send, tile_recv
        d = links.d
        self.core, self.x, self.y = d % 2, (d // 2) % 2, d // 4
        self.z = lax.axis_index(SECTION)
        self.inner = (self.z == 1) | (self.z == 2)
        self.outer = (self.z == 0) | (self.z == 3)

    def view(self, piece, ref, block, count, half=None):
        blocks = pl.ds(pl.multiple_of(block * piece.size, piece.size), count * piece.size)
        across = {None: slice(None), 0: slice(0, piece.split), 1: slice(piece.split, piece.across)}[half]
        return ref.at[across, blocks] if piece.by_columns else ref.at[blocks, across]

    def tile_copy(self, block):
        r = self.pieces[R0]
        src = r.whole.at[:, pl.ds(pl.multiple_of((4 * (1 - self.core) + block) * r.size, r.size), r.size)]
        dst = r.whole_r1.at[:, pl.ds(pl.multiple_of(block * r.size, r.size), r.size)]
        return pltpu.make_async_remote_copy(
            src_ref=src, dst_ref=dst, send_sem=self.tile_send.at[block], recv_sem=self.tile_recv.at[block],
            device_id={DP: self.links.core_n}, device_id_type=pl.DeviceIdType.MESH,
        )

    def copy(self, name, kind, l=0):
        piece = self.pieces[name]
        core, x, y, z, links = self.core, self.x, self.y, self.z, self.links
        mine = 4 * core

        def pair(block, to, at, count, half):
            return self.view(piece, piece.grad, block, count, half), self.view(piece, to, at, count, half)

        if kind == 0:
            src, dst = pair(4 * (1 - core), piece.r1, 0, 4, None)
        elif kind in (1, 2):
            src, dst = pair(mine + 2 * (kind - 1) + 1 - x, piece.r2, kind - 1, 1, 0)
        elif kind == 3:
            src, dst = pair(mine + 2 * (1 - y), piece.r2, 0, 2, 1)
        elif kind == 4:
            src, dst = pair(mine + 2 * (1 - y) + x, piece.r3[l], 0, 1, 0)
        elif kind == 5:
            src, dst = pair(mine + 2 * y + 1 - x, piece.r3[l], 0, 1, 1)
        else:
            src = piece.r3[l]
            dst = piece.rz.at[kind - 6] if kind < 8 else piece.out(l)
        device = (
            {DP: links.core_n}, {DP: links.x_n}, {DP: links.x_n}, {DP: links.y_n}, {DP: links.y_n}, {DP: links.x_n},
            {SECTION: z + 1 - 2 * (z // 3)}, {SECTION: 3 - z}, {SECTION: 3 * (z // 2)},
        )[kind]
        return pltpu.make_async_remote_copy(
            src_ref=src, dst_ref=dst, send_sem=self.send_sem.at[piece.index, kind], recv_sem=self.recv_sem.at[piece.index, kind],
            device_id=device, device_id_type=pl.DeviceIdType.MESH,
        )

    def tile_parts(self, block):
        y, x = block // 2, block % 2
        copies = []
        for name in (R0, R1):
            piece = self.pieces[name]
            for half, kind, to, at in ((0, 1 + y, {DP: self.links.x_n}, y), (1, 3 + 7 * x, {DP: self.links.y_n}, x)):
                copies.append(pltpu.make_async_remote_copy(
                    src_ref=self.view(piece, piece.grad, 4 * self.core + block, 1, half), dst_ref=self.view(piece, piece.r2, at, 1, half),
                    send_sem=self.send_sem.at[piece.index, kind], recv_sem=self.recv_sem.at[piece.index, kind],
                    device_id=to, device_id_type=pl.DeviceIdType.MESH,
                ))
        return copies

    def tile_step(self, block):
        self.tile_copy(block).wait_recv()
        r = self.pieces[R0]
        mine = pl.ds(pl.multiple_of((4 * self.core + block) * r.size, r.size), r.size)
        self.add(r.whole.at[:, mine], r.whole_r1.at[:, r.size * block:r.size * (block + 1)])
        first0, second0, first1, second1 = self.tile_parts(block)

        @pl.when(self.x != block % 2)
        def _():
            first0.start()
            first1.start()

        @pl.when(self.y != block // 2)
        def _():
            second0.start()
            second1.start()

    def add(self, into, other):
        into[...] = (into[...].astype(F32) + other[...].astype(F32)).astype(BF16)

    def step(self, name, number, l):
        piece = self.pieces[name]
        grad, r1, r2, r3, rz = piece.grad, piece.r1, piece.r2, piece.r3[l], piece.rz
        mine = 4 * self.core
        own = mine + 2 * self.y + self.x
        tiles = name in (R0, R1)
        if number == 1:
            self.copy(name, 0, l).start()
        elif number == 2 and tiles:
            if name == R0:
                self.tile_step(3)
        elif number == 2:
            self.copy(name, 0, l).wait_recv()
            self.add(self.view(piece, grad, mine, 4), self.view(piece, r1, 0, 4))
            for kind in (1, 2, 3):
                self.copy(name, kind, l).start()
        elif number == 3:
            for kind in (1, 2):
                self.copy(name, kind, l).wait_recv()
                self.add(self.view(piece, grad, mine + 2 * (kind - 1) + self.x, 1, 0), self.view(piece, r2, kind - 1, 1, 0))
            if tiles:
                for i in range(2):
                    self.half_block(name, i).wait_recv()
            else:
                self.copy(name, 3, l).wait_recv()
            self.add(self.view(piece, grad, mine + 2 * self.y, 2, 1), self.view(piece, r2, 0, 2, 1))
            self.copy(name, 4, l).start()
            self.copy(name, 5, l).start()
        elif number == 4:
            for half in (0, 1):
                self.copy(name, 4 + half, l).wait_recv()
                self.add(self.view(piece, r3, 0, 1, half), self.view(piece, grad, own, 1, half))

            @pl.when(self.outer)
            def _():
                self.copy(name, 6, l).start()

            if not tiles:
                self.copy(name, 0, l).wait_send()
            elif name == R0:
                for block in range(4):
                    self.tile_copy(block).wait_send()
            for kind in (1, 2, 4, 5):
                self.copy(name, kind, l).wait_send()
            if tiles:
                for i in range(2):
                    self.half_block(name, i).wait_send()
            else:
                self.copy(name, 3, l).wait_send()
        elif number == 5:

            @pl.when(self.inner)
            def _():
                self.copy(name, 6, l).wait_recv()
                self.add(r3, rz.at[0])
                self.copy(name, 7, l).start()
        elif number == 6:

            @pl.when(self.inner)
            def _():
                self.copy(name, 7, l).wait()
                self.add(r3, rz.at[1])
                self.copy(name, 8, l).start()
                self.local(piece, l).start()
        elif number == 7:

            @pl.when(self.outer)
            def _():
                self.copy(name, 6, l).wait_send()
                self.copy(name, 8, l).wait_recv()

            @pl.when(self.inner)
            def _():
                self.copy(name, 8, l).wait_send()
                self.local(piece, l).wait()

    def half_block(self, name, x):
        piece = self.pieces[name]
        view = self.view(piece, piece.r2, x, 1, 1)
        return pltpu.make_async_remote_copy(
            src_ref=view, dst_ref=view,
            send_sem=self.send_sem.at[piece.index, 3 + 7 * x], recv_sem=self.recv_sem.at[piece.index, 3 + 7 * x],
            device_id={DP: self.links.y_n}, device_id_type=pl.DeviceIdType.MESH,
        )

    def local(self, piece, l):
        return pltpu.make_async_copy(piece.r3[l], piece.out(l), self.send_sem.at[piece.index, 9])


class Piece:
    def __init__(self, index, refs, size, across, split, out, by_columns=False, whole=None):
        self.index, self.size, self.across, self.split, self.out, self.by_columns = index, size, across, split, out, by_columns
        self.grad, self.r1, self.r2, self.r3, self.rz = refs
        self.whole, self.whole_r1 = whole or (None, None)


def sum_pieces(refs, out_m, out_o, out_e, out_r, out_t):
    def part(n, index):
        views = [refs[name + n].at[index] for name in ("grad_", "r1", "r2")]
        views.append([refs["r3" + n].at[(l,) + index] for l in range(1 if n == "t" else LAYERS)])
        return views + [refs["rz" + n].at[(slice(None),) + index]]

    every = slice(None)
    pieces = {}
    for i in range(2):
        cols = slice(FF // 2 * i, FF // 2 * (i + 1))
        pieces[E0 + i] = Piece(E0 + i, part("e", (every, cols)), 64, FF // 2, FF // 4, lambda l, cols=cols: out_e.at[l, :, cols])
    for i in range(2):
        rows = slice(D // 2 * i, D // 2 * (i + 1))
        pieces[R0 + i] = Piece(
            R0 + i, part("r", (rows, every)), 256, D // 2, D // 4, lambda l, rows=rows: out_r.at[l, rows], True,
            (refs["grad_r"], refs["r1r"]),
        )
    for i in range(4):
        cols = slice(384 * i, 384 * (i + 1))
        pieces[M0 + i] = Piece(
            M0 + i, part("m", (every, cols)), 64, 384, 128 * (1 + i % 2), lambda l, i=i: out_m.at[l, i]
        )
    pieces[O] = Piece(O, part("o", (every, every)), 64, D, D // 2, lambda l: out_o.at[l])
    pieces[T] = Piece(T, part("t", (every, every)), 64, 384, 128, lambda l: out_t)
    return pieces


def by_position(rows):
    size = rows.shape[0] // 8
    return jnp.concatenate([rows[size * i:size * (i + 1)] for i in (0, 2, 4, 6, 1, 3, 5, 7)], axis=0)


def step_kernel(linked, *refs):
    names = (LINKED_IN + LINKED_OUT) if linked else (PLAIN_IN + PLAIN_OUT)
    names += tuple(SCRATCH) + tuple(LINKED_SCRATCH if linked else PLAIN_SCRATCH)
    step_body(linked, **dict(zip(names, refs, strict=True)))


def step_body(
    linked, loss, lg, kept_m, kept_near, x, x1, dx, keys, values, pT, inv1s, cum, oT, hT, g, gT, wide, a1k, m, near, keep_sem, d, ds, doT, dpT, yb, acc,
    columns=None, table=None, gm=None, gf=None, gz=None, wm=None, wo=None, we=None, wr=None, stage=None, stage_half=None, sem=None, sem_half=None,
    dtable=None, dgm=None, dgf=None, dgz=None, dwm=None, dwo=None, dwe=None, dwrt=None,
    tokens=None, mask=None, emb=None, mgain=None, fgain=None, zgain=None, wm_s=None, wo_s=None, we_s=None, wr_s=None, tz=None, gains=None, lgs=None, losss=None,
    send_sem=None, recv_sem=None, zsend=None, zrecv=None, load_sem=None, sum_send=None, sum_recv=None, tile_send=None, tile_recv=None,
    out_m=None, out_o=None, out_e=None, out_r=None, out_t=None, dgains=None, **sums_refs,
):
    table_ref = table
    gm_ref, gf_ref, gz_ref = gm, gf, gz
    wm_ref, wo_ref, we_ref, wr_ref = wm, wo, we, wr
    loss_ref, lg_ref, dtable_ref, dgm_ref, dgf_ref, dgz_ref = loss, lg, dtable, dgm, dgf, dgz
    dwm_ref, dwo_ref, dwe_ref, dwrt_ref = dwm, dwo, dwe, dwrt
    x_ref, x1_ref, dx_ref, pT_ref, inv1_ref, cum_ref = x, x1, dx, pT, inv1s, cum
    oT_ref, hT_ref, g_ref, gT_ref, wide_ref, a1k_ref, near_ref, m_ref, d_ref, ds_ref = oT, hT, g, gT, wide, a1k, near, m, d, ds
    doT_ref, dpT_ref, w_ref, yb_ref, acc_ref = doT, dpT, a1k, yb, acc
    xs = [x_ref.at[0], x_ref.at[1], dx_ref]
    placed = by_position if linked else (lambda rows: rows)
    r, c = iotas(2 * CH, 2 * CH)
    upper = (r <= c).astype(F32).astype(BF16)

    if linked:
        zi = lax.axis_index(SECTION)
        links = Links(
            [(table_ref, 64, 384, 256, False)]
            + [
                entry
                for l in range(LAYERS)
                for entry in (
                    (wm_ref.at[l], 64, 3 * D, 3 * D // 2, SHARED[l][0]),
                    (wo_ref.at[l], 64, D, D // 2, SHARED[l][1]),
                    (we_ref.at[l], 64, FF, FF // 2, SHARED[l][2]),
                    (wr_ref.at[l], 256, D, D // 2, SHARED[l][3]),
                )
            ],
            send_sem, recv_sem,
        )

        def along_z(n, k, src_of, dst):
            target = (zi + k) % 4
            return pltpu.make_async_remote_copy(
                src_ref=src_of(target), dst_ref=dst.at[zi], send_sem=zsend.at[n, k - 1], recv_sem=zrecv.at[n, k - 1],
                device_id={SECTION: target}, device_id_type=pl.DeviceIdType.MESH,
            )

        def table_copy(k):
            return along_z(0, k, lambda target: tz.at[zi], tz)

        def lg_copy(k):
            return along_z(1, k, lambda target: lgs.at[target], lg_ref)

        def loss_copy(k):
            return along_z(2, k, lambda target: losss, loss_ref)

        loads = []
        for l in range(LAYERS):
            pairs = [(wm_s.at[l, :, TILE * j:TILE * (j + 1)], x1_ref.at[l, 64 * j:64 * (j + 1)]) for j in range(3)]
            pairs += [(wo_s.at[l], x1_ref.at[l, 192:256])]
            pairs += [(we_s.at[l, :, TILE * j:TILE * (j + 1)], x1_ref.at[l, 256 + 64 * j:320 + 64 * j]) for j in range(4)]
            pairs += [(wr_s.at[l], x_ref.at[1, 256 * l:256 * (l + 1)])]
            loads.append([pltpu.make_async_copy(src, dst, load_sem.at[l, i]) for i, (src, dst) in enumerate(pairs)])
            for load in loads[l]:
                load.start()

        def take(l, part):
            for i in {"m": (0, 1, 2), "o": (3,), "e": (4, 5, 6, 7), "r": (8,)}[part]:
                loads[l][i].wait()
            if part == "m":
                for j in range(3):
                    wm_ref[l, own64, TILE * j:TILE * (j + 1)] = x1_ref[l, 64 * j:64 * (j + 1)].astype(BF16)
            elif part == "o":
                wo_ref[l, own64] = x1_ref[l, 192:256].astype(BF16)
            elif part == "e":
                for j in range(4):
                    we_ref[l, own64, TILE * j:TILE * (j + 1)] = x1_ref[l, 256 + 64 * j:320 + 64 * j].astype(BF16)
            else:
                wr_ref[l, own256] = x_ref[1, 256 * l:256 * (l + 1)].astype(BF16)

        barrier = pltpu.get_barrier_semaphore()
        for target in (links.core_n, links.x_n, links.y_n):
            pl.semaphore_signal(barrier, inc=1, device_id={DP: target}, device_id_type=pl.DeviceIdType.MESH)
        for k in (1, 2, 3):
            pl.semaphore_signal(barrier, inc=1, device_id={SECTION: (zi + k) % 4}, device_id_type=pl.DeviceIdType.MESH)

        own64 = pl.ds(pl.multiple_of(links.d * 64, 64), 64)
        own256 = pl.ds(pl.multiple_of(links.d * 256, 256), 256)
        r, _ = iotas(8, 64)
        rows = [mgain[0:1], mgain[1:2], fgain[0:1], fgain[1:2], zgain[0:1]]
        gathered = sum(jnp.where(r == i, row, 0.0) for i, row in enumerate(rows))
        gathered = jnp.concatenate([gathered, jnp.zeros((8, 64), F32)], axis=1)
        gathered = jnp.concatenate([gathered, jnp.zeros((120, 128), F32)], axis=0).T[:64]
        small_b = (jnp.concatenate([emb[...], jnp.zeros((64, 64), F32)], axis=1) + pltpu.roll(gathered, 64, 1)).astype(BF16)
        tz[zi] = small_b
        take(0, "m")
        pl.semaphore_wait(barrier, 6)
        for k in (1, 2, 3):
            table_copy(k).start()
        links.own(1)
        r, c = iotas(8, LEN)
        ids = tokens[pl.ds(zi, 1), :].astype(F32)
        scored = mask[pl.ds(zi, 1), :].astype(F32)
        rows = [ids, pltpu.roll(ids, LEN - 1, 1), pltpu.roll(scored, LEN - 1, 1)]
        rows = sum(jnp.where((r == i) & ((c < LEN - 1) | (r == 0)), row, 0.0) for i, row in enumerate(rows))
        columns[...] = rows.T.astype(jnp.int32)
        take(0, "o")
        for k in (1, 2, 3):
            table_copy(k).wait_recv()
        pad = jnp.zeros((64, 64), BF16)
        table_ref[own64, :] = jnp.concatenate([tz[i][:, :64] for i in range(4)] + [small_b[:, 64:], pad], axis=1)
        links.own(0, 2)
        take(0, "e")
        wide_ref[...] = upper
        links.first(1, 0)
        links.own(3)
        links.first(2)
        take(0, "r")
        links.own(4)
        for part in "moer":
            take(1, part)
        links.second(1, 0)
        links.ready(0)
        gains[...] = table_ref[:, 256:].astype(F32).T[:8]
        table_ref = table_ref.at[:, :256]
        gm_ref, gf_ref, gz_ref = [gains[i:i + 1] for i in range(2)], [gains[i:i + 1] for i in range(2, 4)], gains[4:5]
        sums = Sums(
            links, sum_pieces(sums_refs, out_m, out_o, out_e, out_r, out_t), sum_send, sum_recv, tile_send, tile_recv
        )
    else:
        wide_ref[...] = upper
        gm_ref, gf_ref, gz_ref = [gm_ref[i] for i in range(2)], [gf_ref[i] for i in range(2)], gz_ref[...]

    def service(step, index=None, only=lambda at: True):
        if not linked:
            return
        for at, acts in SERVICE.get(step, {}).items():
            if not only(at):
                continue

            def run(acts=acts):
                for act in acts:
                    if isinstance(act[0], int):
                        sums.step(*act)
                    elif act[0] is Sums.tile_step:
                        sums.tile_step(act[1])
                    else:
                        act[0](links, *act[1:])

            if at is None:
                run()
            else:
                pl.when(index == at)(run)

    inv2 = 1.0 / (lax.broadcasted_iota(jnp.int32, (1, LEN), 1).astype(F32) + 1.0)

    def emit(slot, wait_first, value, dst, pool=0):
        into, sems = (stage, sem) if pool == 0 else (stage_half, sem_half)

        def copy():
            return pltpu.make_async_copy(into.at[slot], dst, sems.at[slot])

        if wait_first is True:
            copy().wait()
        elif wait_first is not False:
            pl.when(wait_first)(lambda: copy().wait())
        into[slot] = value.astype(BF16)
        copy().start()

    def put_gain(row, value):
        if linked:
            dgains[row:row + 1] = value
        elif row < 2:
            dgm_ref[row] = value
        elif row < 4:
            dgf_ref[row - 2] = value
        else:
            dgz_ref[...] = value

    def by_rows(run, init=None):
        for i in range(CHUNKS):
            init = run(slice(i * CH, (i + 1) * CH), init)
        return init

    def normed_rows(src, gain, dst, dstT):
        def some(rows, carry):
            block = norm_forward(src[rows], gain).astype(BF16)
            dst[rows] = block
            dstT[:, rows] = placed(block.T)
            return carry

        by_rows(some, 0)

    def back_rows(src, gain, row):
        def some(rows, dgain):
            dv, dg = norm_backward(src[rows], gain, acc_ref[rows])
            dx_ref[rows] += dv
            return dgain + dg

        put_gain(row, by_rows(some, jnp.zeros((1, D), F32)))

    vocab_ids = lax.broadcasted_iota(jnp.int32, (LEN, VOCAB), 1)
    hot = (vocab_ids == columns[:, 0:1]).astype(F32).astype(BF16)
    x_ref[0] = mm_nt(hot, table_ref[...])
    if linked:
        links.ready(1)

    def keep(l, h, e):
        return (
            pltpu.make_async_copy(m_ref.at[e], kept_m.at[l, h], keep_sem.at[e, 0]),
            pltpu.make_async_copy(near_ref.at[e], kept_near.at[l, h], keep_sem.at[e, 1]),
        )

    def fetch(l, h, e):
        return (
            pltpu.make_async_copy(kept_m.at[l, h], m_ref.at[e], keep_sem.at[e, 0]),
            pltpu.make_async_copy(kept_near.at[l, h], near_ref.at[e], keep_sem.at[e, 1]),
        )

    m_ref[...] = jnp.zeros_like(m_ref)
    near_ref[...] = jnp.zeros_like(near_ref)

    def key_sums(l):
        a1k_ref[...] = feature_parts(pT_ref[l, D:2 * D, :].astype(F32))[0].astype(BF16)
        for t0, t1 in WIDE:
            total = mm(a1k_ref[:, t0:t1], wide_ref[:t1 - t0, :t1 - t0])
            cum_ref[:, t0:t1] = total if t0 == 0 else total + cum_ref[:, t0 - 1:t0]

    def attention_forward(l):
        normed_rows(x_ref.at[l], gm_ref[l], yb_ref, hT_ref.at[l])
        h = yb_ref[...]
        for j in range(3):
            part = mm(h, wm_ref[l, :, j * TILE:(j + 1) * TILE]).astype(BF16)
            if j == 1:
                keys[...] = part
            if j == 2:
                values[l] = part
            pT_ref[l, j * TILE:(j + 1) * TILE, :] = part.T
        service((MIXER, l))
        key_sums(l)

        def pair(p, carry):
            base = pl.multiple_of(p * CH, CH)
            for e in range(2):
                row = pl.multiple_of(base + e * HD, HD)
                if l == 0:
                    pl.when(p > 0)(lambda: every(keep(l, 0, e), WAIT))
                else:
                    for copy in keep(l, 0, e):
                        copy.wait()
                qT = pT_ref[l, pl.ds(row, HD), :]
                kT = pT_ref[l, pl.ds(pl.multiple_of(D + row, HD), HD), :]
                vT = pT_ref[l, pl.ds(pl.multiple_of(2 * D + row, HD), HD), :]
                first_k, _, second_k = feature_parts(kT.astype(F32))
                key_feat = jnp.concatenate([first_k.astype(BF16), second_k.astype(BF16)], axis=0).T
                first_q = feature_parts(qT.astype(F32))[0].astype(BF16).astype(F32)
                total = jnp.sum(first_q * cum_ref[pl.ds(row, HD), :], axis=0, keepdims=True)
                inv1 = 1.0 / (total + 1.0)
                inv1_ref[l, 2 * p + e] = inv1
                query_feat2 = query_features(qT, inv1, inv2)[3]
                key_feat2 = jnp.concatenate([key_feat, key_feat], axis=1)
                key_nat = keys[:, pl.ds(base, CH)]
                query_masked = masked_pair(qT, e)
                for t0, t1 in WIDE:
                    mixture = mixture_block(t0, t1, key_nat, key_feat2, query_masked, query_feat2, near_ref.at[e])
                    m_ref[e, :t1, t0:t1] = mixture
                    oT_ref[l, pl.ds(row, HD), t0:t1] = mm(vT[:, :t1], mixture).astype(BF16)
                for copy in keep(l, 2 * p + e, e):
                    copy.start()
                service((HEAD, l), 2 * p + e, lambda at: at % 2 == e)
            return carry

        lax.fori_loop(0, HEADS // 2, pair, 0)
        service((OUTPUT, l))
        o = oT_ref[l].T
        x1_ref[l] = x_ref[l] + mm(o, wo_ref[l])

    def feed_forward(l):
        normed_rows(x1_ref.at[l], gf_ref[l], g_ref, gT_ref.at[l])
        xs[l + 1][...] = x1_ref[l]
        service((FEED, l))

        def tile(j, carry):
            col = pl.multiple_of(j * TILE, TILE)
            active = gelu_parts(mm(g_ref[...], we_ref[l, :, pl.ds(col, TILE)]))[0].astype(BF16)
            service((GELU, l), j)
            xs[l + 1][...] += mm(active, wr_ref[l, pl.ds(col, TILE), :])
            service((FEED_TILE, l), j)
            return carry

        lax.fori_loop(0, FF // TILE, tile, 0)

    def head():
        zT_ref, grad_ref = doT_ref, yb_ref.at[:, :VOCAB]

        def some(rows, carry):
            dgain, cross_sum, val_sum = carry
            x = dx_ref[rows]
            z = norm_forward(x, gz_ref).astype(BF16)
            zT_ref[:, rows] = placed(z.T)
            logits = mm(z, table_ref[...])
            ids = lax.broadcasted_iota(jnp.int32, (CH, VOCAB), 1)
            tgt_hot = (ids == columns[rows, 1:2]).astype(F32)
            val = columns[rows, 2:3].astype(F32)
            peak = jnp.max(logits, axis=-1, keepdims=True)
            grown = jnp.exp(logits - peak)
            total = jnp.sum(grown, axis=-1, keepdims=True)
            lse = peak + jnp.log(total)
            picked = jnp.sum(logits * tgt_hot, axis=-1, keepdims=True)
            cross = (lse - picked) * val
            grad_b = ((grown / total - tgt_hot) * val).astype(BF16)
            grad_ref[rows, :] = grad_b
            if linked:
                grad_bT = grad_b.T
                for i in range(4):
                    lgs[i, :, rows] = grad_bT[64 * i:64 * i + 64]
            else:
                lg_ref[rows, :] = grad_b
            dv, dg = norm_backward(x, gz_ref, mm_nt(grad_b, table_ref[...]))
            dx_ref[rows] = dv
            return (
                dgain + dg,
                cross_sum + jnp.sum(cross, axis=0, keepdims=True),
                val_sum + jnp.sum(val, axis=0, keepdims=True),
            )

        nothing = jnp.zeros((1, 1), F32)
        dgain, cross_sum, val_sum = by_rows(some, (jnp.zeros((1, D), F32), nothing, nothing))
        put_gain(4, dgain)
        loss = jnp.broadcast_to(cross_sum / val_sum, (8, 128))
        if linked:
            losss[...] = loss
            for k in (1, 2, 3):
                lg_copy(k).start()
                loss_copy(k).start()
            pltpu.make_async_copy(lgs.at[zi], lg_ref.at[zi], zsend.at[1, 3]).start()
            pltpu.make_async_copy(losss, loss_ref.at[zi], zsend.at[2, 3]).start()
        else:
            loss_ref[...] = loss
        dtable_head = mm(zT_ref[...], grad_ref[...])
        if linked:
            sums_refs["grad_t"][:, :VOCAB] = dtable_head.astype(BF16)
        else:
            dtable_ref[...] = dtable_head

    def feed_backward(l):
        def some(rows, carry):
            yb = dx_ref[rows].astype(BF16)
            yb_ref[rows] = yb
            doT_ref[:, rows] = yb.T
            if l < LAYERS - 1:
                g_ref[rows] = norm_forward(x1_ref[l, rows], gf_ref[l]).astype(BF16)
            return carry

        by_rows(some, 0)
        acc_ref[...] = jnp.zeros_like(acc_ref)

        def tile(j, carry):
            col = pl.multiple_of(j * TILE, TILE)
            slot = lax.rem(j, 2)
            later = (j >= 2) if l == LAYERS - 1 else True
            value, slope = gelu_parts(mm(g_ref[...], we_ref[l, :, pl.ds(col, TILE)]))
            dreduce = mm(doT_ref[...], value.astype(BF16))
            if linked:
                for i in range(2):
                    place = pl.multiple_of(BACK * j + FF // 2 * i, BACK)
                    sums_refs["grad_r"][:, pl.ds(place, BACK)] = dreduce[:, BACK * i:BACK * (i + 1)].astype(BF16)
                sums.tile_copy(j).start()
            else:
                emit(slot, later, dreduce, dwrt_ref.at[l, :, pl.ds(col, TILE)], 1)
            dact = mm_nt(yb_ref[...], wr_ref[l, pl.ds(col, TILE), :])
            dhid = (dact * slope).astype(BF16)
            dexpand = mm(gT_ref[l], dhid)
            if linked:
                sums_refs["grad_e"][:, pl.ds(col, TILE)] = dexpand.astype(BF16)
            else:
                emit(2 + slot, later, dexpand, dwe_ref.at[l, :, pl.ds(col, TILE)], 1)
            dnormed = mm_nt(dhid, we_ref[l, :, pl.ds(col, TILE)])

            acc_ref[...] += dnormed
            service((BACK_TILE, l), j)
            return carry

        lax.fori_loop(0, FF // TILE, tile, 0)
        service((BACK_FEED, l))
        back_rows(x1_ref.at[l], gf_ref[l], 2 + l)

    def attention_backward(l):
        if l < LAYERS - 1:
            key_sums(l)
        yb_ref[...] = dx_ref[...].astype(BF16)
        yb = yb_ref[...]
        doutput = mm(placed(oT_ref[l]), yb)
        if linked:
            sums_refs["grad_o"][...] = doutput.astype(BF16)
        else:
            emit(0, l < LAYERS - 1, doutput, dwo_ref.at[l])
        service((BACK_OUTPUT, l))
        doT_ref[...] = mm_nt(yb, wo_ref[l]).astype(BF16).T

        for e in range(2):
            for copy in fetch(l, e, e):
                copy.start()

        def pair(p, carry):
            base = pl.multiple_of(p * CH, CH)
            for e in range(2):
                row = pl.multiple_of(base + e * HD, HD)
                qT = pT_ref[l, pl.ds(row, HD), :]
                kT = pT_ref[l, pl.ds(pl.multiple_of(D + row, HD), HD), :]
                doT = doT_ref[pl.ds(row, HD), :]
                inv1 = inv1_ref[l, 2 * p + e]
                first_q, slope1_q, second_q, query_feat2 = query_features(qT, inv1, inv2)
                first_k, slope1_k, second_k = feature_parts(kT.astype(F32))
                key_featT = jnp.concatenate([first_k.astype(BF16), second_k.astype(BF16)], axis=0)
                value_nat = values[l, :, pl.ds(base, CH)]
                do_masked = masked_pair(doT, e)
                for copy in fetch(l, 2 * p + e, e):
                    copy.wait()
                far_q, near_q = [], []
                for t0, t1 in WIDE:
                    dm = mm(value_nat[:t1], do_masked[:, t0:t1])

                    def half(i):
                        r0, end = first_row(i), (i + 1) * CH
                        column = dm[:end, i * CH - t0:end - t0]
                        bottom = column[r0:]
                        near = near_ref[e, i, :end - r0, :]
                        weighted = near * bottom
                        dsum = jnp.sum(weighted, axis=0, keepdims=True)
                        ds = ((weighted - near * dsum) * 0.125).astype(BF16)
                        if i > 0:
                            before = jnp.concatenate([jnp.zeros((CH - REACH, CH), BF16), ds[:REACH]], axis=0)
                            ds_ref[end - 2 * CH:end - CH, CH:] = before
                            ds = ds[REACH:]
                            near_q.append(mm(kT[:, end - 2 * CH:end], jnp.concatenate([before, ds], axis=0)))
                        else:
                            near_q.append(mm(kT[:, :end], ds))
                        ds_ref[end - CH:end, :CH] = ds
                        lower = causal_rows(i, bottom).astype(BF16)
                        if r0 == 0:
                            return lower
                        return jnp.concatenate([column[:r0].astype(BF16), lower], axis=0)

                    dm_b = halves(t0, t1, half)
                    d_ref[:t1, t0:t1] = dm_b
                    far_q.append(mm(key_featT[:, :t1], dm_b))
                farT = jnp.concatenate(far_q, axis=1)
                y1, y2 = farT[:HD], farT[HD:]
                first_qf = first_q.astype(F32)
                m = inv1 * jnp.sum(first_qf * y1, axis=0, keepdims=True)
                cum = cum_ref[pl.ds(row, HD), :]
                dq = jnp.concatenate(near_q, axis=1)
                dq = dq + (inv1 * (y1 - m * cum)) * slope1_q + (inv2 * y2) * (1.0 - second_q * second_q)
                dpT_ref[pl.ds(row, HD), :] = dq.astype(BF16)
                w_ref[pl.ds(row, HD), :] = (first_qf * (m * inv1)).astype(BF16)
                after = 0.0
                for t0, t1 in reversed(WIDE):
                    far = mm_nt(query_feat2[:CH, t0:], d_ref[t0:t1, t0:])
                    back = mm_nt(w_ref[pl.ds(row, HD), t0:t1], wide_ref[:t1 - t0, :t1 - t0]) + after
                    after = back[:, :1]
                    near_k = []
                    for u0 in range(t0, t1, CH):
                        u2 = min(u0 + 2 * CH, LEN)
                        near_k.append(mm_nt(qT[:, u0:u2], ds_ref[u0:u0 + CH, :u2 - u0]))
                    near = near_k[0] if len(near_k) == 1 else jnp.concatenate(near_k, axis=1)
                    dk = near + (far[:HD] - back) * slope1_k[:, t0:t1]
                    dk = dk + far[HD:] * (1.0 - second_k[:, t0:t1] * second_k[:, t0:t1])
                    dpT_ref[pl.ds(pl.multiple_of(D + row, HD), HD), t0:t1] = dk.astype(BF16)
                    dv = mm_nt(doT[:, t0:], m_ref[e, t0:t1, t0:])
                    dpT_ref[pl.ds(pl.multiple_of(2 * D + row, HD), HD), t0:t1] = dv.astype(BF16)
                pl.when(p < HEADS // 2 - 1)(lambda: every(fetch(l, 2 * p + e + 2, e), START))
                service((BACK_HEAD, l), 2 * p + e, lambda at: at % 2 == e)
            if linked:
                for j in range(3):
                    block = mm_nt(hT_ref[l], dpT_ref[pl.ds(pl.multiple_of(j * D + base, CH), CH), :])
                    place = pl.multiple_of(3 * base + j * CH, CH)
                    sums_refs["grad_m"][:, pl.ds(place, CH)] = block.astype(BF16)
                service((BACK_PAIR, l), p)
            return carry

        lax.fori_loop(0, HEADS // 2, pair, 0)
        if not linked:
            for j in range(3):
                block = mm_nt(hT_ref[l], dpT_ref[j * TILE:(j + 1) * TILE, :])
                emit(1 + j, l < LAYERS - 1, block, dwm_ref.at[l, :, j * TILE:(j + 1) * TILE])
        for t0 in range(0, LEN, 256):
            t1 = min(t0 + 256, LEN)
            acc_ref[t0:t1] = mm(wm_ref[l], dpT_ref[:, t0:t1]).T
        service((BACK_MIXER, l))
        back_rows(x_ref.at[l], gm_ref[l], l)
        service((BACK_LAYER, l))

    for l in range(LAYERS):
        service((LAYER, l))
        attention_forward(l)
        feed_forward(l)
    for e in range(2):
        for copy in keep(0, 0, e):
            copy.wait()
    head()
    for l in reversed(range(LAYERS)):
        feed_backward(l)
        attention_backward(l)
    dtable_head = sums_refs["grad_t"][:, :VOCAB].astype(F32) if linked else dtable_ref[...]
    dtable_sum = dtable_head + mm(placed(dx_ref[...].astype(BF16).T), hot)
    if linked:
        sums_refs["grad_t"][:, :VOCAB] = dtable_sum.astype(BF16)
        sums_refs["grad_t"][:, VOCAB:] = placed(jnp.concatenate([dgains[...], jnp.zeros((120, D), F32)], axis=0).T).astype(BF16)
        service((END, 0))
        for k in (1, 2, 3):
            table_copy(k).wait_send()
            lg_copy(k).wait()
            loss_copy(k).wait()
        pltpu.make_async_copy(lgs.at[zi], lg_ref.at[zi], zsend.at[1, 3]).wait()
        pltpu.make_async_copy(losss, loss_ref.at[zi], zsend.at[2, 3]).wait()
        links.finish()
    else:
        dtable_ref[...] = dtable_sum
        for slot in range(4):
            pltpu.make_async_copy(stage.at[slot], dwo_ref.at[0], sem.at[slot]).wait()
            pltpu.make_async_copy(stage_half.at[slot], dwe_ref.at[0, :, :TILE], sem_half.at[slot]).wait()


E0, E1, R0, R1, M0, M1, M2, M3, O, T = range(10)
MIXER, HEAD, FEED, GELU, FEED_TILE, LAYER, BACK_TILE, BACK_FEED, BACK_OUTPUT, BACK_HEAD, BACK_PAIR, BACK_MIXER, BACK_LAYER, END, OUTPUT = range(15)
SHARED = ((False, False, True, False), (True, False, True, False))
SERVICE = {
    (MIXER, 0): {
        None: ((Links.second, 2), (Links.first, 3),),
    },
    (HEAD, 0): {
        1: ((Links.own, 5),),
        3: ((Links.first, 4),),
        4: ((Links.second, 3),),
        5: ((Links.own, 6),),
        6: ((Links.first, 5),),
        7: ((Links.own, 7),),
    },
    (OUTPUT, 0): {
        None: ((Links.ready, 2),),
    },
    (FEED, 0): {
        None: ((Links.second, 4), (Links.third, 3), (Links.ready, 3),),
    },
    (GELU, 0): {
        0: ((Links.ready, 4),),
    },
    (FEED_TILE, 0): {
        0: ((Links.second, 5), (Links.first, 6), (Links.own, 8),),
        2: ((Links.first, 7),),
    },
    (LAYER, 1): {
        None: ((Links.third, 5), (Links.ready, 5),),
    },
    (MIXER, 1): {
        None: ((Links.second, 6), (Links.first, 8),),
    },
    (HEAD, 1): {
        0: ((Links.second, 7),),
        4: ((Links.second, 8),),
        5: ((Links.third, 7),),
    },
    (OUTPUT, 1): {
        None: ((Links.ready, 6),),
    },
    (FEED, 1): {
        None: ((Links.ready, 7),),
    },
    (GELU, 1): {
        0: ((Links.ready, 8),),
    },
    (BACK_TILE, 1): {
        1: ((E0, 1, 1), (Sums.tile_step, 0),),
        2: ((Sums.tile_step, 1),),
        3: ((Sums.tile_step, 2),),
    },
    (BACK_FEED, 1): {
        None: ((E1, 1, 1),),
    },
    (BACK_OUTPUT, 1): {
        None: ((O, 1, 1), (E0, 2, 1),),
    },
    (BACK_HEAD, 1): {
        0: ((E1, 2, 1), (R0, 2, 1),),
        2: ((E0, 3, 1),),
        3: ((R1, 2, 1), (M0, 2, 1),),
        4: ((E1, 3, 1), (R0, 3, 1), (R1, 3, 1),),
        5: ((E0, 4, 1),),
        6: ((E1, 4, 1), (M1, 2, 1),),
        7: ((R0, 4, 1), (M2, 2, 1),),
    },
    (BACK_PAIR, 1): {
        0: ((M0, 1, 1),),
        1: ((M1, 1, 1),),
        2: ((M2, 1, 1), (M0, 3, 1),),
        3: ((M3, 1, 1), (O, 2, 1),),
    },
    (BACK_MIXER, 1): {
        None: ((E0, 5, 1), (R1, 4, 1), (M0, 4, 1), (M3, 2, 1),),
    },
    (BACK_LAYER, 1): {
        None: ((M1, 3, 1),),
    },
    (BACK_TILE, 0): {
        0: ((E1, 5, 1), (M2, 3, 1), (M3, 3, 1), (O, 3, 1),),
        1: ((E0, 1, 0), (Sums.tile_step, 0), (E0, 6, 1), (R0, 5, 1), (M1, 4, 1),),
        2: ((Sums.tile_step, 1), (E1, 6, 1), (R1, 5, 1), (M0, 5, 1), (M2, 4, 1), (M3, 4, 1), (O, 4, 1), (E0, 2, 0),),
        3: ((Sums.tile_step, 2), (R0, 6, 1), (M1, 5, 1), (M2, 5, 1), (E0, 7, 1),),
    },
    (BACK_FEED, 0): {
        None: ((E1, 1, 0),),
    },
    (BACK_OUTPUT, 0): {
        None: ((O, 1, 0), (M3, 5, 1), (R0, 2, 0),),
    },
    (BACK_HEAD, 0): {
        0: ((R1, 6, 1), (M0, 6, 1), (O, 5, 1), (E1, 7, 1), (E1, 2, 0), (E0, 3, 0),),
        1: ((M1, 6, 1), (M2, 6, 1), (M3, 6, 1), (R0, 7, 1), (R0, 3, 0),),
        2: ((O, 6, 1), (R1, 2, 0), (R1, 3, 0),),
        3: ((R1, 7, 1), (E1, 3, 0),),
        4: ((M1, 7, 1), (M2, 7, 1), (R0, 4, 0), (M0, 2, 0),),
        5: ((M3, 7, 1), (R1, 4, 0), (M1, 2, 0),),
        6: ((M0, 3, 0), (M2, 2, 0),),
        7: ((R0, 5, 0), (M1, 3, 0),),
    },
    (BACK_PAIR, 0): {
        0: ((M0, 1, 0),),
        1: ((M1, 1, 0), (M0, 7, 1), (E0, 4, 0),),
        2: ((M2, 1, 0), (O, 7, 1), (E0, 5, 0), (E1, 4, 0), (O, 2, 0),),
        3: ((M3, 1, 0),),
    },
    (BACK_MIXER, 0): {
        None: ((E0, 6, 0), (R1, 5, 0), (M0, 4, 0), (O, 3, 0), (M3, 2, 0),),
    },
    (BACK_LAYER, 0): {
        None: ((M1, 4, 0), (M2, 3, 0),),
    },
    (END, 0): {
        None: (
            (T, 1, 0), (E1, 5, 0), (T, 2, 0), (R0, 6, 0), (O, 4, 0), (M0, 5, 0), (M3, 3, 0), (M1, 5, 0), (M2, 4, 0), (R1, 6, 0),
            (O, 5, 0), (T, 3, 0), (M2, 5, 0), (M3, 4, 0), (E1, 6, 0), (M3, 5, 0), (M0, 6, 0), (T, 4, 0), (M1, 6, 0), (T, 5, 0),
            (O, 6, 0), (M2, 6, 0), (M3, 6, 0), (T, 6, 0), (E0, 7, 0), (R0, 7, 0), (R1, 7, 0), (E1, 7, 0), (M0, 7, 0),
            (M1, 7, 0), (O, 7, 0), (M2, 7, 0), (M3, 7, 0), (T, 7, 0),
        ),
    },
}
PLAIN_IN = ("columns", "table", "gm", "gf", "gz", "wm", "wo", "we", "wr")
PLAIN_OUT = ("loss", "lg", "kept_m", "kept_near", "dtable", "dgm", "dgf", "dgz", "dwm", "dwo", "dwe", "dwrt")
LINKED_IN = ("tokens", "mask", "emb", "mgain", "fgain", "zgain", "wm_s", "wo_s", "we_s", "wr_s")
LINKED_OUT = ("loss", "lg", "kept_m", "kept_near", "out_m", "out_o", "out_e", "out_r", "out_t")
SCRATCH = dict(
    x=pltpu.VMEM((LAYERS, LEN, D), F32),
    x1=pltpu.VMEM((LAYERS, LEN, D), F32),
    dx=pltpu.VMEM((LEN, D), F32),
    keys=pltpu.VMEM((LEN, D), BF16),
    values=pltpu.VMEM((LAYERS, LEN, D), BF16),
    pT=pltpu.VMEM((LAYERS, 3 * D, LEN), BF16),
    inv1s=pltpu.VMEM((LAYERS, HEADS, 1, LEN), F32),
    cum=pltpu.VMEM((D, LEN), F32),
    oT=pltpu.VMEM((LAYERS, D, LEN), BF16),
    hT=pltpu.VMEM((LAYERS, D, LEN), BF16),
    g=pltpu.VMEM((LEN, D), BF16),
    gT=pltpu.VMEM((LAYERS, D, LEN), BF16),
    wide=pltpu.VMEM((2 * CH, 2 * CH), BF16),
    a1k=pltpu.VMEM((D, LEN), BF16),
    m=pltpu.VMEM((2, LEN, LEN), BF16),
    near=pltpu.VMEM((2, CHUNKS, CH + REACH, CH), F32),
    keep_sem=pltpu.SemaphoreType.DMA((2, 2)),
    d=pltpu.VMEM((LEN, LEN), BF16),
    ds=pltpu.VMEM((LEN, 2 * CH), BF16),
    doT=pltpu.VMEM((D, LEN), BF16),
    dpT=pltpu.VMEM((3 * D, LEN), BF16),
    yb=pltpu.VMEM((LEN, D), BF16),
    acc=pltpu.VMEM((LEN, D), F32),
)
PLAIN_SCRATCH = dict(
    stage=pltpu.VMEM((4, D, TILE), BF16),
    stage_half=pltpu.VMEM((4, D, TILE), BF16),
    sem=pltpu.SemaphoreType.DMA((4,)),
    sem_half=pltpu.SemaphoreType.DMA((4,)),
)


def sum_buffers(n, rows, cols, along):
    def shape(blocks):
        return (rows * blocks // 8, cols) if along == 0 else (rows, cols * blocks // 8)

    return {
        "grad_" + n: pltpu.VMEM((rows, cols), BF16),
        "r1" + n: pltpu.VMEM(shape(4), BF16),
        "r2" + n: pltpu.VMEM(shape(2), BF16),
        "r3" + n: pltpu.VMEM((1 if n == "t" else LAYERS,) + shape(1), BF16),
        "rz" + n: pltpu.VMEM((2,) + shape(1), BF16),
    }


LINKED_SCRATCH = dict(
    table=pltpu.VMEM((D, 384), BF16),
    wm=pltpu.VMEM((LAYERS, D, 3 * D), BF16),
    wo=pltpu.VMEM((LAYERS, D, D), BF16),
    we=pltpu.VMEM((LAYERS, D, FF), BF16),
    wr=pltpu.VMEM((LAYERS, FF, D), BF16),
    columns=pltpu.VMEM((LEN, 8), jnp.int32),
    tz=pltpu.VMEM((4, 64, 128), BF16),
    gains=pltpu.VMEM((8, D), F32),
    lgs=pltpu.VMEM((4, 64, LEN), BF16),
    losss=pltpu.VMEM((8, 128), F32),
    send_sem=pltpu.SemaphoreType.DMA((9, 15)),
    recv_sem=pltpu.SemaphoreType.DMA((9, 15)),
    zsend=pltpu.SemaphoreType.DMA((3, 4)),
    zrecv=pltpu.SemaphoreType.DMA((3, 4)),
    load_sem=pltpu.SemaphoreType.DMA((LAYERS, 9)),
    sum_send=pltpu.SemaphoreType.DMA((10, 11)),
    sum_recv=pltpu.SemaphoreType.DMA((10, 11)),
    tile_send=pltpu.SemaphoreType.DMA((4,)),
    tile_recv=pltpu.SemaphoreType.DMA((4,)),
    dgains=pltpu.VMEM((8, D), F32),
    **sum_buffers("m", D, 3 * D, 0),
    **sum_buffers("o", D, D, 0),
    **sum_buffers("e", D, FF, 0),
    **sum_buffers("r", D, FF, 1),
    **sum_buffers("t", D, 384, 0),
)


def local_step(linked, *operands):
    vmem = pl.BlockSpec(memory_space=pltpu.VMEM)
    hbm = pl.BlockSpec(memory_space=pl.ANY)
    shape = jax.ShapeDtypeStruct
    kept = (shape((LAYERS, HEADS, LEN, LEN), BF16), shape((LAYERS, HEADS, CHUNKS, CH + REACH, CH), F32))
    if linked:
        scratch = dict(SCRATCH, **LINKED_SCRATCH)
        in_specs = [vmem] * 6 + [hbm] * 4
        out_shape = (
            shape((4, 8, 128), F32),
            shape((4, 64, LEN), BF16),
            *kept,
            shape((LAYERS, 4, 64, 384), BF16),
            shape((LAYERS, 64, D), BF16),
            shape((LAYERS, 64, FF), BF16),
            shape((LAYERS, D, 256), BF16),
            shape((64, 384), BF16),
        )
        out_specs = (hbm,) * 9
    else:
        scratch = dict(SCRATCH, **PLAIN_SCRATCH)
        in_specs = [vmem] * len(operands)
        out_shape = (
            shape((8, 128), F32),
            shape((LEN, VOCAB), BF16),
            *kept,
            shape((D, VOCAB), F32),
            shape((LAYERS, 1, D), F32),
            shape((LAYERS, 1, D), F32),
            shape((1, D), F32),
            shape((LAYERS, D, 3 * D), BF16),
            shape((LAYERS, D, D), BF16),
            shape((LAYERS, D, FF), BF16),
            shape((LAYERS, D, FF), BF16),
        )
        out_specs = (vmem,) * 2 + (hbm,) * 2 + (vmem,) * 4 + (hbm,) * 4
    return pl.pallas_call(
        functools.partial(step_kernel, linked),
        out_shape=out_shape,
        in_specs=in_specs,
        out_specs=out_specs,
        scratch_shapes=list(scratch.values()),
        compiler_params=pltpu.CompilerParams(
            vmem_limit_bytes=64 * 1024 * 1024,
            collective_id=0 if linked else None,
            has_side_effects=linked,
        ),
        cost_estimate=pl.CostEstimate(flops=40_000_000_000, bytes_accessed=40_000_000, transcendentals=0),
        name="local_step",
    )(*operands)


def finish_kernel(*refs):
    count = 7
    ins, outs = refs[:count], refs[count:count + 10]
    held, made = refs[count + 10:2 * count + 10], refs[2 * count + 10:2 * count + 20]
    in_sem, out_sem = refs[2 * count + 20:]
    copies = [pltpu.make_async_copy(src, dst, in_sem.at[i]) for i, (src, dst) in enumerate(zip(ins, held))]
    leave = [pltpu.make_async_copy(src, dst, out_sem.at[i]) for i, (src, dst) in enumerate(zip(made, outs))]
    every(copies, START)
    loss, lg, dwm, dwo, dwe, dwrt, last = held
    out_loss, out_lg, out_table, out_m, out_o, out_mgain, out_e, out_r, out_fgain, out_zgain = made
    z = lax.axis_index(SECTION)
    copies[4].wait()
    out_e[...] = dwe[...].astype(F32)
    leave[6].start()
    copies[1].wait()
    out_lg[...] = lg[...].astype(F32)
    leave[1].start()
    copies[2].wait()
    for l in range(LAYERS):
        for p in range(4):
            for j in range(3):
                out_m[l, :, D * j + CH * p:D * j + CH * (p + 1)] = dwm[l, p, :, CH * j:CH * (j + 1)].astype(F32)
    leave[3].start()
    copies[5].wait()
    for l in range(LAYERS):
        out_r[l] = dwrt[l].astype(F32).T
    leave[7].start()
    copies[3].wait()
    out_o[...] = dwo[...].astype(F32)
    leave[4].start()
    copies[6].wait()
    table = last[:, :VOCAB].astype(F32)
    out_table[...] = sum(jnp.where(z == i, table[:, 64 * i:64 * (i + 1)], 0.0) for i in range(4))
    leave[2].start()
    gains = last[:, VOCAB:].astype(F32)
    gains = jnp.concatenate([gains, jnp.zeros((64, 128), F32)], axis=0).T
    out_mgain[...] = gains[0:2, :64]
    out_fgain[...] = gains[2:4, :64]
    out_zgain[...] = gains[4:5, :64]
    copies[0].wait()
    r, c = iotas(4, 128)
    out_loss[...] = jnp.sum(jnp.where(r == c, loss[:, 0, :], 0.0), axis=0)[:4]
    for i in (5, 8, 9, 0):
        leave[i].start()
    every(leave, WAIT)


def finish(*operands):
    hbm = pl.BlockSpec(memory_space=pl.ANY)
    shapes = (
        (4,), (4, 64, LEN), (64, 64), (LAYERS, 64, 3 * D), (LAYERS, 64, D), (LAYERS, 64), (LAYERS, 64, FF),
        (LAYERS, 256, D), (LAYERS, 64), (1, 64),
    )
    return pl.pallas_call(
        finish_kernel,
        out_shape=tuple(jax.ShapeDtypeStruct(shape, F32) for shape in shapes),
        in_specs=[hbm] * len(operands),
        out_specs=(hbm,) * len(shapes),
        scratch_shapes=[pltpu.VMEM(operand.shape, operand.dtype) for operand in operands]
        + [pltpu.VMEM(shape, F32) for shape in shapes]
        + [pltpu.SemaphoreType.DMA((len(operands),)), pltpu.SemaphoreType.DMA((len(shapes),))],
        compiler_params=pltpu.CompilerParams(vmem_limit_bytes=60 * 1024 * 1024),
        name="finish",
    )(*operands)


def body(
    tokens,
    padding_mask,
    embedding,
    mixer_weight,
    output_weight,
    mixer_gain,
    expand_weight,
    reduce_weight,
    feed_gain,
    final_gain,
):
    segments = lax.axis_size(SECTION)
    segment_index = lax.axis_index(SECTION)
    item_count = tokens.shape[0]
    assert item_count == segments
    slice_width = embedding.shape[1]

    if segments == 4 and lax.axis_size(DP) == 8:
        loss, lg, _, _, dwm, dwo, dwe, dwrt, last = local_step(
            True, tokens, padding_mask, embedding, mixer_gain, feed_gain, final_gain[None],
            mixer_weight, output_weight, expand_weight, reduce_weight,
        )
        loss, lg, table_grad, dwm, dwo, mixer_gain_grad, dwe, dwr, feed_gain_grad, final_gain_grad = finish(
            loss, lg, dwm, dwo, dwe, dwrt, last
        )
        return (
            loss, jnp.swapaxes(lg, 1, 2), table_grad, dwm, dwo, mixer_gain_grad, dwe, dwr, feed_gain_grad, final_gain_grad[0]
        )

    token_row = lax.dynamic_index_in_dim(tokens, segment_index, 0, keepdims=False)
    mask_row = lax.dynamic_index_in_dim(padding_mask, segment_index, 0, keepdims=False)
    zero = jnp.zeros((1,), jnp.int32)
    columns = jnp.stack(
        [token_row, jnp.concatenate([token_row[1:], zero]), jnp.concatenate([mask_row[1:], zero])], axis=1
    )

    def gather(block, dim):
        return lax.all_gather(block.astype(BF16), DP, axis=dim, tiled=True)

    table = lax.all_gather(gather(embedding, 0), SECTION, axis=1, tiled=True)
    gains = gather(jnp.concatenate([mixer_gain, feed_gain, final_gain[None]], axis=0), 1).astype(F32)
    loss, lg, _, _, dtable, dgm, dgf, dgz, dwm, dwo, dwe, dwrt = local_step(
        False, columns, table, gains[0:2, None], gains[2:4, None], gains[4:5],
        gather(mixer_weight, 1), gather(output_weight, 1), gather(expand_weight, 1), gather(reduce_weight, 1),
    )
    item_loss = lax.all_gather(loss[0, 0], SECTION)
    parts = lg.reshape(LEN, segments, slice_width).transpose(1, 0, 2)
    logit_grad = lax.all_to_all(parts, SECTION, 0, 0, tiled=True).astype(F32)

    def shard(grad, dim):
        part = lax.psum_scatter(grad.astype(BF16), DP, scatter_dimension=dim, tiled=True)
        return lax.psum(part, SECTION).astype(F32)

    table_part = lax.psum_scatter(dtable.astype(BF16), DP, scatter_dimension=0, tiled=True)
    table_grad = lax.psum_scatter(table_part, SECTION, scatter_dimension=1, tiled=True).astype(F32)
    gain_grads = lax.psum_scatter(
        jnp.concatenate([dgm[:, 0], dgf[:, 0], dgz], axis=0), DP, scatter_dimension=1, tiled=True
    )
    gain_grads = lax.psum(gain_grads, SECTION)
    return (
        item_loss,
        logit_grad,
        table_grad,
        shard(dwm, 1),
        shard(dwo, 1),
        gain_grads[0:2],
        shard(dwe, 1),
        jnp.swapaxes(shard(dwrt, 2), 1, 2),
        gain_grads[2:4],
        gain_grads[4],
    )


def solution(mesh):
    placed = (
        P(DP, None),
        P(DP, None),
        P(DP, SECTION),
        P(None, DP, None),
        P(None, DP, None),
        P(None, DP),
        P(None, DP, None),
        P(None, DP, None),
        P(None, DP),
        P(DP),
    )
    return jax.shard_map(
        body,
        mesh=mesh,
        in_specs=placed,
        out_specs=(
            P(DP),
            P(DP, None, SECTION),
            P(DP, SECTION),
            P(None, DP, None),
            P(None, DP, None),
            P(None, DP),
            P(None, DP, None),
            P(None, DP, None),
            P(None, DP),
            P(DP),
        ),
        check_vma=False,
    )
```

```python
import functools

import jax
import jax.numpy as jnp
from jax import lax
from jax.experimental import pallas as pl
from jax.experimental.pallas import tpu as pltpu
from jax.sharding import PartitionSpec as P

D = 512
HEADS = 8
HD = 64
FF = 2048
VOCAB = 256
BAND = 30
LEN = 640
LAYERS = 2
CH = 128
CHUNKS = LEN // CH
REACH = 32
WIDE = tuple((t0, min(t0 + 256, LEN)) for t0 in range(0, LEN, 256))
TILE = 512
BACK = 256
F32 = jnp.float32
DP, SECTION = ("dp", "section")
BF16 = jnp.bfloat16


def mm(left, right):
    return jnp.dot(left, right, preferred_element_type=F32)


def mm_nt(left, right):
    return lax.dot_general(left, right, (((1,), (1,)), ((), ())), preferred_element_type=F32)


def norm_forward(v, gain):
    scale = lax.rsqrt(jnp.mean(v * v, axis=-1, keepdims=True) + 1e-05)
    return v * scale * gain


def norm_backward(v, gain, dy):
    scale = lax.rsqrt(jnp.mean(v * v, axis=-1, keepdims=True) + 1e-05)
    normed = v * scale
    dgain = jnp.sum(dy * normed, axis=0, keepdims=True)
    dyg = dy * gain
    dv = scale * (dyg - normed * jnp.mean(dyg * normed, axis=-1, keepdims=True))
    return dv, dgain


def gelu_parts(u):
    c = 0.7978845608028654
    square = u * u
    t = jnp.tanh(u * (c + (c * 0.044715) * square))
    half = 0.5 * (1.0 + t)
    value = u * half
    slope = half + 0.5 * u * (1.0 - t * t) * (c + (3.0 * c * 0.044715) * square)
    return value, slope


def feature_parts(u):
    low_exp = jnp.exp(jnp.minimum(u, 0.0))
    first = jnp.where(u > 0.0, u + 1.0, low_exp)
    second = jnp.tanh(u)
    return first, low_exp, second


def iotas(rows, cols, row0=0):
    r = lax.broadcasted_iota(jnp.int32, (rows, cols), 0) + row0
    c = lax.broadcasted_iota(jnp.int32, (rows, cols), 1)
    return r, c


def near_part(i, key_rows, query_cols):
    row0 = -REACH if i > 0 else 0
    scores = mm(key_rows, query_cols) * 0.125
    r, c = iotas(CH - row0, CH, row0)
    ok = (r <= c) & (c - r < BAND)
    scores = jnp.where(ok, scores, -1e30)
    peak = jnp.max(scores, axis=0, keepdims=True)
    weights = jnp.exp(scores - peak)
    return weights / jnp.sum(weights, axis=0, keepdims=True)


def causal_rows(i, block):
    row0 = -REACH if i > 0 else 0
    r, c = iotas(CH - row0, CH, row0)
    return jnp.where(r <= c, block, 0.0)


START, WAIT = range(2)


def every(copies, act):
    for copy in copies:
        if act == START:
            copy.start()
        else:
            copy.wait()


def halves(t0, t1, half):
    parts = []
    for i in range(t0 // CH, t1 // CH):
        part = half(i)
        if part.shape[0] < t1:
            part = jnp.concatenate([part, jnp.zeros((t1 - part.shape[0], CH), part.dtype)], axis=0)
        parts.append(part)
    return parts[0] if len(parts) == 1 else jnp.concatenate(parts, axis=1)


def first_row(i):
    return i * CH - REACH if i > 0 else 0


def mixture_block(t0, t1, key_nat, key_feat2, query_masked, query_feat2, near_ref):
    far = mm(key_feat2[:t1], query_feat2[:, t0:t1])

    def half(i):
        r0, end = first_row(i), (i + 1) * CH
        near = near_part(i, key_nat[r0:end], query_masked[:, i * CH:end])
        near_ref[i, :end - r0, :] = near
        column = far[:end, i * CH - t0:end - t0]
        bottom = (causal_rows(i, column[r0:]) + near).astype(BF16)
        if r0 == 0:
            return bottom
        return jnp.concatenate([column[:r0].astype(BF16), bottom], axis=0)

    return halves(t0, t1, half)


def query_features(qT, inv1, inv2):
    first, slope1, second = feature_parts(qT.astype(F32))
    first_b, second_b = first.astype(BF16), second.astype(BF16)
    scaled = jnp.concatenate([first_b.astype(F32) * inv1, second_b.astype(F32) * inv2], axis=0)
    high = scaled.astype(BF16)
    rest = (scaled - high.astype(F32)).astype(BF16)
    return first_b, slope1, second, jnp.concatenate([high, rest], axis=0)


def masked_pair(part, e):
    zero = jnp.zeros_like(part)
    return jnp.concatenate([part, zero] if e == 0 else [zero, part], axis=0)


ALL, MINE, MINE_A, MINE_B, OTHER = range(5)


class Links:
    def __init__(self, pieces, send_sem, recv_sem):
        self.pieces, self.send_sem, self.recv_sem = pieces, send_sem, recv_sem
        d, z = lax.axis_index(DP), lax.axis_index(SECTION)
        core, x, y = d % 2, (d // 2) % 2, d // 4
        self.d, self.half = d, z % 2
        self.core_n, self.x_n, self.y_n, self.z_n = d + 1 - 2 * core, d + 2 - 4 * x, d + 4 - 8 * y, z + 1 - 2 * (z % 2)
        self.diag = self.x_n + 4 - 8 * y

    def columns(self, n, part):
        _, _, cols, cut, shared = self.pieces[n]
        if part == ALL or (part == MINE and not shared):
            return slice(None)
        if not shared:
            return slice(0, cut) if part == MINE_A else slice(cut, cols)
        half, quarter = cols // 2, cols // 4
        start = half * (1 - self.half if part == OTHER else self.half) + (quarter if part == MINE_B else 0)
        return pl.ds(pl.multiple_of(start, quarter), quarter if part in (MINE_A, MINE_B) else half)

    def copy(self, n, kind):
        ref, rows = self.pieces[n][:2]
        core, x, y, z = {DP: self.core_n}, {DP: self.x_n}, {DP: self.y_n}, {SECTION: self.z_n}
        block, part, target = (
            (self.d, MINE, x),
            (self.d, MINE, y),
            (self.y_n, MINE_A, x),
            (self.x_n, MINE_B, y),
            (self.d, ALL, core),
            (self.x_n, MINE, core),
            (self.y_n, MINE, core),
            (self.diag, MINE_A, core),
            (self.diag, MINE_B, core),
            (self.x_n, MINE, z),
            (self.y_n, MINE, z),
            (self.diag, MINE, z),
            (self.x_n, OTHER, core),
            (self.y_n, OTHER, core),
            (self.diag, OTHER, core),
        )[kind]
        view = ref.at[pl.ds(pl.multiple_of(block * rows, rows), rows), self.columns(n, part)]
        return pltpu.make_async_remote_copy(
            src_ref=view, dst_ref=view, send_sem=self.send_sem.at[n, kind], recv_sem=self.recv_sem.at[n, kind],
            device_id=target, device_id_type=pl.DeviceIdType.MESH,
        )

    def own(self, *ns):
        for n in ns:
            for kind in (0, 1, 4):
                self.copy(n, kind).start()

    def first(self, *ns):
        for n in ns:
            shared = self.pieces[n][4]
            self.copy(n, 0).wait_recv()
            self.copy(n, 3).start()
            self.copy(n, 1).wait_recv()
            self.copy(n, 2).start()
            for kind in (9, 10, 5, 6) if shared else (5, 6):
                self.copy(n, kind).start()

    def second(self, *ns):
        for n in ns:
            shared = self.pieces[n][4]
            self.copy(n, 2).wait_recv()
            self.copy(n, 7).start()
            self.copy(n, 3).wait_recv()
            for kind in (11, 8) if shared else (8,):
                self.copy(n, kind).start()

    def third(self, *ns):
        for n in ns:
            for kind in (9, 10, 11):
                self.copy(n, kind).wait_recv()
                self.copy(n, kind + 3).start()

    def ready(self, *ns):
        for n in ns:
            for kind in (4, 5, 6, 7, 8) + ((12, 13, 14) if self.pieces[n][4] else ()):
                self.copy(n, kind).wait_recv()

    def finish(self):
        for n, piece in enumerate(self.pieces):
            for kind in range(15 if piece[4] else 9):
                self.copy(n, kind).wait_send()


class Sums:
    def __init__(self, links, pieces, send_sem, recv_sem, tile_send, tile_recv):
        self.links, self.pieces, self.send_sem, self.recv_sem = links, pieces, send_sem, recv_sem
        self.tile_send, self.tile_recv = tile_send, tile_recv
        d = links.d
        self.core, self.x, self.y = d % 2, (d // 2) % 2, d // 4
        self.z = lax.axis_index(SECTION)
        self.inner = (self.z == 1) | (self.z == 2)
        self.outer = (self.z == 0) | (self.z == 3)

    def view(self, piece, ref, block, count, half=None):
        blocks = pl.ds(pl.multiple_of(block * piece.size, piece.size), count * piece.size)
        across = {None: slice(None), 0: slice(0, piece.split), 1: slice(piece.split, piece.across)}[half]
        return ref.at[across, blocks] if piece.by_columns else ref.at[blocks, across]

    def tile_copy(self, block):
        r = self.pieces[R0]
        src = r.whole.at[:, pl.ds(pl.multiple_of((4 * (1 - self.core) + block) * r.size, r.size), r.size)]
        dst = r.whole_r1.at[:, pl.ds(pl.multiple_of(block * r.size, r.size), r.size)]
        return pltpu.make_async_remote_copy(
            src_ref=src, dst_ref=dst, send_sem=self.tile_send.at[block], recv_sem=self.tile_recv.at[block],
            device_id={DP: self.links.core_n}, device_id_type=pl.DeviceIdType.MESH,
        )

    def copy(self, name, kind, l=0):
        piece = self.pieces[name]
        core, x, y, z, links = self.core, self.x, self.y, self.z, self.links
        mine = 4 * core

        def pair(block, to, at, count, half):
            return self.view(piece, piece.grad, block, count, half), self.view(piece, to, at, count, half)

        if kind == 0:
            src, dst = pair(4 * (1 - core), piece.r1, 0, 4, None)
        elif kind in (1, 2):
            src, dst = pair(mine + 2 * (kind - 1) + 1 - x, piece.r2, kind - 1, 1, 0)
        elif kind == 3:
            src, dst = pair(mine + 2 * (1 - y), piece.r2, 0, 2, 1)
        elif kind == 4:
            src, dst = pair(mine + 2 * (1 - y) + x, piece.r3[l], 0, 1, 0)
        elif kind == 5:
            src, dst = pair(mine + 2 * y + 1 - x, piece.r3[l], 0, 1, 1)
        else:
            src = piece.r3[l]
            dst = piece.rz.at[kind - 6] if kind < 8 else piece.out(l)
        device = (
            {DP: links.core_n}, {DP: links.x_n}, {DP: links.x_n}, {DP: links.y_n}, {DP: links.y_n}, {DP: links.x_n},
            {SECTION: z + 1 - 2 * (z // 3)}, {SECTION: 3 - z}, {SECTION: 3 * (z // 2)},
        )[kind]
        return pltpu.make_async_remote_copy(
            src_ref=src, dst_ref=dst, send_sem=self.send_sem.at[piece.index, kind], recv_sem=self.recv_sem.at[piece.index, kind],
            device_id=device, device_id_type=pl.DeviceIdType.MESH,
        )

    def tile_parts(self, block):
        y, x = block // 2, block % 2
        copies = []
        for name in (R0, R1):
            piece = self.pieces[name]
            for half, kind, to, at in ((0, 1 + y, {DP: self.links.x_n}, y), (1, 3 + 7 * x, {DP: self.links.y_n}, x)):
                copies.append(pltpu.make_async_remote_copy(
                    src_ref=self.view(piece, piece.grad, 4 * self.core + block, 1, half), dst_ref=self.view(piece, piece.r2, at, 1, half),
                    send_sem=self.send_sem.at[piece.index, kind], recv_sem=self.recv_sem.at[piece.index, kind],
                    device_id=to, device_id_type=pl.DeviceIdType.MESH,
                ))
        return copies

    def tile_step(self, block):
        self.tile_copy(block).wait_recv()
        r = self.pieces[R0]
        mine = pl.ds(pl.multiple_of((4 * self.core + block) * r.size, r.size), r.size)
        self.add(r.whole.at[:, mine], r.whole_r1.at[:, r.size * block:r.size * (block + 1)])
        first0, second0, first1, second1 = self.tile_parts(block)

        @pl.when(self.x != block % 2)
        def _():
            first0.start()
            first1.start()

        @pl.when(self.y != block // 2)
        def _():
            second0.start()
            second1.start()

    def add(self, into, other):
        into[...] = (into[...].astype(F32) + other[...].astype(F32)).astype(BF16)

    def step(self, name, number, l):
        piece = self.pieces[name]
        grad, r1, r2, r3, rz = piece.grad, piece.r1, piece.r2, piece.r3[l], piece.rz
        mine = 4 * self.core
        own = mine + 2 * self.y + self.x
        tiles = name in (R0, R1)
        if number == 1:
            self.copy(name, 0, l).start()
        elif number == 2 and tiles:
            if name == R0:
                self.tile_step(3)
        elif number == 2:
            self.copy(name, 0, l).wait_recv()
            self.add(self.view(piece, grad, mine, 4), self.view(piece, r1, 0, 4))
            for kind in (1, 2, 3):
                self.copy(name, kind, l).start()
        elif number == 3:
            for kind in (1, 2):
                self.copy(name, kind, l).wait_recv()
                self.add(self.view(piece, grad, mine + 2 * (kind - 1) + self.x, 1, 0), self.view(piece, r2, kind - 1, 1, 0))
            if tiles:
                for i in range(2):
                    self.half_block(name, i).wait_recv()
            else:
                self.copy(name, 3, l).wait_recv()
            self.add(self.view(piece, grad, mine + 2 * self.y, 2, 1), self.view(piece, r2, 0, 2, 1))
            self.copy(name, 4, l).start()
            self.copy(name, 5, l).start()
        elif number == 4:
            for half in (0, 1):
                self.copy(name, 4 + half, l).wait_recv()
                self.add(self.view(piece, r3, 0, 1, half), self.view(piece, grad, own, 1, half))

            @pl.when(self.outer)
            def _():
                self.copy(name, 6, l).start()

            if not tiles:
                self.copy(name, 0, l).wait_send()
            elif name == R0:
                for block in range(4):
                    self.tile_copy(block).wait_send()
            for kind in (1, 2, 4, 5):
                self.copy(name, kind, l).wait_send()
            if tiles:
                for i in range(2):
                    self.half_block(name, i).wait_send()
            else:
                self.copy(name, 3, l).wait_send()
        elif number == 5:

            @pl.when(self.inner)
            def _():
                self.copy(name, 6, l).wait_recv()
                self.add(r3, rz.at[0])
                self.copy(name, 7, l).start()
        elif number == 6:

            @pl.when(self.inner)
            def _():
                self.copy(name, 7, l).wait()
                self.add(r3, rz.at[1])
                self.copy(name, 8, l).start()
                self.local(piece, l).start()
        elif number == 7:

            @pl.when(self.outer)
            def _():
                self.copy(name, 6, l).wait_send()
                self.copy(name, 8, l).wait_recv()

            @pl.when(self.inner)
            def _():
                self.copy(name, 8, l).wait_send()
                self.local(piece, l).wait()

    def half_block(self, name, x):
        piece = self.pieces[name]
        view = self.view(piece, piece.r2, x, 1, 1)
        return pltpu.make_async_remote_copy(
            src_ref=view, dst_ref=view,
            send_sem=self.send_sem.at[piece.index, 3 + 7 * x], recv_sem=self.recv_sem.at[piece.index, 3 + 7 * x],
            device_id={DP: self.links.y_n}, device_id_type=pl.DeviceIdType.MESH,
        )

    def local(self, piece, l):
        return pltpu.make_async_copy(piece.r3[l], piece.out(l), self.send_sem.at[piece.index, 9])


class Piece:
    def __init__(self, index, refs, size, across, split, out, by_columns=False, whole=None):
        self.index, self.size, self.across, self.split, self.out, self.by_columns = index, size, across, split, out, by_columns
        self.grad, self.r1, self.r2, self.r3, self.rz = refs
        self.whole, self.whole_r1 = whole or (None, None)


def sum_pieces(refs, out_m, out_o, out_e, out_r, out_t):
    def part(n, index):
        views = [refs[name + n].at[index] for name in ("grad_", "r1", "r2")]
        views.append([refs["r3" + n].at[(l,) + index] for l in range(1 if n == "t" else LAYERS)])
        return views + [refs["rz" + n].at[(slice(None),) + index]]

    every = slice(None)
    pieces = {}
    for i in range(2):
        cols = slice(FF // 2 * i, FF // 2 * (i + 1))
        pieces[E0 + i] = Piece(E0 + i, part("e", (every, cols)), 64, FF // 2, FF // 4, lambda l, cols=cols: out_e.at[l, :, cols])
    for i in range(2):
        rows = slice(D // 2 * i, D // 2 * (i + 1))
        pieces[R0 + i] = Piece(
            R0 + i, part("r", (rows, every)), 256, D // 2, D // 4, lambda l, rows=rows: out_r.at[l, rows], True,
            (refs["grad_r"], refs["r1r"]),
        )
    for i in range(4):
        cols = slice(384 * i, 384 * (i + 1))
        pieces[M0 + i] = Piece(
            M0 + i, part("m", (every, cols)), 64, 384, 128 * (1 + i % 2), lambda l, i=i: out_m.at[l, i]
        )
    pieces[O] = Piece(O, part("o", (every, every)), 64, D, D // 2, lambda l: out_o.at[l])
    pieces[T] = Piece(T, part("t", (every, every)), 64, 384, 128, lambda l: out_t)
    return pieces


def by_position(rows):
    size = rows.shape[0] // 8
    return jnp.concatenate([rows[size * i:size * (i + 1)] for i in (0, 2, 4, 6, 1, 3, 5, 7)], axis=0)


def step_kernel(linked, *refs):
    names = (LINKED_IN + LINKED_OUT) if linked else (PLAIN_IN + PLAIN_OUT)
    names += tuple(SCRATCH) + tuple(LINKED_SCRATCH if linked else PLAIN_SCRATCH)
    step_body(linked, **dict(zip(names, refs, strict=True)))


def step_body(
    linked, loss, lg, kept_m, kept_near, x, x1, dx, keys, values, pT, inv1s, cum, oT, hT, g, gT, wide, a1k, m, near, keep_sem, d, ds, doT, dpT, yb, acc,
    columns=None, table=None, gm=None, gf=None, gz=None, wm=None, wo=None, we=None, wr=None, stage=None, stage_half=None, sem=None, sem_half=None,
    dtable=None, dgm=None, dgf=None, dgz=None, dwm=None, dwo=None, dwe=None, dwrt=None,
    tokens=None, mask=None, emb=None, mgain=None, fgain=None, zgain=None, wm_s=None, wo_s=None, we_s=None, wr_s=None, tz=None, gains=None, lgs=None, losss=None,
    send_sem=None, recv_sem=None, zsend=None, zrecv=None, load_sem=None, sum_send=None, sum_recv=None, tile_send=None, tile_recv=None,
    out_m=None, out_o=None, out_e=None, out_r=None, out_t=None, dgains=None, **sums_refs,
):
    table_ref = table
    gm_ref, gf_ref, gz_ref = gm, gf, gz
    wm_ref, wo_ref, we_ref, wr_ref = wm, wo, we, wr
    loss_ref, lg_ref, dtable_ref, dgm_ref, dgf_ref, dgz_ref = loss, lg, dtable, dgm, dgf, dgz
    dwm_ref, dwo_ref, dwe_ref, dwrt_ref = dwm, dwo, dwe, dwrt
    x_ref, x1_ref, dx_ref, pT_ref, inv1_ref, cum_ref = x, x1, dx, pT, inv1s, cum
    oT_ref, hT_ref, g_ref, gT_ref, wide_ref, a1k_ref, near_ref, m_ref, d_ref, ds_ref = oT, hT, g, gT, wide, a1k, near, m, d, ds
    doT_ref, dpT_ref, w_ref, yb_ref, acc_ref = doT, dpT, a1k, yb, acc
    xs = [x_ref.at[0], x_ref.at[1], dx_ref]
    placed = by_position if linked else (lambda rows: rows)
    r, c = iotas(2 * CH, 2 * CH)
    upper = (r <= c).astype(F32).astype(BF16)

    if linked:
        zi = lax.axis_index(SECTION)
        links = Links(
            [(table_ref, 64, 384, 256, False)]
            + [
                entry
                for l in range(LAYERS)
                for entry in (
                    (wm_ref.at[l], 64, 3 * D, 3 * D // 2, SHARED[l][0]),
                    (wo_ref.at[l], 64, D, D // 2, SHARED[l][1]),
                    (we_ref.at[l], 64, FF, FF // 2, SHARED[l][2]),
                    (wr_ref.at[l], 256, D, D // 2, SHARED[l][3]),
                )
            ],
            send_sem, recv_sem,
        )

        def along_z(n, k, src_of, dst):
            target = (zi + k) % 4
            return pltpu.make_async_remote_copy(
                src_ref=src_of(target), dst_ref=dst.at[zi], send_sem=zsend.at[n, k - 1], recv_sem=zrecv.at[n, k - 1],
                device_id={SECTION: target}, device_id_type=pl.DeviceIdType.MESH,
            )

        def table_copy(k):
            return along_z(0, k, lambda target: tz.at[zi], tz)

        def lg_copy(k):
            return along_z(1, k, lambda target: lgs.at[target], lg_ref)

        def loss_copy(k):
            return along_z(2, k, lambda target: losss, loss_ref)

        loads = []
        for l in range(LAYERS):
            pairs = [(wm_s.at[l, :, TILE * j:TILE * (j + 1)], x1_ref.at[l, 64 * j:64 * (j + 1)]) for j in range(3)]
            pairs += [(wo_s.at[l], x1_ref.at[l, 192:256])]
            pairs += [(we_s.at[l, :, TILE * j:TILE * (j + 1)], x1_ref.at[l, 256 + 64 * j:320 + 64 * j]) for j in range(4)]
            pairs += [(wr_s.at[l], x_ref.at[1, 256 * l:256 * (l + 1)])]
            loads.append([pltpu.make_async_copy(src, dst, load_sem.at[l, i]) for i, (src, dst) in enumerate(pairs)])
            for load in loads[l]:
                load.start()

        def take(l, part):
            for i in {"m": (0, 1, 2), "o": (3,), "e": (4, 5, 6, 7), "r": (8,)}[part]:
                loads[l][i].wait()
            if part == "m":
                for j in range(3):
                    wm_ref[l, own64, TILE * j:TILE * (j + 1)] = x1_ref[l, 64 * j:64 * (j + 1)].astype(BF16)
            elif part == "o":
                wo_ref[l, own64] = x1_ref[l, 192:256].astype(BF16)
            elif part == "e":
                for j in range(4):
                    we_ref[l, own64, TILE * j:TILE * (j + 1)] = x1_ref[l, 256 + 64 * j:320 + 64 * j].astype(BF16)
            else:
                wr_ref[l, own256] = x_ref[1, 256 * l:256 * (l + 1)].astype(BF16)

        barrier = pltpu.get_barrier_semaphore()
        for target in (links.core_n, links.x_n, links.y_n):
            pl.semaphore_signal(barrier, inc=1, device_id={DP: target}, device_id_type=pl.DeviceIdType.MESH)
        for k in (1, 2, 3):
            pl.semaphore_signal(barrier, inc=1, device_id={SECTION: (zi + k) % 4}, device_id_type=pl.DeviceIdType.MESH)

        own64 = pl.ds(pl.multiple_of(links.d * 64, 64), 64)
        own256 = pl.ds(pl.multiple_of(links.d * 256, 256), 256)
        r, _ = iotas(8, 64)
        rows = [mgain[0:1], mgain[1:2], fgain[0:1], fgain[1:2], zgain[0:1]]
        gathered = sum(jnp.where(r == i, row, 0.0) for i, row in enumerate(rows))
        gathered = jnp.concatenate([gathered, jnp.zeros((8, 64), F32)], axis=1)
        gathered = jnp.concatenate([gathered, jnp.zeros((120, 128), F32)], axis=0).T[:64]
        small_b = (jnp.concatenate([emb[...], jnp.zeros((64, 64), F32)], axis=1) + pltpu.roll(gathered, 64, 1)).astype(BF16)
        tz[zi] = small_b
        take(0, "m")
        pl.semaphore_wait(barrier, 6)
        for k in (1, 2, 3):
            table_copy(k).start()
        links.own(1)
        r, c = iotas(8, LEN)
        ids = tokens[pl.ds(zi, 1), :].astype(F32)
        scored = mask[pl.ds(zi, 1), :].astype(F32)
        rows = [ids, pltpu.roll(ids, LEN - 1, 1), pltpu.roll(scored, LEN - 1, 1)]
        rows = sum(jnp.where((r == i) & ((c < LEN - 1) | (r == 0)), row, 0.0) for i, row in enumerate(rows))
        columns[...] = rows.T.astype(jnp.int32)
        take(0, "o")
        for k in (1, 2, 3):
            table_copy(k).wait_recv()
        pad = jnp.zeros((64, 64), BF16)
        table_ref[own64, :] = jnp.concatenate([tz[i][:, :64] for i in range(4)] + [small_b[:, 64:], pad], axis=1)
        links.own(0, 2)
        take(0, "e")
        wide_ref[...] = upper
        links.first(1, 0)
        links.own(3)
        links.first(2)
        take(0, "r")
        links.own(4)
        for part in "moer":
            take(1, part)
        links.second(1, 0)
        links.ready(0)
        gains[...] = table_ref[:, 256:].astype(F32).T[:8]
        table_ref = table_ref.at[:, :256]
        gm_ref, gf_ref, gz_ref = [gains[i:i + 1] for i in range(2)], [gains[i:i + 1] for i in range(2, 4)], gains[4:5]
        sums = Sums(
            links, sum_pieces(sums_refs, out_m, out_o, out_e, out_r, out_t), sum_send, sum_recv, tile_send, tile_recv
        )
    else:
        wide_ref[...] = upper
        gm_ref, gf_ref, gz_ref = [gm_ref[i] for i in range(2)], [gf_ref[i] for i in range(2)], gz_ref[...]

    def service(step, index=None, only=lambda at: True):
        if not linked:
            return
        for at, acts in SERVICE.get(step, {}).items():
            if not only(at):
                continue

            def run(acts=acts):
                for act in acts:
                    if isinstance(act[0], int):
                        sums.step(*act)
                    elif act[0] is Sums.tile_step:
                        sums.tile_step(act[1])
                    else:
                        act[0](links, *act[1:])

            if at is None:
                run()
            else:
                pl.when(index == at)(run)

    inv2 = 1.0 / (lax.broadcasted_iota(jnp.int32, (1, LEN), 1).astype(F32) + 1.0)

    def emit(slot, wait_first, value, dst, pool=0):
        into, sems = (stage, sem) if pool == 0 else (stage_half, sem_half)

        def copy():
            return pltpu.make_async_copy(into.at[slot], dst, sems.at[slot])

        if wait_first is True:
            copy().wait()
        elif wait_first is not False:
            pl.when(wait_first)(lambda: copy().wait())
        into[slot] = value.astype(BF16)
        copy().start()

    def put_gain(row, value):
        if linked:
            dgains[row:row + 1] = value
        elif row < 2:
            dgm_ref[row] = value
        elif row < 4:
            dgf_ref[row - 2] = value
        else:
            dgz_ref[...] = value

    def by_rows(run, init=None):
        for i in range(CHUNKS):
            init = run(slice(i * CH, (i + 1) * CH), init)
        return init

    def normed_rows(src, gain, dst, dstT):
        def some(rows, carry):
            block = norm_forward(src[rows], gain).astype(BF16)
            dst[rows] = block
            dstT[:, rows] = placed(block.T)
            return carry

        by_rows(some, 0)

    def back_rows(src, gain, row):
        def some(rows, dgain):
            dv, dg = norm_backward(src[rows], gain, acc_ref[rows])
            dx_ref[rows] += dv
            return dgain + dg

        put_gain(row, by_rows(some, jnp.zeros((1, D), F32)))

    vocab_ids = lax.broadcasted_iota(jnp.int32, (LEN, VOCAB), 1)
    hot = (vocab_ids == columns[:, 0:1]).astype(F32).astype(BF16)
    x_ref[0] = mm_nt(hot, table_ref[...])
    if linked:
        links.ready(1)

    def keep(l, h, e):
        return (
            pltpu.make_async_copy(m_ref.at[e], kept_m.at[l, h], keep_sem.at[e, 0]),
            pltpu.make_async_copy(near_ref.at[e], kept_near.at[l, h], keep_sem.at[e, 1]),
        )

    def fetch(l, h, e):
        return (
            pltpu.make_async_copy(kept_m.at[l, h], m_ref.at[e], keep_sem.at[e, 0]),
            pltpu.make_async_copy(kept_near.at[l, h], near_ref.at[e], keep_sem.at[e, 1]),
        )

    m_ref[...] = jnp.zeros_like(m_ref)
    near_ref[...] = jnp.zeros_like(near_ref)

    def key_sums(l):
        a1k_ref[...] = feature_parts(pT_ref[l, D:2 * D, :].astype(F32))[0].astype(BF16)
        for t0, t1 in WIDE:
            total = mm(a1k_ref[:, t0:t1], wide_ref[:t1 - t0, :t1 - t0])
            cum_ref[:, t0:t1] = total if t0 == 0 else total + cum_ref[:, t0 - 1:t0]

    def attention_forward(l):
        normed_rows(x_ref.at[l], gm_ref[l], yb_ref, hT_ref.at[l])
        h = yb_ref[...]
        for j in range(3):
            part = mm(h, wm_ref[l, :, j * TILE:(j + 1) * TILE]).astype(BF16)
            if j == 1:
                keys[...] = part
            if j == 2:
                values[l] = part
            pT_ref[l, j * TILE:(j + 1) * TILE, :] = part.T
        service((MIXER, l))
        key_sums(l)

        def pair(p, carry):
            base = pl.multiple_of(p * CH, CH)
            for e in range(2):
                row = pl.multiple_of(base + e * HD, HD)
                if l == 0:
                    pl.when(p > 0)(lambda: every(keep(l, 0, e), WAIT))
                else:
                    for copy in keep(l, 0, e):
                        copy.wait()
                qT = pT_ref[l, pl.ds(row, HD), :]
                kT = pT_ref[l, pl.ds(pl.multiple_of(D + row, HD), HD), :]
                vT = pT_ref[l, pl.ds(pl.multiple_of(2 * D + row, HD), HD), :]
                first_k, _, second_k = feature_parts(kT.astype(F32))
                key_feat = jnp.concatenate([first_k.astype(BF16), second_k.astype(BF16)], axis=0).T
                first_q = feature_parts(qT.astype(F32))[0].astype(BF16).astype(F32)
                total = jnp.sum(first_q * cum_ref[pl.ds(row, HD), :], axis=0, keepdims=True)
                inv1 = 1.0 / (total + 1.0)
                inv1_ref[l, 2 * p + e] = inv1
                query_feat2 = query_features(qT, inv1, inv2)[3][:CH]
                key_feat2 = key_feat
                key_nat = keys[:, pl.ds(base, CH)]
                query_masked = masked_pair(qT, e)
                for t0, t1 in WIDE:
                    mixture = mixture_block(t0, t1, key_nat, key_feat2, query_masked, query_feat2, near_ref.at[e])
                    m_ref[e, :t1, t0:t1] = mixture
                    oT_ref[l, pl.ds(row, HD), t0:t1] = mm(vT[:, :t1], mixture).astype(BF16)
                for copy in keep(l, 2 * p + e, e):
                    copy.start()
                service((HEAD, l), 2 * p + e, lambda at: at % 2 == e)
            return carry

        lax.fori_loop(0, HEADS // 2, pair, 0)
        service((OUTPUT, l))
        o = oT_ref[l].T
        x1_ref[l] = x_ref[l] + mm(o, wo_ref[l])

    def feed_forward(l):
        normed_rows(x1_ref.at[l], gf_ref[l], g_ref, gT_ref.at[l])
        xs[l + 1][...] = x1_ref[l]
        service((FEED, l))

        def tile(j, carry):
            col = pl.multiple_of(j * TILE, TILE)
            active = gelu_parts(mm(g_ref[...], we_ref[l, :, pl.ds(col, TILE)]))[0].astype(BF16)
            service((GELU, l), j)
            xs[l + 1][...] += mm(active, wr_ref[l, pl.ds(col, TILE), :])
            service((FEED_TILE, l), j)
            return carry

        lax.fori_loop(0, FF // TILE, tile, 0)

    def head():
        zT_ref, grad_ref = doT_ref, yb_ref.at[:, :VOCAB]

        def some(rows, carry):
            dgain, cross_sum, val_sum = carry
            x = dx_ref[rows]
            z = norm_forward(x, gz_ref).astype(BF16)
            zT_ref[:, rows] = placed(z.T)
            logits = mm(z, table_ref[...])
            ids = lax.broadcasted_iota(jnp.int32, (CH, VOCAB), 1)
            tgt_hot = (ids == columns[rows, 1:2]).astype(F32)
            val = columns[rows, 2:3].astype(F32)
            peak = jnp.max(logits, axis=-1, keepdims=True)
            grown = jnp.exp(logits - peak)
            total = jnp.sum(grown, axis=-1, keepdims=True)
            lse = peak + jnp.log(total)
            picked = jnp.sum(logits * tgt_hot, axis=-1, keepdims=True)
            cross = (lse - picked) * val
            grad_b = ((grown / total - tgt_hot) * val).astype(BF16)
            grad_ref[rows, :] = grad_b
            if linked:
                grad_bT = grad_b.T
                for i in range(4):
                    lgs[i, :, rows] = grad_bT[64 * i:64 * i + 64]
            else:
                lg_ref[rows, :] = grad_b
            dv, dg = norm_backward(x, gz_ref, mm_nt(grad_b, table_ref[...]))
            dx_ref[rows] = dv
            return (
                dgain + dg,
                cross_sum + jnp.sum(cross, axis=0, keepdims=True),
                val_sum + jnp.sum(val, axis=0, keepdims=True),
            )

        nothing = jnp.zeros((1, 1), F32)
        dgain, cross_sum, val_sum = by_rows(some, (jnp.zeros((1, D), F32), nothing, nothing))
        put_gain(4, dgain)
        loss = jnp.broadcast_to(cross_sum / val_sum, (8, 128))
        if linked:
            losss[...] = loss
            for k in (1, 2, 3):
                lg_copy(k).start()
                loss_copy(k).start()
            pltpu.make_async_copy(lgs.at[zi], lg_ref.at[zi], zsend.at[1, 3]).start()
            pltpu.make_async_copy(losss, loss_ref.at[zi], zsend.at[2, 3]).start()
        else:
            loss_ref[...] = loss
        dtable_head = mm(zT_ref[...], grad_ref[...])
        if linked:
            sums_refs["grad_t"][:, :VOCAB] = dtable_head.astype(BF16)
        else:
            dtable_ref[...] = dtable_head

    def feed_backward(l):
        def some(rows, carry):
            yb = dx_ref[rows].astype(BF16)
            yb_ref[rows] = yb
            doT_ref[:, rows] = yb.T
            if l < LAYERS - 1:
                g_ref[rows] = norm_forward(x1_ref[l, rows], gf_ref[l]).astype(BF16)
            return carry

        by_rows(some, 0)
        acc_ref[...] = jnp.zeros_like(acc_ref)

        def tile(j, carry):
            col = pl.multiple_of(j * TILE, TILE)
            slot = lax.rem(j, 2)
            later = (j >= 2) if l == LAYERS - 1 else True
            value, slope = gelu_parts(mm(g_ref[...], we_ref[l, :, pl.ds(col, TILE)]))
            dreduce = mm(doT_ref[...], value.astype(BF16))
            if linked:
                for i in range(2):
                    place = pl.multiple_of(BACK * j + FF // 2 * i, BACK)
                    sums_refs["grad_r"][:, pl.ds(place, BACK)] = dreduce[:, BACK * i:BACK * (i + 1)].astype(BF16)
                sums.tile_copy(j).start()
            else:
                emit(slot, later, dreduce, dwrt_ref.at[l, :, pl.ds(col, TILE)], 1)
            dact = mm_nt(yb_ref[...], wr_ref[l, pl.ds(col, TILE), :])
            dhid = (dact * slope).astype(BF16)
            dexpand = mm(gT_ref[l], dhid)
            if linked:
                sums_refs["grad_e"][:, pl.ds(col, TILE)] = dexpand.astype(BF16)
            else:
                emit(2 + slot, later, dexpand, dwe_ref.at[l, :, pl.ds(col, TILE)], 1)
            dnormed = mm_nt(dhid, we_ref[l, :, pl.ds(col, TILE)])

            acc_ref[...] += dnormed
            service((BACK_TILE, l), j)
            return carry

        lax.fori_loop(0, FF // TILE, tile, 0)
        service((BACK_FEED, l))
        back_rows(x1_ref.at[l], gf_ref[l], 2 + l)

    def attention_backward(l):
        if l < LAYERS - 1:
            key_sums(l)
        yb_ref[...] = dx_ref[...].astype(BF16)
        yb = yb_ref[...]
        doutput = mm(placed(oT_ref[l]), yb)
        if linked:
            sums_refs["grad_o"][...] = doutput.astype(BF16)
        else:
            emit(0, l < LAYERS - 1, doutput, dwo_ref.at[l])
        service((BACK_OUTPUT, l))
        doT_ref[...] = mm_nt(yb, wo_ref[l]).astype(BF16).T

        for e in range(2):
            for copy in fetch(l, e, e):
                copy.start()

        def pair(p, carry):
            base = pl.multiple_of(p * CH, CH)
            for e in range(2):
                row = pl.multiple_of(base + e * HD, HD)
                qT = pT_ref[l, pl.ds(row, HD), :]
                kT = pT_ref[l, pl.ds(pl.multiple_of(D + row, HD), HD), :]
                doT = doT_ref[pl.ds(row, HD), :]
                inv1 = inv1_ref[l, 2 * p + e]
                first_q, slope1_q, second_q, query_feat2 = query_features(qT, inv1, inv2)
                first_k, slope1_k, second_k = feature_parts(kT.astype(F32))
                key_featT = jnp.concatenate([first_k.astype(BF16), second_k.astype(BF16)], axis=0)
                value_nat = values[l, :, pl.ds(base, CH)]
                do_masked = masked_pair(doT, e)
                for copy in fetch(l, 2 * p + e, e):
                    copy.wait()
                far_q, near_q = [], []
                for t0, t1 in WIDE:
                    dm = mm(value_nat[:t1], do_masked[:, t0:t1])

                    def half(i):
                        r0, end = first_row(i), (i + 1) * CH
                        column = dm[:end, i * CH - t0:end - t0]
                        bottom = column[r0:]
                        near = near_ref[e, i, :end - r0, :]
                        weighted = near * bottom
                        dsum = jnp.sum(weighted, axis=0, keepdims=True)
                        ds = ((weighted - near * dsum) * 0.125).astype(BF16)
                        if i > 0:
                            before = jnp.concatenate([jnp.zeros((CH - REACH, CH), BF16), ds[:REACH]], axis=0)
                            ds_ref[end - 2 * CH:end - CH, CH:] = before
                            ds = ds[REACH:]
                            near_q.append(mm(kT[:, end - 2 * CH:end], jnp.concatenate([before, ds], axis=0)))
                        else:
                            near_q.append(mm(kT[:, :end], ds))
                        ds_ref[end - CH:end, :CH] = ds
                        lower = causal_rows(i, bottom).astype(BF16)
                        if r0 == 0:
                            return lower
                        return jnp.concatenate([column[:r0].astype(BF16), lower], axis=0)

                    dm_b = halves(t0, t1, half)
                    d_ref[:t1, t0:t1] = dm_b
                    far_q.append(mm(key_featT[:, :t1], dm_b))
                farT = jnp.concatenate(far_q, axis=1)
                y1, y2 = farT[:HD], farT[HD:]
                first_qf = first_q.astype(F32)
                m = inv1 * jnp.sum(first_qf * y1, axis=0, keepdims=True)
                cum = cum_ref[pl.ds(row, HD), :]
                dq = jnp.concatenate(near_q, axis=1)
                dq = dq + (inv1 * (y1 - m * cum)) * slope1_q + (inv2 * y2) * (1.0 - second_q * second_q)
                dpT_ref[pl.ds(row, HD), :] = dq.astype(BF16)
                w_ref[pl.ds(row, HD), :] = (first_qf * (m * inv1)).astype(BF16)
                after = 0.0
                for t0, t1 in reversed(WIDE):
                    far = mm_nt(query_feat2[:CH, t0:], d_ref[t0:t1, t0:])
                    back = mm_nt(w_ref[pl.ds(row, HD), t0:t1], wide_ref[:t1 - t0, :t1 - t0]) + after
                    after = back[:, :1]
                    near_k = []
                    for u0 in range(t0, t1, CH):
                        u2 = min(u0 + 2 * CH, LEN)
                        near_k.append(mm_nt(qT[:, u0:u2], ds_ref[u0:u0 + CH, :u2 - u0]))
                    near = near_k[0] if len(near_k) == 1 else jnp.concatenate(near_k, axis=1)
                    dk = near + (far[:HD] - back) * slope1_k[:, t0:t1]
                    dk = dk + far[HD:] * (1.0 - second_k[:, t0:t1] * second_k[:, t0:t1])
                    dpT_ref[pl.ds(pl.multiple_of(D + row, HD), HD), t0:t1] = dk.astype(BF16)
                    dv = mm_nt(doT[:, t0:], m_ref[e, t0:t1, t0:])
                    dpT_ref[pl.ds(pl.multiple_of(2 * D + row, HD), HD), t0:t1] = dv.astype(BF16)
                pl.when(p < HEADS // 2 - 1)(lambda: every(fetch(l, 2 * p + e + 2, e), START))
                service((BACK_HEAD, l), 2 * p + e, lambda at: at % 2 == e)
            if linked:
                for j in range(3):
                    block = mm_nt(hT_ref[l], dpT_ref[pl.ds(pl.multiple_of(j * D + base, CH), CH), :])
                    place = pl.multiple_of(3 * base + j * CH, CH)
                    sums_refs["grad_m"][:, pl.ds(place, CH)] = block.astype(BF16)
                service((BACK_PAIR, l), p)
            return carry

        lax.fori_loop(0, HEADS // 2, pair, 0)
        if not linked:
            for j in range(3):
                block = mm_nt(hT_ref[l], dpT_ref[j * TILE:(j + 1) * TILE, :])
                emit(1 + j, l < LAYERS - 1, block, dwm_ref.at[l, :, j * TILE:(j + 1) * TILE])
        for t0 in range(0, LEN, 256):
            t1 = min(t0 + 256, LEN)
            acc_ref[t0:t1] = mm(wm_ref[l], dpT_ref[:, t0:t1]).T
        service((BACK_MIXER, l))
        back_rows(x_ref.at[l], gm_ref[l], l)
        service((BACK_LAYER, l))

    for l in range(LAYERS):
        service((LAYER, l))
        attention_forward(l)
        feed_forward(l)
    for e in range(2):
        for copy in keep(0, 0, e):
            copy.wait()
    head()
    for l in reversed(range(LAYERS)):
        feed_backward(l)
        attention_backward(l)
    dtable_head = sums_refs["grad_t"][:, :VOCAB].astype(F32) if linked else dtable_ref[...]
    dtable_sum = dtable_head + mm(placed(dx_ref[...].astype(BF16).T), hot)
    if linked:
        sums_refs["grad_t"][:, :VOCAB] = dtable_sum.astype(BF16)
        sums_refs["grad_t"][:, VOCAB:] = placed(jnp.concatenate([dgains[...], jnp.zeros((120, D), F32)], axis=0).T).astype(BF16)
        service((END, 0))
        for k in (1, 2, 3):
            table_copy(k).wait_send()
            lg_copy(k).wait()
            loss_copy(k).wait()
        pltpu.make_async_copy(lgs.at[zi], lg_ref.at[zi], zsend.at[1, 3]).wait()
        pltpu.make_async_copy(losss, loss_ref.at[zi], zsend.at[2, 3]).wait()
        links.finish()
    else:
        dtable_ref[...] = dtable_sum
        for slot in range(4):
            pltpu.make_async_copy(stage.at[slot], dwo_ref.at[0], sem.at[slot]).wait()
            pltpu.make_async_copy(stage_half.at[slot], dwe_ref.at[0, :, :TILE], sem_half.at[slot]).wait()


E0, E1, R0, R1, M0, M1, M2, M3, O, T = range(10)
MIXER, HEAD, FEED, GELU, FEED_TILE, LAYER, BACK_TILE, BACK_FEED, BACK_OUTPUT, BACK_HEAD, BACK_PAIR, BACK_MIXER, BACK_LAYER, END, OUTPUT = range(15)
SHARED = ((False, False, True, False), (True, False, True, False))
SERVICE = {
    (MIXER, 0): {
        None: ((Links.second, 2), (Links.first, 3),),
    },
    (HEAD, 0): {
        1: ((Links.own, 5),),
        3: ((Links.first, 4),),
        4: ((Links.second, 3),),
        5: ((Links.own, 6),),
        6: ((Links.first, 5),),
        7: ((Links.own, 7),),
    },
    (OUTPUT, 0): {
        None: ((Links.ready, 2),),
    },
    (FEED, 0): {
        None: ((Links.second, 4), (Links.third, 3), (Links.ready, 3),),
    },
    (GELU, 0): {
        0: ((Links.ready, 4),),
    },
    (FEED_TILE, 0): {
        0: ((Links.second, 5), (Links.first, 6), (Links.own, 8),),
        2: ((Links.first, 7),),
    },
    (LAYER, 1): {
        None: ((Links.third, 5), (Links.ready, 5),),
    },
    (MIXER, 1): {
        None: ((Links.second, 6), (Links.first, 8),),
    },
    (HEAD, 1): {
        0: ((Links.second, 7),),
        4: ((Links.second, 8),),
        5: ((Links.third, 7),),
    },
    (OUTPUT, 1): {
        None: ((Links.ready, 6),),
    },
    (FEED, 1): {
        None: ((Links.ready, 7),),
    },
    (GELU, 1): {
        0: ((Links.ready, 8),),
    },
    (BACK_TILE, 1): {
        1: ((E0, 1, 1), (Sums.tile_step, 0),),
        2: ((Sums.tile_step, 1),),
        3: ((Sums.tile_step, 2),),
    },
    (BACK_FEED, 1): {
        None: ((E1, 1, 1),),
    },
    (BACK_OUTPUT, 1): {
        None: ((O, 1, 1), (E0, 2, 1),),
    },
    (BACK_HEAD, 1): {
        0: ((E1, 2, 1), (R0, 2, 1),),
        2: ((E0, 3, 1),),
        3: ((R1, 2, 1), (M0, 2, 1),),
        4: ((E1, 3, 1), (R0, 3, 1), (R1, 3, 1),),
        5: ((E0, 4, 1),),
        6: ((E1, 4, 1), (M1, 2, 1),),
        7: ((R0, 4, 1), (M2, 2, 1),),
    },
    (BACK_PAIR, 1): {
        0: ((M0, 1, 1),),
        1: ((M1, 1, 1),),
        2: ((M2, 1, 1), (M0, 3, 1),),
        3: ((M3, 1, 1), (O, 2, 1),),
    },
    (BACK_MIXER, 1): {
        None: ((E0, 5, 1), (R1, 4, 1), (M0, 4, 1), (M3, 2, 1),),
    },
    (BACK_LAYER, 1): {
        None: ((M1, 3, 1),),
    },
    (BACK_TILE, 0): {
        0: ((E1, 5, 1), (M2, 3, 1), (M3, 3, 1), (O, 3, 1),),
        1: ((E0, 1, 0), (Sums.tile_step, 0), (E0, 6, 1), (R0, 5, 1), (M1, 4, 1),),
        2: ((Sums.tile_step, 1), (E1, 6, 1), (R1, 5, 1), (M0, 5, 1), (M2, 4, 1), (M3, 4, 1), (O, 4, 1), (E0, 2, 0),),
        3: ((Sums.tile_step, 2), (R0, 6, 1), (M1, 5, 1), (M2, 5, 1), (E0, 7, 1),),
    },
    (BACK_FEED, 0): {
        None: ((E1, 1, 0),),
    },
    (BACK_OUTPUT, 0): {
        None: ((O, 1, 0), (M3, 5, 1), (R0, 2, 0),),
    },
    (BACK_HEAD, 0): {
        0: ((R1, 6, 1), (M0, 6, 1), (O, 5, 1), (E1, 7, 1), (E1, 2, 0), (E0, 3, 0),),
        1: ((M1, 6, 1), (M2, 6, 1), (M3, 6, 1), (R0, 7, 1), (R0, 3, 0),),
        2: ((O, 6, 1), (R1, 2, 0), (R1, 3, 0),),
        3: ((R1, 7, 1), (E1, 3, 0),),
        4: ((M1, 7, 1), (M2, 7, 1), (R0, 4, 0), (M0, 2, 0),),
        5: ((M3, 7, 1), (R1, 4, 0), (M1, 2, 0),),
        6: ((M0, 3, 0), (M2, 2, 0),),
        7: ((R0, 5, 0), (M1, 3, 0),),
    },
    (BACK_PAIR, 0): {
        0: ((M0, 1, 0),),
        1: ((M1, 1, 0), (M0, 7, 1), (E0, 4, 0),),
        2: ((M2, 1, 0), (O, 7, 1), (E0, 5, 0), (E1, 4, 0), (O, 2, 0),),
        3: ((M3, 1, 0),),
    },
    (BACK_MIXER, 0): {
        None: ((E0, 6, 0), (R1, 5, 0), (M0, 4, 0), (O, 3, 0), (M3, 2, 0),),
    },
    (BACK_LAYER, 0): {
        None: ((M1, 4, 0), (M2, 3, 0),),
    },
    (END, 0): {
        None: (
            (T, 1, 0), (E1, 5, 0), (T, 2, 0), (R0, 6, 0), (O, 4, 0), (M0, 5, 0), (M3, 3, 0), (M1, 5, 0), (M2, 4, 0), (R1, 6, 0),
            (O, 5, 0), (T, 3, 0), (M2, 5, 0), (M3, 4, 0), (E1, 6, 0), (M3, 5, 0), (M0, 6, 0), (T, 4, 0), (M1, 6, 0), (T, 5, 0),
            (O, 6, 0), (M2, 6, 0), (M3, 6, 0), (T, 6, 0), (E0, 7, 0), (R0, 7, 0), (R1, 7, 0), (E1, 7, 0), (M0, 7, 0),
            (M1, 7, 0), (O, 7, 0), (M2, 7, 0), (M3, 7, 0), (T, 7, 0),
        ),
    },
}
PLAIN_IN = ("columns", "table", "gm", "gf", "gz", "wm", "wo", "we", "wr")
PLAIN_OUT = ("loss", "lg", "kept_m", "kept_near", "dtable", "dgm", "dgf", "dgz", "dwm", "dwo", "dwe", "dwrt")
LINKED_IN = ("tokens", "mask", "emb", "mgain", "fgain", "zgain", "wm_s", "wo_s", "we_s", "wr_s")
LINKED_OUT = ("loss", "lg", "kept_m", "kept_near", "out_m", "out_o", "out_e", "out_r", "out_t")
SCRATCH = dict(
    x=pltpu.VMEM((LAYERS, LEN, D), F32),
    x1=pltpu.VMEM((LAYERS, LEN, D), F32),
    dx=pltpu.VMEM((LEN, D), F32),
    keys=pltpu.VMEM((LEN, D), BF16),
    values=pltpu.VMEM((LAYERS, LEN, D), BF16),
    pT=pltpu.VMEM((LAYERS, 3 * D, LEN), BF16),
    inv1s=pltpu.VMEM((LAYERS, HEADS, 1, LEN), F32),
    cum=pltpu.VMEM((D, LEN), F32),
    oT=pltpu.VMEM((LAYERS, D, LEN), BF16),
    hT=pltpu.VMEM((LAYERS, D, LEN), BF16),
    g=pltpu.VMEM((LEN, D), BF16),
    gT=pltpu.VMEM((LAYERS, D, LEN), BF16),
    wide=pltpu.VMEM((2 * CH, 2 * CH), BF16),
    a1k=pltpu.VMEM((D, LEN), BF16),
    m=pltpu.VMEM((2, LEN, LEN), BF16),
    near=pltpu.VMEM((2, CHUNKS, CH + REACH, CH), F32),
    keep_sem=pltpu.SemaphoreType.DMA((2, 2)),
    d=pltpu.VMEM((LEN, LEN), BF16),
    ds=pltpu.VMEM((LEN, 2 * CH), BF16),
    doT=pltpu.VMEM((D, LEN), BF16),
    dpT=pltpu.VMEM((3 * D, LEN), BF16),
    yb=pltpu.VMEM((LEN, D), BF16),
    acc=pltpu.VMEM((LEN, D), F32),
)
PLAIN_SCRATCH = dict(
    stage=pltpu.VMEM((4, D, TILE), BF16),
    stage_half=pltpu.VMEM((4, D, TILE), BF16),
    sem=pltpu.SemaphoreType.DMA((4,)),
    sem_half=pltpu.SemaphoreType.DMA((4,)),
)


def sum_buffers(n, rows, cols, along):
    def shape(blocks):
        return (rows * blocks // 8, cols) if along == 0 else (rows, cols * blocks // 8)

    return {
        "grad_" + n: pltpu.VMEM((rows, cols), BF16),
        "r1" + n: pltpu.VMEM(shape(4), BF16),
        "r2" + n: pltpu.VMEM(shape(2), BF16),
        "r3" + n: pltpu.VMEM((1 if n == "t" else LAYERS,) + shape(1), BF16),
        "rz" + n: pltpu.VMEM((2,) + shape(1), BF16),
    }


LINKED_SCRATCH = dict(
    table=pltpu.VMEM((D, 384), BF16),
    wm=pltpu.VMEM((LAYERS, D, 3 * D), BF16),
    wo=pltpu.VMEM((LAYERS, D, D), BF16),
    we=pltpu.VMEM((LAYERS, D, FF), BF16),
    wr=pltpu.VMEM((LAYERS, FF, D), BF16),
    columns=pltpu.VMEM((LEN, 8), jnp.int32),
    tz=pltpu.VMEM((4, 64, 128), BF16),
    gains=pltpu.VMEM((8, D), F32),
    lgs=pltpu.VMEM((4, 64, LEN), BF16),
    losss=pltpu.VMEM((8, 128), F32),
    send_sem=pltpu.SemaphoreType.DMA((9, 15)),
    recv_sem=pltpu.SemaphoreType.DMA((9, 15)),
    zsend=pltpu.SemaphoreType.DMA((3, 4)),
    zrecv=pltpu.SemaphoreType.DMA((3, 4)),
    load_sem=pltpu.SemaphoreType.DMA((LAYERS, 9)),
    sum_send=pltpu.SemaphoreType.DMA((10, 11)),
    sum_recv=pltpu.SemaphoreType.DMA((10, 11)),
    tile_send=pltpu.SemaphoreType.DMA((4,)),
    tile_recv=pltpu.SemaphoreType.DMA((4,)),
    dgains=pltpu.VMEM((8, D), F32),
    **sum_buffers("m", D, 3 * D, 0),
    **sum_buffers("o", D, D, 0),
    **sum_buffers("e", D, FF, 0),
    **sum_buffers("r", D, FF, 1),
    **sum_buffers("t", D, 384, 0),
)


def local_step(linked, *operands):
    vmem = pl.BlockSpec(memory_space=pltpu.VMEM)
    hbm = pl.BlockSpec(memory_space=pl.ANY)
    shape = jax.ShapeDtypeStruct
    kept = (shape((LAYERS, HEADS, LEN, LEN), BF16), shape((LAYERS, HEADS, CHUNKS, CH + REACH, CH), F32))
    if linked:
        scratch = dict(SCRATCH, **LINKED_SCRATCH)
        in_specs = [vmem] * 6 + [hbm] * 4
        out_shape = (
            shape((4, 8, 128), F32),
            shape((4, 64, LEN), BF16),
            *kept,
            shape((LAYERS, 4, 64, 384), BF16),
            shape((LAYERS, 64, D), BF16),
            shape((LAYERS, 64, FF), BF16),
            shape((LAYERS, D, 256), BF16),
            shape((64, 384), BF16),
        )
        out_specs = (hbm,) * 9
    else:
        scratch = dict(SCRATCH, **PLAIN_SCRATCH)
        in_specs = [vmem] * len(operands)
        out_shape = (
            shape((8, 128), F32),
            shape((LEN, VOCAB), BF16),
            *kept,
            shape((D, VOCAB), F32),
            shape((LAYERS, 1, D), F32),
            shape((LAYERS, 1, D), F32),
            shape((1, D), F32),
            shape((LAYERS, D, 3 * D), BF16),
            shape((LAYERS, D, D), BF16),
            shape((LAYERS, D, FF), BF16),
            shape((LAYERS, D, FF), BF16),
        )
        out_specs = (vmem,) * 2 + (hbm,) * 2 + (vmem,) * 4 + (hbm,) * 4
    return pl.pallas_call(
        functools.partial(step_kernel, linked),
        out_shape=out_shape,
        in_specs=in_specs,
        out_specs=out_specs,
        scratch_shapes=list(scratch.values()),
        compiler_params=pltpu.CompilerParams(
            vmem_limit_bytes=64 * 1024 * 1024,
            collective_id=0 if linked else None,
            has_side_effects=linked,
        ),
        cost_estimate=pl.CostEstimate(flops=40_000_000_000, bytes_accessed=40_000_000, transcendentals=0),
        name="local_step",
    )(*operands)


def finish_kernel(*refs):
    count = 7
    ins, outs = refs[:count], refs[count:count + 10]
    held, made = refs[count + 10:2 * count + 10], refs[2 * count + 10:2 * count + 20]
    in_sem, out_sem = refs[2 * count + 20:]
    copies = [pltpu.make_async_copy(src, dst, in_sem.at[i]) for i, (src, dst) in enumerate(zip(ins, held))]
    leave = [pltpu.make_async_copy(src, dst, out_sem.at[i]) for i, (src, dst) in enumerate(zip(made, outs))]
    every(copies, START)
    loss, lg, dwm, dwo, dwe, dwrt, last = held
    out_loss, out_lg, out_table, out_m, out_o, out_mgain, out_e, out_r, out_fgain, out_zgain = made
    z = lax.axis_index(SECTION)
    copies[4].wait()
    out_e[...] = dwe[...].astype(F32)
    leave[6].start()
    copies[1].wait()
    out_lg[...] = lg[...].astype(F32)
    leave[1].start()
    copies[2].wait()
    for l in range(LAYERS):
        for p in range(4):
            for j in range(3):
                out_m[l, :, D * j + CH * p:D * j + CH * (p + 1)] = dwm[l, p, :, CH * j:CH * (j + 1)].astype(F32)
    leave[3].start()
    copies[5].wait()
    for l in range(LAYERS):
        out_r[l] = dwrt[l].astype(F32).T
    leave[7].start()
    copies[3].wait()
    out_o[...] = dwo[...].astype(F32)
    leave[4].start()
    copies[6].wait()
    table = last[:, :VOCAB].astype(F32)
    out_table[...] = sum(jnp.where(z == i, table[:, 64 * i:64 * (i + 1)], 0.0) for i in range(4))
    leave[2].start()
    gains = last[:, VOCAB:].astype(F32)
    gains = jnp.concatenate([gains, jnp.zeros((64, 128), F32)], axis=0).T
    out_mgain[...] = gains[0:2, :64]
    out_fgain[...] = gains[2:4, :64]
    out_zgain[...] = gains[4:5, :64]
    copies[0].wait()
    r, c = iotas(4, 128)
    out_loss[...] = jnp.sum(jnp.where(r == c, loss[:, 0, :], 0.0), axis=0)[:4]
    for i in (5, 8, 9, 0):
        leave[i].start()
    every(leave, WAIT)


def finish(*operands):
    hbm = pl.BlockSpec(memory_space=pl.ANY)
    shapes = (
        (4,), (4, 64, LEN), (64, 64), (LAYERS, 64, 3 * D), (LAYERS, 64, D), (LAYERS, 64), (LAYERS, 64, FF),
        (LAYERS, 256, D), (LAYERS, 64), (1, 64),
    )
    return pl.pallas_call(
        finish_kernel,
        out_shape=tuple(jax.ShapeDtypeStruct(shape, F32) for shape in shapes),
        in_specs=[hbm] * len(operands),
        out_specs=(hbm,) * len(shapes),
        scratch_shapes=[pltpu.VMEM(operand.shape, operand.dtype) for operand in operands]
        + [pltpu.VMEM(shape, F32) for shape in shapes]
        + [pltpu.SemaphoreType.DMA((len(operands),)), pltpu.SemaphoreType.DMA((len(shapes),))],
        compiler_params=pltpu.CompilerParams(vmem_limit_bytes=60 * 1024 * 1024),
        name="finish",
    )(*operands)


def body(
    tokens,
    padding_mask,
    embedding,
    mixer_weight,
    output_weight,
    mixer_gain,
    expand_weight,
    reduce_weight,
    feed_gain,
    final_gain,
):
    segments = lax.axis_size(SECTION)
    segment_index = lax.axis_index(SECTION)
    item_count = tokens.shape[0]
    assert item_count == segments
    slice_width = embedding.shape[1]

    if segments == 4 and lax.axis_size(DP) == 8:
        loss, lg, _, _, dwm, dwo, dwe, dwrt, last = local_step(
            True, tokens, padding_mask, embedding, mixer_gain, feed_gain, final_gain[None],
            mixer_weight, output_weight, expand_weight, reduce_weight,
        )
        loss, lg, table_grad, dwm, dwo, mixer_gain_grad, dwe, dwr, feed_gain_grad, final_gain_grad = finish(
            loss, lg, dwm, dwo, dwe, dwrt, last
        )
        return (
            loss, jnp.swapaxes(lg, 1, 2), table_grad, dwm, dwo, mixer_gain_grad, dwe, dwr, feed_gain_grad, final_gain_grad[0]
        )

    token_row = lax.dynamic_index_in_dim(tokens, segment_index, 0, keepdims=False)
    mask_row = lax.dynamic_index_in_dim(padding_mask, segment_index, 0, keepdims=False)
    zero = jnp.zeros((1,), jnp.int32)
    columns = jnp.stack(
        [token_row, jnp.concatenate([token_row[1:], zero]), jnp.concatenate([mask_row[1:], zero])], axis=1
    )

    def gather(block, dim):
        return lax.all_gather(block.astype(BF16), DP, axis=dim, tiled=True)

    table = lax.all_gather(gather(embedding, 0), SECTION, axis=1, tiled=True)
    gains = gather(jnp.concatenate([mixer_gain, feed_gain, final_gain[None]], axis=0), 1).astype(F32)
    loss, lg, _, _, dtable, dgm, dgf, dgz, dwm, dwo, dwe, dwrt = local_step(
        False, columns, table, gains[0:2, None], gains[2:4, None], gains[4:5],
        gather(mixer_weight, 1), gather(output_weight, 1), gather(expand_weight, 1), gather(reduce_weight, 1),
    )
    item_loss = lax.all_gather(loss[0, 0], SECTION)
    parts = lg.reshape(LEN, segments, slice_width).transpose(1, 0, 2)
    logit_grad = lax.all_to_all(parts, SECTION, 0, 0, tiled=True).astype(F32)

    def shard(grad, dim):
        part = lax.psum_scatter(grad.astype(BF16), DP, scatter_dimension=dim, tiled=True)
        return lax.psum(part, SECTION).astype(F32)

    table_part = lax.psum_scatter(dtable.astype(BF16), DP, scatter_dimension=0, tiled=True)
    table_grad = lax.psum_scatter(table_part, SECTION, scatter_dimension=1, tiled=True).astype(F32)
    gain_grads = lax.psum_scatter(
        jnp.concatenate([dgm[:, 0], dgf[:, 0], dgz], axis=0), DP, scatter_dimension=1, tiled=True
    )
    gain_grads = lax.psum(gain_grads, SECTION)
    return (
        item_loss,
        logit_grad,
        table_grad,
        shard(dwm, 1),
        shard(dwo, 1),
        gain_grads[0:2],
        shard(dwe, 1),
        jnp.swapaxes(shard(dwrt, 2), 1, 2),
        gain_grads[2:4],
        gain_grads[4],
    )


def solution(mesh):
    placed = (
        P(DP, None),
        P(DP, None),
        P(DP, SECTION),
        P(None, DP, None),
        P(None, DP, None),
        P(None, DP),
        P(None, DP, None),
        P(None, DP, None),
        P(None, DP),
        P(DP),
    )
    return jax.shard_map(
        body,
        mesh=mesh,
        in_specs=placed,
        out_specs=(
            P(DP),
            P(DP, None, SECTION),
            P(DP, SECTION),
            P(None, DP, None),
            P(None, DP, None),
            P(None, DP),
            P(None, DP, None),
            P(None, DP, None),
            P(None, DP),
            P(DP),
        ),
        check_vma=False,
    )
```
